32 devices in a mesh: dp: 8 (over z, x), seq: 4 (over y, core).
Axes of the slice: x: 2, y: 2, z: 4, core: 2. Of those that a mesh axis runs over, the one named last changes fastest.
Arguments:
- tokens: bfloat16 [32, 512, 768], P('dp', 'seq'), may hold values from -6 to 6
- seg_lengths: int32 [32, 8], P('dp'), may hold values from 1 to 392, 512 in all within a row
- w_query: bfloat16 [768, 768], replicated, may hold values from -0.3125 to 0.3125
- b_query: bfloat16 [768], replicated, may hold values from -3 to 3
- w_key: bfloat16 [768, 768], replicated, may hold values from -0.3125 to 0.3125
- w_value: bfloat16 [768, 768], replicated, may hold values from -0.21875 to 0.21875
- b_value: bfloat16 [768], replicated, may hold values from -3 to 3
- w_out: bfloat16 [768, 768], replicated, may hold values from -0.625 to 0.625
- b_out: bfloat16 [768], replicated, may hold values from -3 to 3
- gain_attn: bfloat16 [768], replicated, may hold values from 0.25 to 1.75
- shift_attn: bfloat16 [768], replicated, may hold values from -3 to 3
- w_up: bfloat16 [768, 3072], replicated, may hold values from -0.21875 to 0.21875
- b_up: bfloat16 [3072], replicated, may hold values from -3 to 3
- w_down: bfloat16 [3072, 768], replicated, may hold values from -0.109375 to 0.109375
- b_down: bfloat16 [768], replicated, may hold values from -3 to 3
- gain_ffn: bfloat16 [768], replicated, may hold values from 0.25 to 1.75
- shift_ffn: bfloat16 [768], replicated, may hold values from -3 to 3
- grad_output: bfloat16 [32, 512, 768], P('dp', 'seq'), may hold values from -6 to 6
- grad_pooled: bfloat16 [32, 8, 768], P('dp'), may hold values from -12 to 12
Outputs:
- output: bfloat16 [32, 512, 768], P('dp', 'seq')
- pooled: float32 [32, 8, 768], P('dp')
- grad_tokens: bfloat16 [32, 512, 768], P('dp', 'seq')
- grad_w_query: float32 [768, 768], P(None, 'dp')
- grad_b_query: float32 [768], P('dp')
- grad_w_key: float32 [768, 768], P(None, 'dp')
- grad_w_value: float32 [768, 768], P(None, 'dp')
- grad_b_value: float32 [768], P('dp')
- grad_w_out: float32 [768, 768], P(None, 'dp')
- grad_b_out: float32 [768], P('dp')
- grad_gain_attn: float32 [768], P('dp')
- grad_shift_attn: float32 [768], P('dp')
- grad_w_up: float32 [768, 3072], P(None, 'dp')
- grad_b_up: float32 [3072], P('dp')
- grad_w_down: float32 [3072, 768], P(None, 'dp')
- grad_b_down: float32 [768], P('dp')
- grad_gain_ffn: float32 [768], P('dp')
- grad_shift_ffn: float32 [768], P('dp')
The draws below stay inside these ranges and needn't reach their ends.
Inputs may be any that keep to these rules, and one draw needn't show every extreme that they name: `seg_lengths`: in every row the 8 lengths are at least 1 and sum to 512; the longest in every row equals the stated maximum.
All inputs are finite; a program needn't handle non-finite values.
Results may differ from the reference program's by a relative error of at most 0.024.
Values may be sent and summed in bfloat16 or wider, within the bound.
No kernel may reach another device: no remote copies, remote signals or barrier semaphores. Data moves between devices by JAX's collectives and lax.ppermute only.
A program may use at most 192 MiB of HBM per device.

```python
import math
import jax
import jax.numpy as jnp
import numpy as np
from jax import lax

D = 768
H = 12
HD = 64
FF = 3072
L = 512
SEGS = 8
ROWS_DEV = 4
ROWS = 32
N_SEQ = 4


def block_scale(rng, dims, split, low, largest):
    def one(position, blocks):
        steps = jax.random.uniform(jax.random.fold_in(jax.random.fold_in(rng, 6), position), (blocks,), jnp.float32, low / len(split), largest / len(split))
        return jnp.repeat(jnp.exp(steps), dims[position] // blocks).reshape((-1,) + (1,) * (len(dims) - position - 1))

    level = one(*split[0])
    for cut in split[1:]:
        level = level * one(*cut)
    return level


def length_profile(number_of, total, reach, skew):
    loads = [(1 << 20) // math.isqrt(rank ** skew) + 1 for rank in range(2, number_of + 1)]
    surplus, holding = total - reach - (number_of - 1), [1] * (number_of - 1)
    while surplus > 0:
        free = [i for i in range(number_of - 1) if holding[i] < reach]
        whole, budget = sum([loads[i] for i in free]), surplus
        for i in free:
            more = min(reach - holding[i], max(1, budget * loads[i] // whole), surplus)
            holding[i] = holding[i] + more
            surplus = surplus - more
    return np.array([reach] + holding)


def uneven(own_key, count, total, reach, skew):
    if count == 2:
        one = jax.random.randint(own_key, (), max(1, total - reach), min(reach, total - 1) + 1)
        return jnp.stack([one, total - one])
    sizes = jnp.asarray(length_profile(count, total, reach, skew), jnp.int32)
    twos = (count - 1) // 2
    source_of, taker = sizes[1:1 + 2 * twos:2], sizes[2:2 + 2 * twos:2]
    margin = jnp.minimum(source_of - 1, reach - taker)
    passed = jax.random.randint(jax.random.fold_in(own_key, 1), (twos,), 0, 1 << 20) % (margin + 1)
    sizes = sizes.at[1:1 + 2 * twos:2].set(source_of - passed).at[2:2 + 2 * twos:2].set(taker + passed)
    return sizes[jax.random.permutation(jax.random.fold_in(own_key, 2), count)]


def scatter_about(stream_key, dims, width, most, split=(), held_as=jnp.bfloat16):
    values = jax.random.normal(stream_key, dims, jnp.float32) * width
    if len(split) > 0:
        values = block_scale(stream_key, dims, split, -0.22, 0.18) * values
    return jnp.clip(values, min=-most, max=most).astype(held_as)


def setup_inputs(seed: int = 0) -> dict:
    arg_keys = jax.random.split(jax.random.key(seed), 20)
    tokens = scatter_about(arg_keys[0], (ROWS, L, D), 1.0, 6.0, ((0, 8), (1, 4)))
    seg_lengths = jax.vmap(lambda own: uneven(own, SEGS, L, L - L // N_SEQ + SEGS, 2))(jax.random.split(arg_keys[1], ROWS)).reshape((ROWS, SEGS)).astype(jnp.int32)
    w_query = scatter_about(arg_keys[2], (D, D), (D // 2) ** -0.5, 0.3125)
    b_query = scatter_about(arg_keys[3], (D,), 0.5, 3.0)
    w_key = scatter_about(arg_keys[4], (D, D), (D // 2) ** -0.5, 0.3125)
    w_value = scatter_about(arg_keys[5], (D, D), D ** -0.5, 0.21875)
    b_value = scatter_about(arg_keys[6], (D,), 0.5, 3.0)
    w_out = scatter_about(arg_keys[7], (D, D), (D // 8) ** -0.5, 0.625)
    b_out = scatter_about(arg_keys[8], (D,), 0.5, 3.0)
    gain_attn = jnp.clip(1.0 + 0.15 * jax.random.normal(arg_keys[9], (D,), jnp.float32), 0.25, 1.75).astype(jnp.bfloat16)
    shift_attn = scatter_about(arg_keys[10], (D,), 0.5, 3.0)
    w_up = scatter_about(arg_keys[11], (D, FF), D ** -0.5, 0.21875)
    b_up = scatter_about(arg_keys[12], (FF,), 0.5, 3.0)
    w_down = scatter_about(arg_keys[13], (FF, D), FF ** -0.5, 0.109375)
    b_down = scatter_about(arg_keys[14], (D,), 0.5, 3.0)
    gain_ffn = jnp.clip(1.0 + 0.15 * jax.random.normal(arg_keys[15], (D,), jnp.float32), 0.25, 1.75).astype(jnp.bfloat16)
    shift_ffn = scatter_about(arg_keys[16], (D,), 0.5, 3.0)
    grad_output = scatter_about(arg_keys[17], (ROWS, L, D), 1.0, 6.0, ((0, 8), (1, 4)))
    grad_pooled = scatter_about(arg_keys[18], (ROWS, SEGS, D), 2.0, 12.0, ((0, 8),))
    return {"tokens": tokens, "seg_lengths": seg_lengths, "w_query": w_query, "b_query": b_query, "w_key": w_key, "w_value": w_value, "b_value": b_value, "w_out": w_out, "b_out": b_out, "gain_attn": gain_attn, "shift_attn": shift_attn, "w_up": w_up, "b_up": b_up, "w_down": w_down, "b_down": b_down, "gain_ffn": gain_ffn, "shift_ffn": shift_ffn, "grad_output": grad_output, "grad_pooled": grad_pooled}


epsilon = 1e-06
masked = -1e+30

@jax.custom_vjp
def low(v):
    return lax.optimization_barrier(v.astype(jnp.bfloat16)).astype(jnp.float32)

@jax.custom_vjp
def low_back(v):
    return v

def low_keep(v):
    return (low(v), None)

def low_pass(kept, grad):
    return (grad,)

def back_keep(v):
    return (v, None)

def back_low(kept, grad):
    return (low(grad),)
low.defvjp(low_keep, low_pass)
low_back.defvjp(back_keep, back_low)

def matmul(left, right):
    return jnp.dot(left, right, precision=lax.Precision.HIGHEST)

def layer_norm(value, gain, shift):
    centre = value - lax.optimization_barrier(jnp.mean(value, axis=-1, keepdims=True))
    inverse = lax.rsqrt(lax.optimization_barrier(jnp.mean(centre * centre, axis=-1, keepdims=True)) + epsilon)
    return centre * inverse * gain + shift

def segment_ids(lengths):
    seg_ends = jnp.cumsum(lengths, axis=1)
    places = jnp.arange(L, dtype=jnp.int32)
    return lax.optimization_barrier(jnp.sum((places[None, :, None] >= seg_ends[:, None, :]).astype(jnp.int32), axis=2))

def row_group(params, rows_in, lengths):
    w_query, b_query, w_key, w_value, b_value, w_out, b_out, gain_attn, shift_attn, w_up, b_up, w_down, b_down, gain_ffn, shift_ffn = params
    groups = rows_in.shape[0]
    flat_in = rows_in.reshape(groups * L, D)
    query = low(low_back(matmul(flat_in, w_query) + b_query))
    keys = low(low_back(matmul(flat_in, w_key)))
    values = low(low_back(matmul(flat_in, w_value) + b_value))
    head_shape = (groups, L, H, HD)
    scores = jnp.einsum('gqhd,gkhd->ghqk', query.reshape(head_shape), keys.reshape(head_shape), precision=lax.Precision.HIGHEST) * HD ** (-0.5)
    scores = low_back(scores)
    seg_rows = segment_ids(lengths)
    allowed = (seg_rows[:, :, None] == seg_rows[:, None, :])[:, None]
    scores = jnp.where(allowed, scores, masked)
    row_max = lax.optimization_barrier(jnp.max(scores, axis=-1, keepdims=True))
    expwts = jnp.where(allowed, jnp.exp(scores - row_max), 0.0)
    probability = expwts / lax.optimization_barrier(jnp.sum(expwts, axis=-1, keepdims=True))
    attended = jnp.einsum('ghqk,gkhd->gqhd', low(probability), values.reshape(head_shape), precision=lax.Precision.HIGHEST)
    attended = low(low_back(attended.reshape(groups * L, D)))
    mixed = low_back(matmul(attended, w_out) + b_out)
    hidden = layer_norm(flat_in + mixed, gain_attn, shift_attn)
    pre_act = low_back(matmul(low(hidden), w_up) + b_up)
    activated = low(jax.nn.gelu(pre_act, approximate=False))
    ffn_out = low_back(matmul(activated, w_down) + b_down)
    result = layer_norm(hidden + ffn_out, gain_ffn, shift_ffn)
    onehot = (seg_rows[:, :, None] == jnp.arange(SEGS, dtype=jnp.int32)[None, None, :]).astype(jnp.float32)
    result_rows = result.reshape(groups, L, D)
    sums = jnp.einsum('gls,gld->gsd', onehot, result_rows, precision=lax.Precision.HIGHEST)
    pooled = sums / lengths.astype(jnp.float32)[:, :, None]
    return (result_rows, pooled)

def reference(tokens, seg_lengths, w_query, b_query, w_key, w_value, b_value, w_out, b_out, gain_attn, shift_attn, w_up, b_up, w_down, b_down, gain_ffn, shift_ffn, grad_output, grad_pooled):
    params = tuple((weight.astype(jnp.float32) for weight in (w_query, b_query, w_key, w_value, b_value, w_out, b_out, gain_attn, shift_attn, w_up, b_up, w_down, b_down, gain_ffn, shift_ffn)))
    inputs = tokens.astype(jnp.float32)
    blocks = ROWS // ROWS_DEV

    def forward(weights, values_in):
        rows_in = values_in.reshape(blocks, ROWS_DEV, L, D)
        lengths = seg_lengths.reshape(blocks, ROWS_DEV, SEGS)

        def one_block(pair):
            return row_group(weights, pair[0], pair[1])
        result, pooled = lax.map(jax.checkpoint(one_block), (rows_in, lengths))
        return (result.reshape(ROWS, L, D), pooled.reshape(ROWS, SEGS, D))
    (result, pooled), pullback = jax.vjp(forward, params, inputs)
    grads, grad_in = pullback((grad_output.astype(jnp.float32), grad_pooled.astype(jnp.float32)))
    g_wq, g_bq, g_wk, g_wv, g_bv, g_wo, g_bo, g_ga, g_sa, g_wu, g_bu, g_wd, g_bd, g_gf, g_sf = grads
    return (result.astype(jnp.bfloat16), pooled, grad_in.astype(jnp.bfloat16), g_wq, g_bq, g_wk, g_wv, g_bv, g_wo, g_bo, g_ga, g_sa, g_wu, g_bu, g_wd, g_bd, g_gf, g_sf)
```

```python
import functools

import jax
import jax.numpy as jnp
from jax import lax
from jax.experimental import pallas as pl
from jax.experimental.pallas import tpu as pltpu
from jax.sharding import PartitionSpec as P

HD = 64
SEGS = 8
BF = jnp.bfloat16
F32 = jnp.float32
EPS = 1e-06
NEG = -1e30
LANES = 128
VMEM_BYTES = 56 * 1024 * 1024

PART = 16


def nn(a, b):
    return jnp.dot(a, b, preferred_element_type=F32)


def nt(a, b):
    return lax.dot_general(a, b, (((1,), (1,)), ((), ())), preferred_element_type=F32)


def three_parts(v):
    hi = v.astype(BF)
    rest = v - hi.astype(F32)
    mid = rest.astype(BF)
    low = (rest - mid.astype(F32)).astype(BF)
    return hi, mid, low


def two_parts(v):
    hi = v.astype(BF)
    return hi, (v - hi.astype(F32)).astype(BF)


def norm(value):
    centre = value - jnp.mean(value, axis=-1, keepdims=True)
    inverse = lax.rsqrt(jnp.mean(centre * centre, axis=-1, keepdims=True) + EPS)
    return centre * inverse, inverse


def norm_back(grad, normed, inverse):
    a = jnp.mean(grad, axis=-1, keepdims=True)
    b = jnp.mean(grad * normed, axis=-1, keepdims=True)
    return (grad - a - normed * b) * inverse


def gelu_both(x):
    z = jnp.abs(x) * (0.5**0.5)
    e = jnp.exp(-z * z)
    t = 1.0 / (1.0 + 0.3275911 * z)
    poly = t * (
        0.254829592
        + t * (-0.284496736 + t * (1.421413741 + t * (-1.453152027 + t * 1.061405429)))
    )
    tail = 0.5 * poly * e
    phi = jnp.where(x >= 0, 1.0 - tail, tail)
    return x * phi, phi + x * e * 0.3989422804014327


def head_lane(h):
    lane = lax.broadcasted_iota(jnp.int32, (1, LANES), 1)
    return (lane % PART == h) & (lane >= PART) & (lane < 4 * PART)


def put_shards(res, out_ref, info, lay, cols, first=0):
    n, rs, ra, hb = lay
    for j in range(n):
        pj = info[j]
        base = j * rs
        out_ref[pj, pl.ds(first, ra), cols] = res[base : base + ra].astype(BF)
        for a in range(2 if hb else 0):
            yrow = first + ra + jnp.where(info[9] == a, 0, hb)
            at = base + ra + a * hb
            out_ref[pj, pl.ds(pl.multiple_of(yrow, 16), hb), cols] = res[at : at + hb].astype(BF)


def split_kernel(info, x_ref, g_ref, *outs):
    me = info[10]
    for r in range(4):
        outs[r][...] = x_ref[me ^ r]
        outs[4 + r][...] = g_ref[me ^ r]


def join_kernel(info, *refs):
    me = info[10]
    out = refs[-1]
    for r in range(4):
        out[me ^ r] = refs[r][...]


def attend_kernel(
    x0, x1, x2, x3, oh_ref, ka_ref, wq, bq, wk, wv, bv, wo, bo,
    x_out, q_out, k_out, v_out, att_out, n1_out, inv_out, qa_out, stat,
):
    n = x0.shape[0]
    for r, ref in enumerate((x0, x1, x2, x3)):
        x_out[r * n : (r + 1) * n] = ref[...]
    x = x_out[...]
    q_out[...] = ((nn(x, wq[...]) + bq[...]).astype(BF).astype(F32) * (HD**-0.5)).astype(BF)
    k_out[...] = nn(x, wk[...]).astype(BF)
    v_out[...] = (nn(x, wv[...]) + bv[...]).astype(BF)
    tok, width = x.shape
    stat[...] = jnp.zeros_like(stat)
    ones = jnp.ones((16, tok), BF)

    def pair(p, carry):
        sl = pl.ds(pl.multiple_of(p * LANES, LANES), LANES)
        qcat = jnp.concatenate([q_out[:, sl], oh_ref[...]], axis=1)
        kp = k_out[:, sl]
        vt = v_out[:, sl].T
        lane = lax.broadcasted_iota(jnp.int32, (1, LANES), 1)
        parts = []
        for h in range(2):
            kh = jnp.where((lane < HD) == (h == 0), kp, jnp.zeros_like(kp))
            st = nt(jnp.concatenate([kh, ka_ref[...]], axis=1), qcat)
            m = jnp.max(st, axis=0, keepdims=True)
            pb = jnp.exp(st - m).astype(BF)
            ot = nn(jnp.concatenate([vt[h * HD : (h + 1) * HD], ones], axis=0), pb)
            total = ot[HD : HD + 1]
            stat[pl.ds(2 * p + h, 1), :] = m + jnp.log(total)
            parts.append(ot[:HD] / total)
        att_out[:, sl] = jnp.concatenate(parts, axis=0).T
        return carry

    lax.fori_loop(0, width // LANES, pair, 0)
    hi, mid, low = three_parts(stat[...])
    zero = jnp.zeros((PART, tok), BF)
    qa_out[...] = jnp.concatenate([zero, hi, mid, low, zero, zero, zero, zero], axis=0).T + oh_ref[...]
    mixed = nn(att_out[...].astype(BF), wo[...]) + bo[...]
    n1, inv = norm(x.astype(F32) + mixed)
    n1_out[...] = n1
    inv_out[...] = jnp.broadcast_to(inv, inv_out.shape)


def ffn_kernel(
    lay, info, n1_ref, ga, sa, wu, bu, wd, bd, gf, sf, g0, g1, g2, g3, oh_ref, oht_ref, gpl,
    o0, o1, o2, o3, pool_out, r2_out, gp_out, vec_out, send, keep,
    hl, acc, act, gt,
):
    t = pl.program_id(0)
    tile = wu.shape[1]
    n = g0.shape[0]

    @pl.when(t == 0)
    def _():
        hl[...] = (n1_ref[...] * ga[...] + sa[...]).astype(BF)
        acc[...] = jnp.zeros_like(acc)

    for r in range(4):
        rows = pl.ds(r * n, n)
        pre = nn(hl[rows, :], wu[...]) + bu[...]
        a, d = gelu_both(pre)
        ab = a.astype(BF)
        act[rows, pl.ds(pl.multiple_of(t * tile, tile), tile)] = ab
        gp_out[rows, :] = d.astype(BF)
        acc[rows, :] += nn(ab, wd[...])

    @pl.when(t == pl.num_programs(0) - 1)
    def _():
        width = acc.shape[1]
        gain = jnp.zeros((1, width), F32)
        shift = jnp.zeros((1, width), F32)
        bias = jnp.zeros((1, width), F32)
        pool = jnp.zeros(pool_out.shape, F32)
        for r, (o, g) in enumerate(((o0, g0), (o1, g1), (o2, g2), (o3, g3))):
            rows = pl.ds(r * n, n)
            hidden = n1_ref[rows, :] * ga[...] + sa[...]
            n2, inv = norm(hidden + (acc[rows, :] + bd[...]))
            result = n2 * gf[...] + sf[...]
            o[...] = result.astype(BF)
            hi, low = two_parts(result)
            oht = oht_ref[:, r * n : (r + 1) * n]
            pool += nn(oht, hi) + nn(oht, low)
            oh = oh_ref[rows, :]
            gout = g[...].astype(F32) + nn(jnp.concatenate([oh, oh], axis=1), gpl[...])
            gain += jnp.sum(gout * n2, axis=0, keepdims=True)
            shift += jnp.sum(gout, axis=0, keepdims=True)
            gr2 = norm_back(gout * gf[...], n2, inv)
            r2_out[rows, :] = gr2
            low_g = gr2.astype(BF)
            bias += jnp.sum(low_g.astype(F32), axis=0, keepdims=True)
            gt[:, r * n : (r + 1) * n] = low_g.T
        pool_out[...] = pool
        vec_out[...] = jnp.concatenate([bias, gain, shift, jnp.zeros((5, width), F32)], axis=0)
        half = act.shape[1] // 2
        step = 256

        def piece(i, carry):
            for rc, ref in ((1, send), (0, keep)):
                at = (info[8] ^ rc) * half + i * step
                res = nn(gt[...], act[:, pl.ds(pl.multiple_of(at, step), step)])
                put_shards(res, ref, info, lay, pl.ds(pl.multiple_of(i * step, step), step))
            return carry

        lax.fori_loop(0, half // step, piece, 0)


def ffn_back_kernel(
    lay_up, lay_out, info, r2_ref, gp, wd, wu, n1_ref, inv_ref, ga, sa, wo, att,
    send, keep, bup_out, r1_out, gatt_out, gaug_out, vec_out, osend, okeep,
    gl, hlt, acc, gt,
):
    t = pl.program_id(0)
    width = acc.shape[1]
    half = width // 2

    @pl.when(t == 0)
    def _():
        gl[...] = r2_ref[...].astype(BF)
        hlt[...] = (n1_ref[...] * ga[...] + sa[...]).astype(BF).T
        acc[...] = r2_ref[...]

    gpre = (nt(gl[...], wd[...]) * gp[...].astype(F32)).astype(BF)
    bup_out[...] = jnp.broadcast_to(
        jnp.sum(gpre.astype(F32), axis=0, keepdims=True), bup_out.shape
    )
    acc[...] += nt(gpre, wu[...])
    ra, hb = lay_up
    for rc, ref in ((1, send), (0, keep)):
        at = pl.multiple_of((info[8] ^ rc) * half, half)
        res = nn(hlt[pl.ds(at, half), :], gpre).astype(BF)
        ref[0, :ra, :] = res[:ra]
        for a in range(2 if hb else 0):
            yrow = ra + jnp.where(info[9] == a, 0, hb)
            ref[0, pl.ds(pl.multiple_of(yrow, 16), hb), :] = res[ra + a * hb : ra + (a + 1) * hb]

    @pl.when(t == pl.num_programs(0) - 1)
    def _():
        n = acc.shape[0] // 4
        gain = jnp.zeros((1, width), F32)
        shift = jnp.zeros((1, width), F32)
        bias = jnp.zeros((1, width), F32)
        row = lax.broadcasted_iota(jnp.int32, (width, LANES), 0) // HD
        lane = lax.broadcasted_iota(jnp.int32, (width, LANES), 1)
        pick = ((lane % PART == row) & (lane >= PART) & (lane < 4 * PART)).astype(BF)
        lane1 = lax.broadcasted_iota(jnp.int32, (1, LANES), 1)
        for r in range(4):
            rows = pl.ds(r * n, n)
            gh = acc[rows, :]
            n1 = n1_ref[rows, :]
            gain += jnp.sum(gh * n1, axis=0, keepdims=True)
            shift += jnp.sum(gh, axis=0, keepdims=True)
            gr1 = norm_back(gh * ga[...], n1, inv_ref[rows, :1])
            r1_out[rows, :] = gr1
            gm = gr1.astype(BF)
            bias += jnp.sum(gm.astype(F32), axis=0, keepdims=True)
            gt[:, r * n : (r + 1) * n] = gm.T
            gatt = nt(gm, wo[...]).astype(BF)
            gatt_out[rows, :] = gatt
            a, b, c = three_parts(gatt.astype(F32) * att[rows, :])
            delta = nn(a, pick) + nn(b, pick) + nn(c, pick)
            a, b, c = three_parts(delta)
            gaug_out[rows, :] = jnp.where(lane1 < 2 * PART, a, jnp.where(lane1 < 3 * PART, b, c))
        vec_out[...] = jnp.concatenate([bias, gain, shift, jnp.zeros((5, width), F32)], axis=0)
        step = 128

        def piece(i, carry):
            for rc, ref in ((1, osend), (0, okeep)):
                at = (info[8] ^ rc) * half + i * step
                right = att[:, pl.ds(pl.multiple_of(at, step), step)].astype(BF)
                res = nn(gt[...], right)
                put_shards(res, ref, info, lay_out, pl.ds(pl.multiple_of(i * step, step), step))
            return carry

        lax.fori_loop(0, half // step, piece, 0)


def attend_back_kernel(
    lay, info, q, k, v, g, qa, ka, ga, x_ref, vecs, bups,
    gq_out, gk_out, gv_out, send, keep, vec_out,
    gqt, gkt, gvt,
):
    width = q.shape[1]
    tok = q.shape[0]

    def pair(p, carry):
        sl = pl.ds(pl.multiple_of(p * LANES, LANES), LANES)
        qp, kp, vp, gp = q[:, sl], k[:, sl], v[:, sl], g[:, sl]
        qcat = jnp.concatenate([qp, qa[...]], axis=1)
        gcat = jnp.concatenate([gp, ga[...]], axis=1)
        kt = kp.T
        lane = lax.broadcasted_iota(jnp.int32, (1, LANES), 1)
        gk = jnp.zeros((tok, LANES), F32)
        gv = jnp.zeros((tok, LANES), F32)
        parts = []
        zero = jnp.zeros_like(kp)
        for h in range(2):
            mine = (lane < HD) == (h == 0)
            pick = head_lane(2 * p + h)
            kaug = jnp.where(pick, -jnp.ones((), BF), ka[...])
            vaug = jnp.where(pick, -jnp.ones((), BF), jnp.zeros((tok, LANES), BF))
            prob = jnp.exp(nt(jnp.concatenate([jnp.where(mine, kp, zero), kaug], axis=1), qcat))
            dp = nt(jnp.concatenate([jnp.where(mine, vp, zero), vaug], axis=1), gcat)
            ds = (prob * dp).astype(BF)
            gv += nn(prob.astype(BF), jnp.where(mine, gp, zero))
            gk += nn(ds, jnp.where(mine, qp, zero))
            parts.append(nn(kt[h * HD : (h + 1) * HD], ds))
        gqp = (jnp.concatenate(parts, axis=0) * (HD**-0.5)).astype(BF)
        gqt[sl, :] = gqp
        gq_out[:, sl] = gqp.T
        gkb, gvb = gk.astype(BF), gv.astype(BF)
        gk_out[:, sl] = gkb
        gv_out[:, sl] = gvb
        gkt[sl, :] = gkb.T
        gvt[sl, :] = gvb.T
        return carry

    lax.fori_loop(0, width // LANES, pair, 0)
    bq = jnp.sum(gq_out[...].astype(F32), axis=0, keepdims=True)
    bv = jnp.sum(gv_out[...].astype(F32), axis=0, keepdims=True)
    allv = jnp.concatenate([bq, bv, vecs[...]], axis=0)
    vec_out[...] = allv
    half = width // 2
    n, rs, ra, hb = lay
    rows_a = 3 * ra + 16
    if n > 1:
        lanes = rs
        for j in range(n):
            bup = bups[:, j * 4 * lanes : (j + 1) * 4 * lanes]
            block = jnp.concatenate(
                [allv[:8, j * lanes : (j + 1) * lanes]]
                + [bup[:, c * lanes : (c + 1) * lanes] for c in range(4)]
                + [jnp.zeros((4, lanes), F32)],
                axis=0,
            )
            block = jnp.concatenate([block, jnp.zeros((16, half - lanes), F32)], axis=1)
            pj = info[j]
            first = jnp.where(info[8] == 0, 1.0, 0.0)
            keep[pj, 3 * ra : rows_a, :] = (block * first).astype(BF)
            send[pj, 3 * ra : rows_a, :] = (block * (1.0 - first)).astype(BF)
    step = 128

    def piece(i, carry):
        cols = pl.ds(pl.multiple_of(i * step, step), step)
        for rc, ref in ((1, send), (0, keep)):
            at = (info[8] ^ rc) * half + i * step
            right = x_ref[:, pl.ds(pl.multiple_of(at, step), step)]
            for w, left in enumerate((gqt, gkt, gvt)):
                res = nn(left[...], right)
                for j in range(n):
                    pj = info[j]
                    base = j * rs
                    ref[pj, pl.ds(w * ra, ra), cols] = res[base : base + ra].astype(BF)
                    for a in range(2 if hb else 0):
                        yrow = rows_a + jnp.where(info[9] == a, 0, 3 * hb) + w * hb
                        s = base + ra + a * hb
                        ref[pj, pl.ds(pl.multiple_of(yrow, 16), hb), cols] = res[s : s + hb].astype(BF)
        return carry

    lax.fori_loop(0, half // step, piece, 0)


def input_kernel(r1, gq, gk, gv, wq, wk, wv, o0, o1, o2, o3):
    n = o0.shape[0]
    for r, o in enumerate((o0, o1, o2, o3)):
        rows = pl.ds(r * n, n)
        o[...] = (
            r1[rows, :]
            + nt(gq[rows, :], wq[...])
            + nt(gk[rows, :], wk[...])
            + nt(gv[rows, :], wv[...])
        ).astype(BF)


WHOLE = pl.BlockSpec(memory_space=pltpu.VMEM)
SCALARS = pl.BlockSpec(memory_space=pltpu.SMEM)


def shape(dims, dtype=BF):
    return jax.ShapeDtypeStruct(tuple(dims), dtype)


def params():
    return pltpu.CompilerParams(vmem_limit_bytes=VMEM_BYTES)


def call(kernel, outs, args, scalars=(), scratch=(), name=None, flops=0, nbytes=0):
    ins = [SCALARS if i in scalars else WHOLE for i in range(len(args))]
    return pl.pallas_call(
        kernel,
        out_shape=outs,
        in_specs=ins,
        out_specs=jax.tree.map(lambda _: WHOLE, outs),
        scratch_shapes=list(scratch),
        compiler_params=params(),
        cost_estimate=pl.CostEstimate(flops=flops, bytes_accessed=nbytes, transcendentals=0),
        name=name,
    )(*args)


def relative(x, axis_pairs):
    return lax.ppermute(x, "seq", axis_pairs)


def add(a, b):
    return (a.astype(F32) + b.astype(F32)).astype(BF)


def local(n_dp, n_seq, *args):
    (
        tokens, seg_lengths, w_query, b_query, w_key, w_value, b_value, w_out, b_out,
        gain_attn, shift_attn, w_up, b_up, w_down, b_down, gain_ffn, shift_ffn,
        grad_output, grad_pooled,
    ) = args
    me = lax.axis_index("seq")
    dp = lax.axis_index("dp")
    core, y = me % 2, me // 2
    rows, piece, width = tokens.shape
    tok = n_seq * piece
    ff = w_up.shape[1]
    fast = n_dp == 8
    n = n_dp if fast else 1
    rs = width // n
    half = width // 2
    xor = [[(i, i ^ r) for i in range(n_seq)] for r in range(n_seq)]

    if fast:
        j = jnp.arange(8, dtype=jnp.int32)
        pos = ((j % 2) ^ (dp % 2)) * 4 + ((j // 2) - (dp // 2)) % 4
    else:
        pos = jnp.zeros((8,), jnp.int32)
    info = jnp.concatenate([pos, jnp.stack([core, y, me]), jnp.zeros((5,), jnp.int32)]).astype(jnp.int32)

    pieces = call(
        split_kernel, [shape((piece, width))] * 8, (info, tokens, grad_output), scalars=(0,), name="split"
    )
    xs = [pieces[0]] + [lax.ppermute(pieces[r], "seq", xor[r]) for r in range(1, 4)]
    gs = [pieces[4]] + [lax.ppermute(pieces[4 + r], "seq", xor[r]) for r in range(1, 4)]

    lengths = lax.dynamic_index_in_dim(seg_lengths, me, 0, keepdims=False)
    ends = jnp.cumsum(lengths)
    order = me ^ jnp.arange(n_seq, dtype=jnp.int32)
    places = (order[:, None] * piece + jnp.arange(piece, dtype=jnp.int32)[None, :]).reshape(tok)
    seg = jnp.sum((places[:, None] >= ends[None, :]).astype(jnp.int32), axis=1)
    lane = jnp.arange(LANES, dtype=jnp.int32)
    hot = seg[:, None] == lane[None, :]
    onehot = hot.astype(BF)
    kaug = jnp.where((lane < SEGS)[None, :] & ~hot, NEG, 0.0).astype(BF)
    onehot_t = (seg[None, :] == jnp.arange(16, dtype=jnp.int32)[:, None]).astype(BF)
    length_col = lengths.astype(F32)[:, None]
    gpool = lax.dynamic_index_in_dim(grad_pooled, me, 0, keepdims=False).astype(F32) / length_col
    gp_hi = gpool.astype(BF)
    gp_low = (gpool - gp_hi.astype(F32)).astype(BF)
    zeros = jnp.zeros((LANES - SEGS, width), BF)
    gpl = jnp.concatenate([gp_hi, zeros, gp_low, zeros], axis=0)

    def vec(v):
        return v.astype(F32).reshape(1, -1)

    sq = shape((tok, width))
    sqf = shape((tok, width), F32)
    x, q, k, v, att, n1, inv, qaug = call(
        attend_kernel,
        [sq, sq, sq, sq, sqf, sqf, shape((tok, LANES), F32), shape((tok, LANES))],
        (*xs, onehot, kaug, w_query, vec(b_query), w_key, w_value, vec(b_value), w_out, vec(b_out)),
        scratch=[pltpu.VMEM((PART, tok), F32)],
        name="attend",
    )

    ra_d, hb_d = (64, 16) if fast else (width, 0)
    lay_d = (n, rs, ra_d, hb_d)
    rows_d = ra_d + 2 * hb_d
    tile = 768
    const = lambda *_: (0, 0)
    full = lambda a, b: pl.BlockSpec((a, b), const)
    vspec = full(1, width)
    pspec = full(piece, width)
    half_ff = ff // 2
    wire_d = shape((n, rows_d, half_ff))
    wire_spec = lambda dims: pl.BlockSpec(dims, lambda *_: (0,) * len(dims))
    *outs, pool, r2, gp, vec_b, d_send, d_keep = pl.pallas_call(
        functools.partial(ffn_kernel, lay_d),
        grid_spec=pltpu.PrefetchScalarGridSpec(
            num_scalar_prefetch=1,
            grid=(ff // tile,),
            in_specs=[
                full(tok, width), vspec, vspec,
                pl.BlockSpec((width, tile), lambda t, s: (0, t)),
                pl.BlockSpec((1, tile), lambda t, s: (0, t)),
                pl.BlockSpec((tile, width), lambda t, s: (t, 0)),
                vspec, vspec, vspec, pspec, pspec, pspec, pspec,
                full(tok, LANES), full(16, tok), full(2 * LANES, width),
            ],
            out_specs=[
                pspec, pspec, pspec, pspec, full(16, width), full(tok, width),
                pl.BlockSpec((tok, tile), lambda t, s: (0, t)),
                full(8, width), wire_spec(wire_d.shape), wire_spec(wire_d.shape),
            ],
            scratch_shapes=[
                pltpu.VMEM((tok, width), BF), pltpu.VMEM((tok, width), F32),
                pltpu.VMEM((tok, ff), BF), pltpu.VMEM((width, tok), BF),
            ],
        ),
        out_shape=[shape((piece, width))] * 4
        + [shape((16, width), F32), sqf, shape((tok, ff)), shape((8, width), F32), wire_d, wire_d],
        compiler_params=params(),
        name="ffn",
    )(
        info, n1, vec(gain_attn), vec(shift_attn), w_up, vec(b_up), w_down, vec(b_down),
        vec(gain_ffn), vec(shift_ffn), *gs, onehot, onehot_t, gpl,
    )

    ra_u, hb_u = (256, 64) if fast else (half, 0)
    lay_o = lay_d
    tile = 384
    steps = ff // tile
    wire_u = shape((n, half, ff // n))
    wire_o = shape((n, rows_d, half))
    if fast:
        up_spec = pl.BlockSpec((1, half, tile), lambda t, s: (s[t], 0, 0))
    else:
        up_spec = pl.BlockSpec((1, half, tile), lambda t, s: (0, 0, t))
    u_send, u_keep, bup, r1, gatt, gaug, vec_c, o_send, o_keep = pl.pallas_call(
        functools.partial(ffn_back_kernel, (ra_u, hb_u), lay_o),
        grid_spec=pltpu.PrefetchScalarGridSpec(
            num_scalar_prefetch=1,
            grid=(steps,),
            in_specs=[
                full(tok, width),
                pl.BlockSpec((tok, tile), lambda t, s: (0, t)),
                pl.BlockSpec((tile, width), lambda t, s: (t, 0)),
                pl.BlockSpec((width, tile), lambda t, s: (0, t)),
                full(tok, width), full(tok, LANES), vspec, vspec, full(width, width), full(tok, width),
            ],
            out_specs=[
                up_spec, up_spec, pl.BlockSpec((8, tile), lambda t, s: (0, t)),
                full(tok, width), full(tok, width), full(tok, LANES), full(8, width),
                wire_spec(wire_o.shape), wire_spec(wire_o.shape),
            ],
            scratch_shapes=[
                pltpu.VMEM((tok, width), BF), pltpu.VMEM((width, tok), BF),
                pltpu.VMEM((tok, width), F32), pltpu.VMEM((width, tok), BF),
            ],
        ),
        out_shape=[
            wire_u, wire_u, shape((8, ff), F32), sqf, sq, shape((tok, LANES)), shape((8, width), F32),
            wire_o, wire_o,
        ],
        compiler_params=params(),
        name="ffn_back",
    )(info, r2, gp, w_down, w_up, n1, inv, vec(gain_attn), vec(shift_attn), w_out, att)

    rows_q = 3 * rs + 16
    wire_q = shape((n, rows_q, half))
    vecs = jnp.concatenate([vec_c[:3], vec_b[:3], jnp.zeros((8, width), F32)], axis=0)
    gq, gk, gv, q_send, q_keep, vec_all = call(
        functools.partial(attend_back_kernel, lay_d),
        [sq, sq, sq, wire_q, wire_q, shape((16, width), F32)],
        (info, q, k, v, gatt, qaug, kaug, gaug, x, vecs, bup[:1]),
        scalars=(0,),
        scratch=[pltpu.VMEM((width, tok), BF)] * 3,
        name="attend_back",
    )
    ins = call(
        input_kernel, [shape((piece, width))] * 4, (r1, gq, gk, gv, w_query, w_key, w_value), name="input"
    )

    def back(parts, name):
        got = [parts[0]] + [lax.ppermute(parts[r], "seq", xor[r]) for r in range(1, 4)]
        return call(join_kernel, shape((rows, piece, width)), (info, *got), scalars=(0,), name=name)

    output = back(outs, "join_out")
    grad_tokens = back(ins, "join_in")
    own = pool[:SEGS] / length_col
    got = [own] + [lax.ppermute(own, "seq", xor[r]) for r in range(1, 4)]
    pooled = call(
        join_kernel, shape((rows, SEGS, width), F32), (info, *got), scalars=(0,), name="join_pool"
    )

    if fast:
        def reduce_all(send, keep, ra, hb):
            pp_core = lambda a: lax.ppermute(a, "seq", xor[1])
            pp_y = lambda a: lax.ppermute(a, "seq", xor[2])
            pp_x = lambda a: lax.ppermute(a, "dp", [(i, i ^ 1) for i in range(8)])
            pp_z = lambda a: lax.ppermute(a, "dp", [(i, (i + 2) % 8) for i in range(8)])

            def along_z(got, own):
                moving = add(got[3], own[3])
                for s in (2, 1, 0):
                    moving = (
                        got[s].astype(F32) + own[s].astype(F32) + pp_z(moving).astype(F32)
                    ).astype(BF)
                return moving

            r = pp_core(send)
            a1 = add(r[4:, :ra], keep[4:, :ra])
            b1 = add(r[:, ra + hb :], keep[:, ra + hb :])
            ax, by = pp_x(a1), pp_y(b1)
            a0 = add(r[:4, :ra], keep[:4, :ra])
            b0 = add(r[:, ra : ra + hb], keep[:, ra : ra + hb])
            a = along_z(ax, a0)
            b1 = add(by[4:], b0[4:])
            bx = pp_x(b1)
            b = along_z(bx, add(by[:4], b0[:4]))
            a = add(a, pp_y(a))
            b2 = pp_y(b)
            mine = jnp.concatenate([a, jnp.where(y == 0, b, b2), jnp.where(y == 0, b2, b)], axis=0)
            other = pp_core(mine)
            return jnp.where(core == 0, mine, other), jnp.where(core == 0, other, mine)

        dl, dh = reduce_all(d_send, d_keep, ra_d, hb_d)
        ul, uh = reduce_all(u_send, u_keep, ra_u, hb_u)
        ol, oh = reduce_all(o_send, o_keep, ra_d, hb_d)
        ql, qh = reduce_all(q_send, q_keep, 3 * ra_d + 16, 3 * hb_d)
        g_down = jnp.concatenate([dl, dh], axis=1).astype(F32).T
        g_up = jnp.concatenate([ul, uh], axis=0).astype(F32)
        g_out = jnp.concatenate([ol, oh], axis=1).astype(F32).T
        qf = jnp.concatenate([ql, qh], axis=1)
        at_b = 3 * ra_d + 16
        g_qkv = []
        for w in range(3):
            part = [qf[w * ra_d : (w + 1) * ra_d]] + [
                qf[at_b + (3 * a + w) * hb_d : at_b + (3 * a + w + 1) * hb_d] for a in range(2)
            ]
            g_qkv.append(jnp.concatenate(part, axis=0).astype(F32).T)
        vs = ql[3 * ra_d : 3 * ra_d + 16, :rs].astype(F32)
        small = [vs[i] for i in range(8)] + [vs[8:12].reshape(-1)]
    else:
        def total(send, keep, dim):
            h = keep.astype(F32) + lax.ppermute(send, "seq", xor[1]).astype(F32)
            h = (h + lax.ppermute(h.astype(BF), "seq", xor[2]).astype(F32))
            return lax.psum_scatter(h, "dp", scatter_dimension=dim, tiled=True).astype(BF)

        def whole(send, keep, dim, along):
            mine = total(send, keep, dim)
            other = lax.ppermute(mine, "seq", xor[1])
            lo, hi = jnp.where(core == 0, mine, other), jnp.where(core == 0, other, mine)
            return jnp.concatenate([lo, hi], axis=along).astype(F32)

        g_down = whole(d_send[0], d_keep[0], 0, 1).T
        g_up = whole(u_send[0], u_keep[0], 1, 0)
        g_out = whole(o_send[0], o_keep[0], 0, 1).T
        g_qkv = [
            whole(q_send[0, w * width : (w + 1) * width], q_keep[0, w * width : (w + 1) * width], 0, 1).T
            for w in range(3)
        ]
        flat = lax.psum(jnp.concatenate([vec_all[:8].reshape(-1), bup[0]]), ("dp", "seq"))
        mine = width // n_dp
        small = [
            lax.dynamic_slice_in_dim(flat, i * width + dp * mine, mine) for i in range(8)
        ] + [lax.dynamic_slice_in_dim(flat, 8 * width + dp * 4 * mine, 4 * mine)]

    bq, bv, b_o, gain1, shift1, b_d, gain2, shift2, b_u = small
    return (
        output, pooled, grad_tokens, g_qkv[0], bq, g_qkv[1], g_qkv[2], bv, g_out, b_o, gain1, shift1,
        g_up, b_u, g_down, b_d, gain2, shift2,
    )


def solution(mesh):
    rows = P("dp", "seq", None)
    placed = (rows, P("dp", None)) + (P(),) * 15 + (rows, P("dp", None, None))
    col, one = P(None, "dp"), P("dp")
    return jax.shard_map(
        functools.partial(local, mesh.shape["dp"], mesh.shape["seq"]),
        mesh=mesh,
        in_specs=placed,
        out_specs=(
            rows, P("dp", None, None), rows, col, one, col, col, one, col, one, one, one,
            col, one, col, one, one, one,
        ),
        check_vma=False,
    )
```

```python
import functools

import jax
import jax.numpy as jnp
from jax import lax
from jax.experimental import pallas as pl
from jax.experimental.pallas import tpu as pltpu
from jax.sharding import PartitionSpec as P

HD = 64
SEGS = 8
BF = jnp.bfloat16
F32 = jnp.float32
EPS = 1e-06
NEG = -1e30
LANES = 128

PART = 16


def nn(a, b):
    return jnp.dot(a, b, preferred_element_type=F32)


def nt(a, b):
    return lax.dot_general(a, b, (((1,), (1,)), ((), ())), preferred_element_type=F32)


def three_parts(v):
    hi = v.astype(BF)
    rest = v - hi.astype(F32)
    mid = rest.astype(BF)
    low = (rest - mid.astype(F32)).astype(BF)
    return hi, mid, low


def two_parts(v):
    hi = v.astype(BF)
    return hi, (v - hi.astype(F32)).astype(BF)


def norm(value):
    centre = value - jnp.mean(value, axis=-1, keepdims=True)
    inverse = lax.rsqrt(jnp.mean(centre * centre, axis=-1, keepdims=True) + EPS)
    return centre * inverse, inverse


def norm_back(grad, normed, inverse):
    a = jnp.mean(grad, axis=-1, keepdims=True)
    b = jnp.mean(grad * normed, axis=-1, keepdims=True)
    return (grad - a - normed * b) * inverse


def gelu_both(x):
    phi = 0.5 + 0.5 * lax.erf(x * (0.5**0.5))
    density = 0.3989422804014327 * jnp.exp(x * x * -0.5)
    return x * phi, phi + x * density


def head_lane(h):
    lane = lax.broadcasted_iota(jnp.int32, (1, LANES), 1)
    return (lane % PART == h) & (lane >= PART) & (lane < 4 * PART)


def put_rows(out_ref, lead, y, rows, halves, cols, value):
    n = value.shape[0] // halves
    for a in range(halves):
        side = jnp.where(y == a, 0, 1) if halves > 1 else 0
        out_ref[side, lead, pl.ds(rows, n), cols] = value[a * n : (a + 1) * n].astype(BF)


def put_shards(out_ref, info, lay, cols, value, rows=0, first=0):
    n, halves, rs = lay
    count = value.shape[0] // rs
    for i in range(count):
        lead = info[first * count + i] if n > 1 else 0
        put_rows(out_ref, lead, info[9], rows, halves, cols, value[i * rs : (i + 1) * rs])


def copies(pairs, sems, first=0):
    out = []
    for i, (src, dst) in enumerate(pairs):
        out.append(pltpu.make_async_copy(src, dst, sems.at[first + i]))
        out[-1].start()
    return out


def wait(moves):
    for m in moves:
        m.wait()


def split_kernel(info, x_ref, *refs):
    outs, sems = refs[:-1], refs[-1]
    wait(copies([(x_ref.at[info[10] ^ r], outs[r]) for r in range(len(outs))], sems))


def join_kernel(info, *refs):
    me = info[10]
    out = refs[-1]
    for r in range(4):
        out[me ^ r] = refs[r][...]


def attend_kernel(
    x0, x1, x2, x3, wq_h, wk_h, wv_h, wo_h, oh_ref, ka_ref, bq, bv, bo,
    x_h, q_h, k_h, v_h, att_h, inv_h, qa_h, n1_out,
    x_out, q_out, k_out, v_out, att_out, inv_out, qa_out, wq, wk, wv, wo, stat, sems,
):
    n = x0.shape[0]
    ws = copies([(wq_h, wq), (wk_h, wk), (wv_h, wv), (wo_h, wo)], sems, 4)
    for r, ref in enumerate((x0, x1, x2, x3)):
        x_out[r * n : (r + 1) * n] = ref[...]
    outs = copies([(x_out, x_h)], sems, 8)
    x = x_out[...]
    ws[0].wait()
    q_out[...] = ((nn(x, wq[...]) + bq[...]).astype(BF).astype(F32) * (HD**-0.5)).astype(BF)
    outs += copies([(q_out, q_h)], sems, 9)
    ws[1].wait()
    k_out[...] = nn(x, wk[...]).astype(BF)
    outs += copies([(k_out, k_h)], sems, 10)
    ws[2].wait()
    v_out[...] = (nn(x, wv[...]) + bv[...]).astype(BF)
    outs += copies([(v_out, v_h)], sems, 11)
    tok, width = x.shape
    stat[...] = jnp.zeros_like(stat)
    ones = jnp.ones((16, tok), BF)

    def pair(p, carry):
        sl = pl.ds(pl.multiple_of(p * LANES, LANES), LANES)
        qcat = jnp.concatenate([q_out[:, sl], oh_ref[...]], axis=1)
        kp = k_out[:, sl]
        vt = v_out[:, sl].T
        lane = lax.broadcasted_iota(jnp.int32, (1, LANES), 1)
        parts = []
        for h in range(2):
            kh = jnp.where((lane < HD) == (h == 0), kp, jnp.zeros_like(kp))
            st = nt(jnp.concatenate([kh, ka_ref[...]], axis=1), qcat)
            m = jnp.max(st, axis=0, keepdims=True)
            pb = jnp.exp(st - m).astype(BF)
            ot = nn(jnp.concatenate([vt[h * HD : (h + 1) * HD], ones], axis=0), pb)
            total = ot[HD : HD + 1]
            stat[pl.ds(2 * p + h, 1), :] = m + jnp.log(total)
            parts.append(ot[:HD] / total)
        att_out[:, sl] = jnp.concatenate(parts, axis=0).T
        return carry

    lax.fori_loop(0, width // LANES, pair, 0)
    outs += copies([(att_out, att_h)], sems, 12)
    hi, mid, low = three_parts(stat[...])
    zero = jnp.zeros((PART, tok), BF)
    qa_out[...] = jnp.concatenate([zero, hi, mid, low, zero, zero, zero, zero], axis=0).T + oh_ref[...]
    outs += copies([(qa_out, qa_h)], sems, 13)
    ws[3].wait()
    mixed = nn(att_out[...].astype(BF), wo[...]) + bo[...]
    n1, inv = norm(x.astype(F32) + mixed)
    n1_out[...] = n1
    inv_out[...] = jnp.broadcast_to(inv, inv_out.shape)
    outs += copies([(inv_out, inv_h)], sems, 14)
    wait(outs)


def ffn_kernel(
    lay, info, n1_ref, ga, sa, wu, bu, wd, bd, gf, sf, g0, g1, g2, g3, oh_ref, oht_ref, gpl,
    o0, o1, o2, o3, gp_h, send, keep, pool_out, r2_out, vec_out,
    hl, acc, act, gt, gp_out, sem_g,
):
    n = g0.shape[0]
    tok, width = acc.shape
    ff = act.shape[1]
    tile = width
    steps = ff // tile

    def slopes(t):
        cols = pl.ds(pl.multiple_of(t * tile, tile), tile)
        return pltpu.make_async_copy(gp_out.at[:, cols], gp_h.at[:, cols], sem_g.at[t])

    hl[...] = (n1_ref[...] * ga[...] + sa[...]).astype(BF)
    acc[...] = jnp.zeros_like(acc)

    def step(t, carry):
        cols = pl.ds(pl.multiple_of(t * tile, tile), tile)
        for r in range(4):
            rows = pl.ds(r * n, n)
            a, d = gelu_both(nn(hl[rows, :], wu[:, cols]) + bu[:, cols])
            ab = a.astype(BF)
            act[rows, cols] = ab
            gp_out[rows, cols] = d.astype(BF)
            acc[rows, :] += nn(ab, wd[cols, :])
        slopes(t).start()
        return carry

    lax.fori_loop(0, steps, step, 0)
    gain = jnp.zeros((1, width), F32)
    shift = jnp.zeros((1, width), F32)
    bias = jnp.zeros((1, width), F32)
    pool = jnp.zeros(pool_out.shape, F32)
    for r, (o, g) in enumerate(((o0, g0), (o1, g1), (o2, g2), (o3, g3))):
        rows = pl.ds(r * n, n)
        hidden = n1_ref[rows, :] * ga[...] + sa[...]
        n2, inv = norm(hidden + (acc[rows, :] + bd[...]))
        result = n2 * gf[...] + sf[...]
        o[...] = result.astype(BF)
        hi, low = two_parts(result)
        oht = oht_ref[:, r * n : (r + 1) * n]
        pool += nn(oht, hi) + nn(oht, low)
        oh = oh_ref[rows, :]
        gout = g[...].astype(F32) + nn(jnp.concatenate([oh, oh], axis=1), gpl[...])
        gain += jnp.sum(gout * n2, axis=0, keepdims=True)
        shift += jnp.sum(gout, axis=0, keepdims=True)
        gr2 = norm_back(gout * gf[...], n2, inv)
        r2_out[rows, :] = gr2
        low_g = gr2.astype(BF)
        bias += jnp.sum(low_g.astype(F32), axis=0, keepdims=True)
        gt[:, r * n : (r + 1) * n] = low_g.T
    pool_out[...] = pool
    vec_out[...] = jnp.concatenate([bias, gain, shift, jnp.zeros((5, width), F32)], axis=0)
    half = ff // 2
    part = 512

    def piece(i, carry):
        for rc, ref in ((1, send), (0, keep)):
            at = (info[8] ^ rc) * half + i * part
            res = nn(gt[...], act[:, pl.ds(pl.multiple_of(at, part), part)])
            put_shards(ref, info, lay, pl.ds(pl.multiple_of(i * part, part), part), res)
        return carry

    lax.fori_loop(0, half // part, piece, 0)
    for t in range(steps):
        slopes(t).wait()


def ffn_back_kernel(
    lay, info, r2_ref, gp_h, wd, n1_ref, ga, sa,
    send, keep, bup_out, gpre_out,
    gl, hlt, gp, sem_w,
):
    width = hlt.shape[0]
    half = width // 2
    ff = gp.shape[1]
    tile = width
    steps = ff // tile

    def load(t):
        cols = pl.ds(pl.multiple_of(t * tile, tile), tile)
        return pltpu.make_async_copy(gp_h.at[:, cols], gp.at[:, cols], sem_w.at[t])

    for t in range(steps):
        load(t).start()
    gl[...] = r2_ref[...].astype(BF)
    hlt[...] = (n1_ref[...] * ga[...] + sa[...]).astype(BF).T
    per = 2 if lay[0] > 1 else 1

    def step(t, carry):
        cols = pl.ds(pl.multiple_of(t * tile, tile), tile)
        load(t).wait()
        gpre = (nt(gl[...], wd[cols, :]) * gp[:, cols].astype(F32)).astype(BF)
        gpre_out[:, cols] = gpre
        bup_out[:, cols] = jnp.broadcast_to(
            jnp.sum(gpre.astype(F32), axis=0, keepdims=True), (bup_out.shape[0], tile)
        )
        for rc, ref in ((1, send), (0, keep)):
            at = pl.multiple_of((info[8] ^ rc) * half, half)
            res = nn(hlt[pl.ds(at, half), :], gpre)
            for i in range(per):
                if lay[0] > 1:
                    put_rows(ref, info[per * t + i], info[9], 0, lay[1], slice(None), res[:, i * half : (i + 1) * half])
                else:
                    put_rows(ref, 0, info[9], 0, lay[1], cols, res)
        return carry

    lax.fori_loop(0, steps, step, 0)


def norm_back_kernel(
    lay, info, r2_ref, gpre, wu, n1_ref, inv_ref, ga, wo, att,
    r1_h, gatt_out, gaug_out, vec_out, osend, okeep,
    gt, r1_out, acc, sems,
):
    tok, width = r2_ref.shape
    half = width // 2
    n = tok // 4
    gain = jnp.zeros((1, width), F32)
    shift = jnp.zeros((1, width), F32)
    bias = jnp.zeros((1, width), F32)
    row = lax.broadcasted_iota(jnp.int32, (width, LANES), 0) // HD
    lane = lax.broadcasted_iota(jnp.int32, (width, LANES), 1)
    pick = ((lane % PART == row) & (lane >= PART) & (lane < 4 * PART)).astype(BF)
    lane1 = lax.broadcasted_iota(jnp.int32, (1, LANES), 1)
    outs = []

    def step(t, carry):
        cols = pl.ds(pl.multiple_of(t * width, width), width)
        acc[...] += nt(gpre[:, cols], wu[:, cols])
        return carry

    acc[...] = r2_ref[...]
    lax.fori_loop(0, gpre.shape[1] // width, step, 0)
    for r in range(4):
        rows = pl.ds(r * n, n)
        gh = acc[rows, :]
        n1 = n1_ref[rows, :]
        gain += jnp.sum(gh * n1, axis=0, keepdims=True)
        shift += jnp.sum(gh, axis=0, keepdims=True)
        gr1 = norm_back(gh * ga[...], n1, inv_ref[rows, :1])
        r1_out[rows, :] = gr1
        outs += copies([(r1_out.at[rows, :], r1_h.at[rows, :])], sems, r)
        gm = gr1.astype(BF)
        bias += jnp.sum(gm.astype(F32), axis=0, keepdims=True)
        gt[:, r * n : (r + 1) * n] = gm.T
        gatt = nt(gm, wo[...]).astype(BF)
        gatt_out[rows, :] = gatt
        a, b, c = three_parts(gatt.astype(F32) * att[rows, :])
        delta = nn(a, pick) + nn(b, pick) + nn(c, pick)
        a, b, c = three_parts(delta)
        gaug_out[rows, :] = jnp.where(lane1 < 2 * PART, a, jnp.where(lane1 < 3 * PART, b, c))
    vec_out[...] = jnp.concatenate([bias, gain, shift, jnp.zeros((5, width), F32)], axis=0)
    sides = [att[:, pl.ds(pl.multiple_of((info[8] ^ rc) * half, half), half)].astype(BF) for rc in (1, 0)]
    res = nn(gt[...], jnp.concatenate(sides, axis=1))
    put_shards(osend, info, lay, slice(None), res[:, :half])
    put_shards(okeep, info, lay, slice(None), res[:, half:])
    wait(outs)


def attend_back_kernel(
    q, k, v, g, qa, ka, ga,
    gq, gk, gv, gqt, gkt, gvt, vec_out,
):
    tok, width = q.shape

    def pair(p, carry):
        sl = pl.ds(pl.multiple_of(p * LANES, LANES), LANES)
        qp, kp, vp, gp = q[:, sl], k[:, sl], v[:, sl], g[:, sl]
        qcat = jnp.concatenate([qp, qa[...]], axis=1)
        gcat = jnp.concatenate([gp, ga[...]], axis=1)
        kt = kp.T
        lane = lax.broadcasted_iota(jnp.int32, (1, LANES), 1)
        gkp = jnp.zeros((tok, LANES), F32)
        gvp = jnp.zeros((tok, LANES), F32)
        parts = []
        zero = jnp.zeros_like(kp)
        for h in range(2):
            mine = (lane < HD) == (h == 0)
            pick = head_lane(2 * p + h)
            kaug = jnp.where(pick, -jnp.ones((), BF), ka[...])
            vaug = jnp.where(pick, -jnp.ones((), BF), jnp.zeros((tok, LANES), BF))
            prob = jnp.exp(nt(jnp.concatenate([jnp.where(mine, kp, zero), kaug], axis=1), qcat))
            dp = nt(jnp.concatenate([jnp.where(mine, vp, zero), vaug], axis=1), gcat)
            ds = (prob * dp).astype(BF)
            gvp += nn(prob.astype(BF), jnp.where(mine, gp, zero))
            gkp += nn(ds, jnp.where(mine, qp, zero))
            parts.append(nn(kt[h * HD : (h + 1) * HD], ds))
        gqp = (jnp.concatenate(parts, axis=0) * (HD**-0.5)).astype(BF)
        gqt[sl, :] = gqp
        gq[:, sl] = gqp.T
        gkb, gvb = gkp.astype(BF), gvp.astype(BF)
        gk[:, sl] = gkb
        gv[:, sl] = gvb
        gkt[sl, :] = gkb.T
        gvt[sl, :] = gvb.T
        return carry

    lax.fori_loop(0, width // LANES, pair, 0)
    bq = jnp.sum(gq[...].astype(F32), axis=0, keepdims=True)
    bv = jnp.sum(gv[...].astype(F32), axis=0, keepdims=True)
    vec_out[...] = jnp.concatenate([bq, bv, jnp.zeros((6, width), F32)], axis=0)


def project_back_kernel(
    lay, info, gq, gk, gv, gqt, gkt, gvt, x_ref, r1, wq, wk, wv, vecs, bups,
    send, keep, o0, o1, o2, o3,
):
    width = x_ref.shape[1]
    n, halves, rs = lay
    half = width // 2
    sides = [x_ref[:, pl.ds(pl.multiple_of((info[8] ^ rc) * half, half), half)] for rc in (1, 0)]
    right = jnp.concatenate(sides, axis=1)
    for m, left in enumerate((gqt, gkt, gvt)):
        both = nn(left[...], right)
        for rc, ref in ((1, send), (0, keep)):
            res = both[:, :half] if rc else both[:, half:]
            if n > 1:
                for j in range(n):
                    lead, at = info[j], j * rs
                    if m == 1:
                        put_rows(ref, lead, info[9], 48, halves, slice(None), res[at : at + 32])
                        put_rows(ref, lead, info[9], 128, halves, slice(None), res[at + 32 : at + rs])
                    else:
                        put_rows(ref, lead, info[9], 40 * m, halves, slice(None), res[at : at + rs])
            else:
                ref[0, 0, pl.ds(m * width, width), :] = res.astype(BF)
    if n > 1:
        for j in range(n):
            bup = bups[:1, j * 4 * rs : (j + 1) * 4 * rs]
            block = jnp.concatenate(
                [vecs[:, j * rs : (j + 1) * rs], jnp.zeros((8, rs), F32)]
                + [bup[:, c * rs : (c + 1) * rs] for c in range(4)]
                + [jnp.zeros((12, rs), F32)],
                axis=0,
            )
            block = jnp.concatenate([block, jnp.zeros((32, half - rs), F32)], axis=1)
            for rc, ref in ((1, send), (0, keep)):
                mine = jnp.where((info[8] ^ rc) == 0, 1.0, 0.0)
                put_rows(ref, info[j], info[9], 64, halves, slice(None), block * mine)

    total = r1[...] + nt(gq[...], wq[...]) + nt(gk[...], wk[...]) + nt(gv[...], wv[...])
    for r, o in enumerate((o0, o1, o2, o3)):
        c = o.shape[0]
        o[...] = total[r * c : (r + 1) * c].astype(BF)


WHOLE = pl.BlockSpec(memory_space=pltpu.VMEM)
SCALARS = pl.BlockSpec(memory_space=pltpu.SMEM)
FAR = pl.BlockSpec(memory_space=pltpu.HBM)


def shape(dims, dtype=BF):
    return jax.ShapeDtypeStruct(tuple(dims), dtype)


def buf(dims, dtype=BF):
    return pltpu.VMEM(tuple(dims), dtype)


def sems(count):
    return pltpu.SemaphoreType.DMA((count,))


def params(mib):
    return pltpu.CompilerParams(vmem_limit_bytes=mib * 1024 * 1024)


COST = pl.CostEstimate(flops=10**9, bytes_accessed=10**6, transcendentals=0)


class Line:
    def __init__(self):
        self.token = None

    def call(self, kernel, outs, args, scalars=(), scratch=(), name=None, mib=8, far_in=(), far_out=()):
        args = [pltpu.with_memory_space_constraint(a, pltpu.HBM) if i in far_in else a for i, a in enumerate(args)]
        ins = [SCALARS if i in scalars else FAR if i in far_in else WHOLE for i in range(len(args))]
        to = [FAR if i in far_out else WHOLE for i in range(len(outs))]
        outs = [pltpu.HBM(o.shape, o.dtype) if i in far_out else o for i, o in enumerate(outs)]
        tokens = [] if self.token is None else [self.token]
        n_in, n_tok, n_out = len(args), len(tokens), len(outs)

        def body(*refs):
            left, right = refs[:n_in], refs[n_in + n_tok :]
            kernel(*left, *right[:n_out], *right[n_out + 1 :])
            right[n_out][...] = jnp.zeros((8, LANES), F32)

        *got, self.token = pl.pallas_call(
            body,
            out_shape=[*outs, shape((8, LANES), F32)],
            in_specs=ins + [WHOLE] * n_tok,
            out_specs=[*to, WHOLE],
            scratch_shapes=list(scratch),
            compiler_params=params(mib),
            cost_estimate=COST,
            name=name,
        )(*args, *tokens)
        return got


def kernel_name(kernel):
    return getattr(kernel, "func", kernel).__name__.split("_")[0]


def plus(a, b):
    return (a.astype(F32) + b.astype(F32)).astype(BF)


def view(ref, cut):
    return ref[:, :, slice(*cut[0]), slice(*cut[1])]


def one_kernel(cuts_a, cuts_b, count, *refs):
    got, kept = refs[:count], refs[count : 2 * count]
    sa, sb, ka, kb = refs[2 * count :]
    at = 0
    for i, cut in cuts_a:
        total = plus(view(got[i], cut), view(kept[i], cut))
        m = total.shape[2]
        sa[:, :, at : at + m, :] = total[:, 4:]
        ka[:, :, at : at + m, :] = total[:, :4]
        at += m
    at = 0
    for i, cut in cuts_b:
        total = plus(view(got[i], cut), view(kept[i], cut))
        m = total.shape[2]
        sb[:, at : at + m, :] = total[1]
        kb[:, at : at + m, :] = total[0]
        at += m


def two_kernel(ga, gb, ka, kb, sa, sb, la, lb):
    a = plus(ga[...], ka[...])
    sa[...] = a[1]
    la[...] = a[0]
    b = plus(gb[...], kb[...])
    sb[...] = b[4:]
    lb[...] = b[:4]


def three_kernel(ga, gb, ka, kb, send, keep):
    m = ga.shape[1]
    a, b = plus(ga[...], ka[...]), plus(gb[...], kb[...])
    send[:, :m, :] = a[2:]
    keep[:, :m, :] = a[:2]
    send[:, m:, :] = b[2:]
    keep[:, m:, :] = b[:2]


def four_kernel(got, kept, send, keep):
    total = plus(got[...], kept[...])
    send[...] = total[1]
    keep[...] = total[0]


def five_kernel(got, kept, mine):
    mine[...] = plus(got[...], kept[...])


def six_kernel(info, mine, other, both):
    both[info[9]] = mine[...]
    both[1 - info[9]] = other[...]


def down_kernel(info, mine, other, out):
    m = mine.shape[1] // 2
    cols = mine.shape[2]
    for rc, ref in ((0, mine), (1, other)):
        for p in range(2):
            block = jnp.concatenate([ref[0, p * m : (p + 1) * m], ref[1, p * m : (p + 1) * m]], axis=0)
            at = (info[8] ^ rc) * 2 * cols + p * cols
            out[:, pl.ds(pl.multiple_of(at, cols), cols)] = block.astype(F32)


def up_kernel(info, mine, other, out):
    half = out.shape[0] // 2
    m = half // 2
    for rc, ref in ((0, mine), (1, other)):
        for a in range(2):
            at = (info[8] ^ rc) * half + a * m
            out[pl.ds(pl.multiple_of(at, m), m), :] = ref[a].astype(F32)


def qkv_kernel(info, mine, other, gq, gk, gv, go, vec):
    half = gq.shape[1] // 2
    for rc, ref in ((0, mine), (1, other)):
        at = pl.ds(pl.multiple_of((info[8] ^ rc) * half, half), half)

        def put(out, *spans):
            parts = [ref[a, i : i + m] for i, m in spans for a in range(2)]
            out[:, at] = jnp.concatenate(parts, axis=0).astype(F32)

        put(gq, (0, 48))
        put(gk, (48, 16), (176, 32))
        put(gv, (128, 48))
        put(go, (80, 48))
    rs = vec.shape[1]
    low = jnp.where(info[8] == 0, mine[:, 64:80, :].astype(F32), other[:, 64:80, :].astype(F32))
    vec[...] = jnp.concatenate([low[0, :8, :rs], low[1, :8, :rs]], axis=0)


def local(n_dp, n_seq, *args):
    (
        tokens, seg_lengths, w_query, b_query, w_key, w_value, b_value, w_out, b_out,
        gain_attn, shift_attn, w_up, b_up, w_down, b_down, gain_ffn, shift_ffn,
        grad_output, grad_pooled,
    ) = args
    line = Line()
    me = lax.axis_index("seq")
    dp = lax.axis_index("dp")
    core, y = me % 2, me // 2
    rows, piece, width = tokens.shape
    tok = n_seq * piece
    ff = w_up.shape[1]
    fast = n_dp == 8
    n = n_dp if fast else 1
    rs = width // n
    half = width // 2
    xor = [[(i, i ^ r) for i in range(n_seq)] for r in range(n_seq)]

    if fast:
        j = jnp.arange(8, dtype=jnp.int32) ^ dp
        pos = (j % 2) * 4 + (j // 2 % 2) * 2 + j // 4
    else:
        pos = jnp.zeros((8,), jnp.int32)
    info = jnp.concatenate([pos, jnp.stack([core, y, me]), jnp.zeros((5,), jnp.int32)]).astype(jnp.int32)

    def rel(a, name):
        parts = line.call(
            split_kernel, [shape((piece, width))] * n_seq, (info, a), scalars=(0,), scratch=[sems(n_seq)],
            name=name, far_in=(1,),
        )
        return [parts[0]] + [lax.ppermute(parts[r], "seq", xor[r]) for r in range(1, n_seq)]

    xs = rel(tokens, "split_tokens")
    gs = rel(grad_output, "split_grads")

    lengths = lax.dynamic_index_in_dim(seg_lengths, me, 0, keepdims=False)
    ends = jnp.cumsum(lengths)
    order = me ^ jnp.arange(n_seq, dtype=jnp.int32)
    places = (order[:, None] * piece + jnp.arange(piece, dtype=jnp.int32)[None, :]).reshape(tok)
    seg = jnp.sum((places[:, None] >= ends[None, :]).astype(jnp.int32), axis=1)
    lane = jnp.arange(LANES, dtype=jnp.int32)
    hot = seg[:, None] == lane[None, :]
    onehot = hot.astype(BF)
    kaug = jnp.where((lane < SEGS)[None, :] & ~hot, NEG, 0.0).astype(BF)
    onehot_t = (seg[None, :] == jnp.arange(16, dtype=jnp.int32)[:, None]).astype(BF)
    length_col = lengths.astype(F32)[:, None]
    gpool = lax.dynamic_index_in_dim(grad_pooled, me, 0, keepdims=False).astype(F32) / length_col
    gp_hi = gpool.astype(BF)
    gp_low = (gpool - gp_hi.astype(F32)).astype(BF)
    zeros = jnp.zeros((LANES - SEGS, width), BF)
    gpl = jnp.concatenate([gp_hi, zeros, gp_low, zeros], axis=0)

    def vec(v):
        return v.astype(F32).reshape(1, -1)

    sq = shape((tok, width))
    sqf = shape((tok, width), F32)
    lanes = shape((tok, LANES))
    lanes_f = shape((tok, LANES), F32)
    x, q, k, v, att, inv, qaug, n1 = line.call(
        attend_kernel,
        [sq, sq, sq, sq, sqf, lanes_f, lanes, sqf],
        (*xs, w_query, w_key, w_value, w_out, onehot, kaug, vec(b_query), vec(b_value), vec(b_out)),
        scratch=[buf((tok, width))] * 4
        + [buf((tok, width), F32), buf((tok, LANES), F32), buf((tok, LANES))]
        + [buf((width, width))] * 4
        + [buf((PART, tok), F32), sems(15)],
        name="attend",
        mib=20,
        far_in=range(4, 8),
        far_out=range(7),
    )

    halves = 2 if fast else 1
    lay = (n, halves, rs)
    wire_d = shape((halves, n, rs // halves, ff // 2))
    steps = ff // width
    *outs, gp, d_send, d_keep, pool, r2, vec_b = line.call(
        functools.partial(ffn_kernel, lay),
        [shape((piece, width))] * 4
        + [shape((tok, ff)), wire_d, wire_d, shape((16, width), F32), sqf, shape((8, width), F32)],
        (
            info, n1, vec(gain_attn), vec(shift_attn), w_up, vec(b_up), w_down, vec(b_down),
            vec(gain_ffn), vec(shift_ffn), *gs, onehot, onehot_t, gpl,
        ),
        scalars=(0,),
        scratch=[
            buf((tok, width)), buf((tok, width), F32), buf((tok, ff)), buf((width, tok)), buf((tok, ff)), sems(steps),
        ],
        name="ffn",
        mib=18,
        far_out=(4,),
    )

    pp_core = lambda a: lax.ppermute(a, "seq", xor[1])
    pp_y = lambda a: lax.ppermute(a, "seq", xor[2])

    def pp_dp(bit):
        return lambda a: lax.ppermute(a, "dp", [(i, i ^ bit) for i in range(n_dp)])

    pp_x, pp_z1, pp_z2 = pp_dp(1), pp_dp(2), pp_dp(4)

    def join_rows(parts):
        return parts[0] if len(parts) == 1 else jnp.concatenate(parts, axis=-2)

    class Sum:
        def __init__(self, name, got, kept, cuts_a, cuts_b):
            self.name, self.got, self.kept = name, got, kept
            self.cuts = cuts_a, cuts_b

        def run(self, kernel, outs, args, scalars=()):
            return line.call(
                kernel, [shape(o) for o in outs], args, scalars=scalars, name=self.name + kernel_name(kernel), mib=16
            )

        def one(self):
            a, b = (sum(r1 - r0 for _, ((r0, r1), _) in cut) for cut in self.cuts)
            c = self.cuts[0][0][1][1]
            c = c[1] - c[0]
            sa, sb, ka, kb = self.run(
                functools.partial(one_kernel, *self.cuts, len(self.got)),
                [(2, 4, a, c), (8, b, c), (2, 4, a, c), (8, b, c)],
                (*self.got, *self.kept),
            )
            self.got, self.kept = (pp_x(sa), pp_y(sb)), (ka, kb)
            self.dims = a, b, c

        def two(self):
            a, b, c = self.dims
            sa, sb, ka, kb = self.run(two_kernel, [(4, a, c), (4, b, c)] * 2, (*self.got, *self.kept))
            self.got, self.kept = (pp_y(sa), pp_x(sb)), (ka, kb)

        def three(self):
            a, b, c = self.dims
            send, keep = self.run(three_kernel, [(2, a + b, c)] * 2, (*self.got, *self.kept))
            self.got, self.kept = pp_z1(send), keep

        def four(self):
            a, b, c = self.dims
            send, keep = self.run(four_kernel, [(a + b, c)] * 2, (self.got, self.kept))
            self.got, self.kept = pp_z2(send), keep

        def five(self):
            a, b, c = self.dims
            (mine,) = self.run(five_kernel, [(a + b, c)], (self.got, self.kept))
            self.got, self.kept = pp_y(mine), mine

        def six(self):
            a, b, c = self.dims
            (both,) = self.run(six_kernel, [(2, a + b, c)], (info, self.kept, self.got), scalars=(0,))
            self.got, self.kept = pp_core(both), both

        def end(self, kernel, outs):
            return line.call(
                kernel, outs, (info, self.kept, self.got), scalars=(0,), name=self.name + "end", mib=16
            )

    def there(parts):
        return [parts[0]] + [lax.ppermute(parts[r], "seq", xor[r]) for r in range(1, 4)]

    def joined(got, name):
        (whole,) = line.call(
            join_kernel, [shape((rows, *got[0].shape), got[0].dtype)], (info, *got), scalars=(0,), name=name
        )
        return whole

    out_got = there(outs)
    pool_got = there([pool[:SEGS] / length_col] * n_seq)

    wire_u = shape((halves, n, half // halves, ff // n))
    if fast:
        d_got = pp_core(d_send)
    u_send, u_keep, bup, gpre = line.call(
        functools.partial(ffn_back_kernel, lay),
        [wire_u, wire_u, shape((8, ff), F32), shape((tok, ff))],
        (info, r2, gp, w_down, n1, vec(gain_attn), vec(shift_attn)),
        scalars=(0,),
        scratch=[buf((tok, width)), buf((width, tok)), buf((tok, ff)), sems(steps)],
        name="ffn_back",
        mib=12,
        far_in=(2,),
    )
    if fast:
        u_got = pp_core(u_send)
        c, m = ff // 4, rs // 2
        down = Sum("down_", [d_got], [d_keep], [(0, ((0, m), (0, c)))], [(0, ((0, m), (c, 2 * c)))])
        down.one()
    wire_o = shape((halves, n, rs // halves, half))
    r1, gatt, gaug, vec_c, o_send, o_keep = line.call(
        functools.partial(norm_back_kernel, lay),
        [sqf, sq, shape((tok, LANES)), shape((8, width), F32), wire_o, wire_o],
        (info, r2, gpre, w_up, n1, inv, vec(gain_attn), w_out, att),
        scalars=(0,),
        scratch=[buf((width, tok)), buf((tok, width), F32), buf((tok, width), F32), sems(4)],
        name="norm_back",
        mib=14,
        far_out=(0,),
    )
    output = joined(out_got, "join_out")
    pooled = joined(pool_got, "join_pool")
    if fast:
        o_got = pp_core(o_send)
        m = half // 2
        up = Sum("up_", [u_got], [u_keep], [(0, ((0, m // 2), (0, half)))], [(0, ((m // 2, m), (0, half)))])
        up.one()

    gq, gk, gv, gqt, gkt, gvt, vec_d = line.call(
        attend_back_kernel,
        [sq] * 3 + [shape((width, tok))] * 3 + [shape((8, width), F32)],
        (q, k, v, gatt, qaug, kaug, gaug),
        name="attend_back",
        mib=10,
    )
    vecs = jnp.concatenate([vec_d[:2], vec_c[:3], vec_b[:3]], axis=0)
    if fast:
        down.two()
        up.two()
    rows_q = 160 if fast else 3 * width
    wire_q = shape((halves, n, rows_q, half))
    q_send, q_keep, *ins = line.call(
        functools.partial(project_back_kernel, lay),
        [wire_q, wire_q] + [shape((piece, width))] * 4,
        (info, gq, gk, gv, gqt, gkt, gvt, x, r1, w_query, w_key, w_value, vecs, bup),
        scalars=(0,),
        name="project_back",
        mib=16,
    )
    in_got = there(ins)
    if fast:
        q_got = pp_core(q_send)
        qkv = Sum(
            "qkv_", [q_got, o_got], [q_keep, o_keep],
            [(0, ((0, 80), (0, half))), (1, ((0, 48), (0, half)))],
            [(0, ((80, 160), (0, half)))],
        )
        f32 = lambda *d: shape(d, F32)
        down.three()
        qkv.one()
        up.three()
        down.four()
        qkv.two()
        up.four()
        down.five()
        qkv.three()
        down.six()
        up.five()
        grad_tokens = joined(in_got, "join_in")
        qkv.four()
        up.six()
        (g_down,) = down.end(down_kernel, [f32(rs, ff)])
        qkv.five()
        (g_up,) = up.end(up_kernel, [f32(width, ff // n)])
        qkv.six()
        *g_qkv, g_out, vs = qkv.end(qkv_kernel, [f32(rs, width)] * 4 + [f32(16, rs)])
        g_down, g_out, g_qkv = g_down.T, g_out.T, [g.T for g in g_qkv]
        small = [vs[i] for i in range(8)] + [vs[8:12].reshape(-1)]
    else:
        grad_tokens = joined(in_got, "join_in")

        def total(send, keep, dim):
            h = keep.astype(F32) + pp_core(send).astype(F32)
            h = h + pp_y(h.astype(BF)).astype(F32)
            return lax.psum_scatter(h, "dp", scatter_dimension=dim, tiled=True).astype(BF)

        def whole(send, keep, dim, along):
            mine = total(send, keep, dim)
            other = pp_core(mine)
            lo, hi = jnp.where(core == 0, mine, other), jnp.where(core == 0, other, mine)
            return jnp.concatenate([lo, hi], axis=along).astype(F32)

        g_down = whole(d_send[0, 0], d_keep[0, 0], 0, 1).T
        g_up = whole(u_send[0, 0], u_keep[0, 0], 1, 0)
        g_out = whole(o_send[0, 0], o_keep[0, 0], 0, 1).T
        g_qkv = [
            whole(q_send[0, 0, w * width : (w + 1) * width], q_keep[0, 0, w * width : (w + 1) * width], 0, 1).T
            for w in range(3)
        ]
        flat = lax.psum(jnp.concatenate([vecs.reshape(-1), bup[0]]), ("dp", "seq"))
        mine = width // n_dp
        small = [
            lax.dynamic_slice_in_dim(flat, i * width + dp * mine, mine) for i in range(8)
        ] + [lax.dynamic_slice_in_dim(flat, 8 * width + dp * 4 * mine, 4 * mine)]

    bq, bv, b_o, gain1, shift1, b_d, gain2, shift2, b_u = small
    return (
        output, pooled, grad_tokens, g_qkv[0], bq, g_qkv[1], g_qkv[2], bv, g_out, b_o, gain1, shift1,
        g_up, b_u, g_down, b_d, gain2, shift2,
    )


def solution(mesh):
    rows = P("dp", "seq", None)
    placed = (rows, P("dp", None)) + (P(),) * 15 + (rows, P("dp", None, None))
    col, one = P(None, "dp"), P("dp")
    return jax.shard_map(
        functools.partial(local, mesh.shape["dp"], mesh.shape["seq"]),
        mesh=mesh,
        in_specs=placed,
        out_specs=(
            rows, P("dp", None, None), rows, col, one, col, col, one, col, one, one, one,
            col, one, col, one, one, one,
        ),
        check_vma=False,
    )
```

```python
import functools

import jax
import jax.numpy as jnp
from jax import lax
from jax.experimental import pallas as pl
from jax.experimental.pallas import tpu as pltpu
from jax.sharding import PartitionSpec as P

HD = 64
SEGS = 8
BF = jnp.bfloat16
F32 = jnp.float32
EPS = 1e-06
NEG = -1e30
LANES = 128

PART = 16


def nn(a, b):
    return jnp.dot(a, b, preferred_element_type=F32)


def nt(a, b):
    return lax.dot_general(a, b, (((1,), (1,)), ((), ())), preferred_element_type=F32)


def three_parts(v):
    hi = v.astype(BF)
    rest = v - hi.astype(F32)
    mid = rest.astype(BF)
    low = (rest - mid.astype(F32)).astype(BF)
    return hi, mid, low


def two_parts(v):
    hi = v.astype(BF)
    return hi, (v - hi.astype(F32)).astype(BF)


def norm(value):
    centre = value - jnp.mean(value, axis=-1, keepdims=True)
    inverse = lax.rsqrt(jnp.mean(centre * centre, axis=-1, keepdims=True) + EPS)
    return centre * inverse, inverse


def norm_back(grad, normed, inverse):
    a = jnp.mean(grad, axis=-1, keepdims=True)
    b = jnp.mean(grad * normed, axis=-1, keepdims=True)
    return (grad - a - normed * b) * inverse


def gelu_both(x):
    phi = 0.5 + 0.5 * lax.erf(x * (0.5**0.5))
    density = 0.3989422804014327 * jnp.exp(x * x * -0.5)
    return x * phi, phi + x * density


def row(ref):
    return ref[...].astype(F32).reshape(1, ref.shape[0])


def head_lane(h):
    lane = lax.broadcasted_iota(jnp.int32, (1, LANES), 1)
    return (lane % PART == h) & (lane >= PART) & (lane < 4 * PART)


def put_rows(out_ref, lead, y, rows, halves, cols, value):
    n = value.shape[0] // halves
    for a in range(halves):
        side = jnp.where(y == a, 0, 1) if halves > 1 else 0
        out_ref[side, lead, pl.ds(rows, n), cols] = value[a * n : (a + 1) * n].astype(BF)


def put_shards(out_ref, info, lay, cols, value, rows=0, first=0):
    n, halves, rs = lay
    count = value.shape[0] // rs
    for i in range(count):
        lead = info[first * count + i] if n > 1 else 0
        put_rows(out_ref, lead, info[9], rows, halves, cols, value[i * rs : (i + 1) * rs])


def copies(pairs, sems, first=0):
    out = []
    for i, (src, dst) in enumerate(pairs):
        out.append(pltpu.make_async_copy(src, dst, sems.at[first + i]))
        out[-1].start()
    return out


def wait(moves):
    for m in moves:
        m.wait()


def split_kernel(info, x_ref, *refs):
    outs, sems = refs[:-1], refs[-1]
    wait(copies([(x_ref.at[info[10] ^ r], outs[r]) for r in range(len(outs))], sems))


def pack_kernel(o0, o1, o2, o3, i0, i1, i2, i3, pool, p0, p1, p2, p3):
    n = o0.shape[0]
    hi, low = two_parts(pool[:SEGS, :])
    for p, o, i in ((p0, o0, i0), (p1, o1, i1), (p2, o2, i2), (p3, o3, i3)):
        p[:n, :] = o[...]
        p[n : 2 * n, :] = i[...]
        p[2 * n : 2 * n + SEGS, :] = hi
        p[2 * n + SEGS :, :] = low


def unpack_kernel(info, lengths, p0, p1, p2, p3, out, grad, pool):
    me = info[10]
    n = out.shape[1]
    for r, p in enumerate((p0, p1, p2, p3)):
        out[me ^ r] = p[:n, :]
        grad[me ^ r] = p[n : 2 * n, :]
        sums = p[2 * n :, :].astype(F32)
        pool[me ^ r] = (sums[:SEGS] + sums[SEGS:]) / lengths[me ^ r][:, :1]


def attend_kernel(
    x0, x1, x2, x3, wq_h, wk_h, wv_h, wo_h, oh_ref, ka_ref, bq_ref, bv_ref, bo_ref,
    x_h, q_h, k_h, v_h, att_h, inv_h, qa_h, n1_out,
    x_out, q_out, k_out, v_out, att_out, inv_out, qa_out, wq, wk, wv, wo, stat, sems,
):
    n = x0.shape[0]
    bq, bv, bo = row(bq_ref), row(bv_ref), row(bo_ref)
    ws = copies([(wq_h, wq), (wk_h, wk), (wv_h, wv), (wo_h, wo)], sems, 4)
    for r, ref in enumerate((x0, x1, x2, x3)):
        x_out[r * n : (r + 1) * n] = ref[...]
    outs = copies([(x_out, x_h)], sems, 8)
    x = x_out[...]
    ws[0].wait()
    q_out[...] = ((nn(x, wq[...]) + bq).astype(BF).astype(F32) * (HD**-0.5)).astype(BF)
    outs += copies([(q_out, q_h)], sems, 9)
    ws[1].wait()
    k_out[...] = nn(x, wk[...]).astype(BF)
    outs += copies([(k_out, k_h)], sems, 10)
    ws[2].wait()
    v_out[...] = (nn(x, wv[...]) + bv).astype(BF)
    outs += copies([(v_out, v_h)], sems, 11)
    tok, width = x.shape
    stat[...] = jnp.zeros_like(stat)
    ones = jnp.ones((16, tok), BF)

    def pair(p, carry):
        sl = pl.ds(pl.multiple_of(p * LANES, LANES), LANES)
        qcat = jnp.concatenate([q_out[:, sl], oh_ref[...]], axis=1)
        kp = k_out[:, sl]
        vt = v_out[:, sl].T
        lane = lax.broadcasted_iota(jnp.int32, (1, LANES), 1)
        parts = []
        for h in range(2):
            kh = jnp.where((lane < HD) == (h == 0), kp, jnp.zeros_like(kp))
            st = nt(jnp.concatenate([kh, ka_ref[...]], axis=1), qcat)
            m = jnp.max(st, axis=0, keepdims=True)
            pb = jnp.exp(st - m).astype(BF)
            ot = nn(jnp.concatenate([vt[h * HD : (h + 1) * HD], ones], axis=0), pb)
            total = ot[HD : HD + 1]
            stat[pl.ds(2 * p + h, 1), :] = m + jnp.log(total)
            parts.append(ot[:HD] / total)
        att_out[:, sl] = jnp.concatenate(parts, axis=0).T
        return carry

    lax.fori_loop(0, width // LANES, pair, 0)
    outs += copies([(att_out, att_h)], sems, 12)
    hi, mid, low = three_parts(stat[...])
    zero = jnp.zeros((PART, tok), BF)
    qa_out[...] = jnp.concatenate([zero, hi, mid, low, zero, zero, zero, zero], axis=0).T + oh_ref[...]
    outs += copies([(qa_out, qa_h)], sems, 13)
    ws[3].wait()
    mixed = nn(att_out[...].astype(BF), wo[...]) + bo
    n1, inv = norm(x.astype(F32) + mixed)
    n1_out[...] = n1
    inv_out[...] = jnp.broadcast_to(inv, inv_out.shape)
    outs += copies([(inv_out, inv_h)], sems, 14)
    wait(outs)


def ffn_kernel(
    lay, info, n1_ref, ga_ref, sa_ref, bd_ref, gf_ref, sf_ref, wu, bu_ref, wd_h, g0, g1, g2, g3, oh_ref, oht_ref, gpl,
    o0, o1, o2, o3, gp_h, send, keep, pool_out, r2_out, vec_out,
    hl, acc, act, gt, gp_out, wd, bu, sem_g, sem_w,
):
    n = g0.shape[0]
    ga, sa, bd, gf, sf = row(ga_ref), row(sa_ref), row(bd_ref), row(gf_ref), row(sf_ref)
    bu[...] = row(bu_ref)
    tok, width = acc.shape
    ff = act.shape[1]
    tile = width
    steps = ff // tile

    def slopes(t):
        cols = pl.ds(pl.multiple_of(t * tile, tile), tile)
        return pltpu.make_async_copy(gp_out.at[:, cols], gp_h.at[:, cols], sem_g.at[t])

    def weights(t):
        rows = pl.ds(pl.multiple_of(t * tile, tile), tile)
        return pltpu.make_async_copy(wd_h.at[rows, :], wd.at[rows, :], sem_w.at[t])

    for t in range(steps):
        weights(t).start()
    hl[...] = (n1_ref[...] * ga + sa).astype(BF)
    acc[...] = jnp.zeros_like(acc)

    def step(t, carry):
        cols = pl.ds(pl.multiple_of(t * tile, tile), tile)
        weights(t).wait()
        for r in range(4):
            rows = pl.ds(r * n, n)
            a, d = gelu_both(nn(hl[rows, :], wu[:, cols]) + bu[:, cols])
            ab = a.astype(BF)
            act[rows, cols] = ab
            gp_out[rows, cols] = d.astype(BF)
            acc[rows, :] += nn(ab, wd[cols, :])
        slopes(t).start()
        return carry

    lax.fori_loop(0, steps, step, 0)
    gain = jnp.zeros((1, width), F32)
    shift = jnp.zeros((1, width), F32)
    bias = jnp.zeros((1, width), F32)
    pool = jnp.zeros(pool_out.shape, F32)
    for r, (o, g) in enumerate(((o0, g0), (o1, g1), (o2, g2), (o3, g3))):
        rows = pl.ds(r * n, n)
        hidden = n1_ref[rows, :] * ga + sa
        n2, inv = norm(hidden + (acc[rows, :] + bd))
        result = n2 * gf + sf
        o[...] = result.astype(BF)
        hi, low = two_parts(result)
        oht = oht_ref[:, r * n : (r + 1) * n]
        pool += nn(oht, hi) + nn(oht, low)
        oh = oh_ref[rows, :]
        gout = g[...].astype(F32) + nn(jnp.concatenate([oh, oh], axis=1), gpl[...])
        gain += jnp.sum(gout * n2, axis=0, keepdims=True)
        shift += jnp.sum(gout, axis=0, keepdims=True)
        gr2 = norm_back(gout * gf, n2, inv)
        r2_out[rows, :] = gr2
        low_g = gr2.astype(BF)
        bias += jnp.sum(low_g.astype(F32), axis=0, keepdims=True)
        gt[:, r * n : (r + 1) * n] = low_g.T
    pool_out[...] = pool
    vec_out[...] = jnp.concatenate([bias, gain, shift, jnp.zeros((5, width), F32)], axis=0)
    half = ff // 2
    part = 512

    def piece(i, carry):
        for rc, ref in ((1, send), (0, keep)):
            at = (info[8] ^ rc) * half + i * part
            res = nn(gt[...], act[:, pl.ds(pl.multiple_of(at, part), part)])
            put_shards(ref, info, lay, pl.ds(pl.multiple_of(i * part, part), part), res)
        return carry

    lax.fori_loop(0, half // part, piece, 0)
    for t in range(steps):
        slopes(t).wait()


def ffn_back_kernel(
    lay, info, r2_ref, gp_h, wd, n1_ref, ga_ref, sa_ref,
    send, keep, bup_out, gpre_out,
    gl, hlt, gp, sem_w,
):
    ga, sa = row(ga_ref), row(sa_ref)
    width = hlt.shape[0]
    half = width // 2
    ff = gp.shape[1]
    tile = width
    steps = ff // tile

    def load(t):
        cols = pl.ds(pl.multiple_of(t * tile, tile), tile)
        return pltpu.make_async_copy(gp_h.at[:, cols], gp.at[:, cols], sem_w.at[t])

    for t in range(steps):
        load(t).start()
    gl[...] = r2_ref[...].astype(BF)
    hlt[...] = (n1_ref[...] * ga + sa).astype(BF).T
    per = 2 if lay[0] > 1 else 1

    def step(t, carry):
        cols = pl.ds(pl.multiple_of(t * tile, tile), tile)
        load(t).wait()
        gpre = (nt(gl[...], wd[cols, :]) * gp[:, cols].astype(F32)).astype(BF)
        gpre_out[:, cols] = gpre
        bup_out[:, cols] = jnp.broadcast_to(
            jnp.sum(gpre.astype(F32), axis=0, keepdims=True), (bup_out.shape[0], tile)
        )
        for rc, ref in ((1, send), (0, keep)):
            at = pl.multiple_of((info[8] ^ rc) * half, half)
            res = nn(hlt[pl.ds(at, half), :], gpre)
            for i in range(per):
                if lay[0] > 1:
                    put_rows(ref, info[per * t + i], info[9], 0, lay[1], slice(None), res[:, i * half : (i + 1) * half])
                else:
                    put_rows(ref, 0, info[9], 0, lay[1], cols, res)
        return carry

    lax.fori_loop(0, steps, step, 0)


def norm_back_kernel(
    lay, info, r2_ref, gpre, wu, n1_ref, inv_ref, ga_ref, wo, att,
    r1_h, gatt_out, gaug_out, vec_out, osend, okeep,
    gt, r1_out, acc, sems,
):
    ga = row(ga_ref)
    tok, width = r2_ref.shape
    half = width // 2
    n = tok // 4
    gain = jnp.zeros((1, width), F32)
    shift = jnp.zeros((1, width), F32)
    bias = jnp.zeros((1, width), F32)
    head = lax.broadcasted_iota(jnp.int32, (width, LANES), 0) // HD
    lane = lax.broadcasted_iota(jnp.int32, (width, LANES), 1)
    pick = ((lane % PART == head) & (lane >= PART) & (lane < 4 * PART)).astype(BF)
    lane1 = lax.broadcasted_iota(jnp.int32, (1, LANES), 1)
    outs = []

    def step(t, carry):
        cols = pl.ds(pl.multiple_of(t * width, width), width)
        acc[...] += nt(gpre[:, cols], wu[:, cols])
        return carry

    acc[...] = r2_ref[...]
    lax.fori_loop(0, gpre.shape[1] // width, step, 0)
    for r in range(4):
        rows = pl.ds(r * n, n)
        gh = acc[rows, :]
        n1 = n1_ref[rows, :]
        gain += jnp.sum(gh * n1, axis=0, keepdims=True)
        shift += jnp.sum(gh, axis=0, keepdims=True)
        gr1 = norm_back(gh * ga, n1, inv_ref[rows, :1])
        r1_out[rows, :] = gr1
        outs += copies([(r1_out.at[rows, :], r1_h.at[rows, :])], sems, r)
        gm = gr1.astype(BF)
        bias += jnp.sum(gm.astype(F32), axis=0, keepdims=True)
        gt[:, r * n : (r + 1) * n] = gm.T
        gatt = nt(gm, wo[...]).astype(BF)
        gatt_out[rows, :] = gatt
        a, b, c = three_parts(gatt.astype(F32) * att[rows, :])
        delta = nn(a, pick) + nn(b, pick) + nn(c, pick)
        a, b, c = three_parts(delta)
        gaug_out[rows, :] = jnp.where(lane1 < 2 * PART, a, jnp.where(lane1 < 3 * PART, b, c))
    vec_out[...] = jnp.concatenate([bias, gain, shift, jnp.zeros((5, width), F32)], axis=0)
    sides = [att[:, pl.ds(pl.multiple_of((info[8] ^ rc) * half, half), half)].astype(BF) for rc in (1, 0)]
    res = nn(gt[...], jnp.concatenate(sides, axis=1))
    put_shards(osend, info, lay, slice(None), res[:, :half])
    put_shards(okeep, info, lay, slice(None), res[:, half:])
    wait(outs)


def attend_back_kernel(
    q, k, v, g, qa, ka, ga,
    gq, gk, gv, gqt, gkt, gvt, vec_out,
):
    tok, width = q.shape

    def pair(p, carry):
        sl = pl.ds(pl.multiple_of(p * LANES, LANES), LANES)
        qp, kp, vp, gp = q[:, sl], k[:, sl], v[:, sl], g[:, sl]
        qcat = jnp.concatenate([qp, qa[...]], axis=1)
        gcat = jnp.concatenate([gp, ga[...]], axis=1)
        kt = kp.T
        lane = lax.broadcasted_iota(jnp.int32, (1, LANES), 1)
        gkp = jnp.zeros((tok, LANES), F32)
        gvp = jnp.zeros((tok, LANES), F32)
        parts = []
        zero = jnp.zeros_like(kp)
        for h in range(2):
            mine = (lane < HD) == (h == 0)
            pick = head_lane(2 * p + h)
            kaug = jnp.where(pick, -jnp.ones((), BF), ka[...])
            vaug = jnp.where(pick, -jnp.ones((), BF), jnp.zeros((tok, LANES), BF))
            prob = jnp.exp(nt(jnp.concatenate([jnp.where(mine, kp, zero), kaug], axis=1), qcat))
            dp = nt(jnp.concatenate([jnp.where(mine, vp, zero), vaug], axis=1), gcat)
            ds = (prob * dp).astype(BF)
            gvp += nn(prob.astype(BF), jnp.where(mine, gp, zero))
            gkp += nn(ds, jnp.where(mine, qp, zero))
            parts.append(nn(kt[h * HD : (h + 1) * HD], ds))
        gqp = (jnp.concatenate(parts, axis=0) * (HD**-0.5)).astype(BF)
        gqt[sl, :] = gqp
        gq[:, sl] = gqp.T
        gkb, gvb = gkp.astype(BF), gvp.astype(BF)
        gk[:, sl] = gkb
        gv[:, sl] = gvb
        gkt[sl, :] = gkb.T
        gvt[sl, :] = gvb.T
        return carry

    lax.fori_loop(0, width // LANES, pair, 0)
    bq = jnp.sum(gq[...].astype(F32), axis=0, keepdims=True)
    bv = jnp.sum(gv[...].astype(F32), axis=0, keepdims=True)
    vec_out[...] = jnp.concatenate([bq, bv, jnp.zeros((6, width), F32)], axis=0)


def project_back_kernel(
    lay, info, gq, gk, gv, gqt, gkt, gvt, x_ref, r1, wq, wk, wv, vecs, bups,
    send_a, send_b, keep_a, keep_b, o0, o1, o2, o3,
):
    width = x_ref.shape[1]
    n, halves, rs = lay
    half = width // 2
    sides = [x_ref[:, pl.ds(pl.multiple_of((info[8] ^ rc) * half, half), half)] for rc in (1, 0)]
    right = jnp.concatenate(sides, axis=1)
    wires = ((1, (send_a, send_b)), (0, (keep_a, keep_b)))
    for m, left in enumerate((gqt, gkt, gvt)):
        both = nn(left[...], right)
        for rc, (wa, wb) in wires:
            res = both[:, :half] if rc else both[:, half:]
            if n > 1:
                for j in range(n):
                    rows = res[j * rs : (j + 1) * rs]
                    put = functools.partial(put_rows, lead=info[j], y=info[9], halves=halves, cols=slice(None))
                    if m == 0:
                        put(wa, rows=0, value=rows)
                    elif m == 1:
                        put(wa, rows=48, value=rows[:32])
                        put(wb, rows=48, value=rows[32:])
                    else:
                        put(wb, rows=0, value=rows)
            elif m < 2:
                wa[0, 0, pl.ds(m * width, width), :] = res.astype(BF)
            else:
                wb[0, 0] = res.astype(BF)
    if n > 1:
        for j in range(n):
            bup = bups[:1, j * 4 * rs : (j + 1) * 4 * rs]
            block = jnp.concatenate(
                [vecs[:, j * rs : (j + 1) * rs], jnp.zeros((8, rs), F32)]
                + [bup[:, c * rs : (c + 1) * rs] for c in range(4)]
                + [jnp.zeros((12, rs), F32)],
                axis=0,
            )
            block = jnp.concatenate([block, jnp.zeros((32, half - rs), F32)], axis=1)
            for rc, (wa, _) in wires:
                mine = jnp.where((info[8] ^ rc) == 0, 1.0, 0.0)
                put_rows(wa, info[j], info[9], 64, halves, slice(None), block * mine)

    total = r1[...] + nt(gq[...], wq[...]) + nt(gk[...], wk[...]) + nt(gv[...], wv[...])
    for r, o in enumerate((o0, o1, o2, o3)):
        c = o.shape[0]
        o[...] = total[r * c : (r + 1) * c].astype(BF)


WHOLE = pl.BlockSpec(memory_space=pltpu.VMEM)
SCALARS = pl.BlockSpec(memory_space=pltpu.SMEM)
FAR = pl.BlockSpec(memory_space=pltpu.HBM)


def shape(dims, dtype=BF):
    return jax.ShapeDtypeStruct(tuple(dims), dtype)


def buf(dims, dtype=BF):
    return pltpu.VMEM(tuple(dims), dtype)


def sems(count):
    return pltpu.SemaphoreType.DMA((count,))


def params(mib):
    return pltpu.CompilerParams(vmem_limit_bytes=mib * 1024 * 1024)


def cost(us):
    return pl.CostEstimate(flops=int(us * 10**9) + 1, bytes_accessed=1, transcendentals=0)


COSTS = {
    "down_one": 0.1, "up_one": 0.1, "down_two": 0.1, "up_two": 1.0, "down_three": 8.0, "qkv_one": 0.1, "up_three": 3.0,
    "down_four": 1.0, "down_end": 0.02, "up_end": 0.02,
}


class Line:
    def __init__(self):
        self.token = None

    def call(self, kernel, outs, args, scalars=(), scratch=(), name=None, mib=8, far_in=(), far_out=(), us=0.0):
        args = [pltpu.with_memory_space_constraint(a, pltpu.HBM) if i in far_in else a for i, a in enumerate(args)]
        ins = [SCALARS if i in scalars else FAR if i in far_in else WHOLE for i in range(len(args))]
        to = [FAR if i in far_out else WHOLE for i in range(len(outs))]
        outs = [pltpu.HBM(o.shape, o.dtype) if i in far_out else o for i, o in enumerate(outs)]
        tokens = [] if self.token is None else [self.token]
        n_in, n_tok, n_out = len(args), len(tokens), len(outs)

        def body(*refs):
            left, right = refs[:n_in], refs[n_in + n_tok :]
            kernel(*left, *right[:n_out], *right[n_out + 1 :])
            right[n_out][...] = jnp.zeros((8, LANES), F32)

        *got, self.token = pl.pallas_call(
            body,
            out_shape=[*outs, shape((8, LANES), F32)],
            in_specs=ins + [WHOLE] * n_tok,
            out_specs=[*to, WHOLE],
            scratch_shapes=list(scratch),
            compiler_params=params(mib),
            cost_estimate=cost(us),
            name=name,
        )(*args, *tokens)
        return got


def kernel_name(kernel):
    return getattr(kernel, "func", kernel).__name__.split("_")[0]


def plus(a, b):
    return (a.astype(F32) + b.astype(F32)).astype(BF)


def view(ref, cut):
    return ref[:, :, slice(*cut[0]), slice(*cut[1])]


def one_kernel(cuts_a, cuts_b, count, *refs):
    got, kept = refs[:count], refs[count : 2 * count]
    sa, sb, ka, kb = refs[2 * count :]
    at = 0
    for i, cut in cuts_a:
        total = plus(view(got[i], cut), view(kept[i], cut))
        m = total.shape[2]
        sa[:, :, at : at + m, :] = total[:, 4:]
        ka[:, :, at : at + m, :] = total[:, :4]
        at += m
    at = 0
    for i, cut in cuts_b:
        total = plus(view(got[i], cut), view(kept[i], cut))
        m = total.shape[2]
        sb[:, at : at + m, :] = total[1]
        kb[:, at : at + m, :] = total[0]
        at += m


def two_kernel(ga, gb, ka, kb, sa, sb, la, lb):
    a = plus(ga[...], ka[...])
    sa[...] = a[1]
    la[...] = a[0]
    b = plus(gb[...], kb[...])
    sb[...] = b[4:]
    lb[...] = b[:4]


def two_with_out_kernel(split, ga, gb, ka, kb, go, ko, sa, sb, la, lb, lx, ly):
    ma, mb, mo = ka.shape[2], kb.shape[1], ko.shape[2]
    two_kernel(ga, gb, ka, kb, sa.at[:, :ma, :], sb.at[:, :mb, :], la, lb)
    total = plus(go[...], ko[...])
    rest = mo - split
    sb[:, mb : mb + split, :] = total[0, 4:, :split]
    sb[:, mb + split :, :] = total[1, 4:, :split]
    lx[...] = total[:, :4, :split]
    sa[:, ma : ma + rest, :] = total[1, :4, split:]
    sa[:, ma + rest :, :] = total[1, 4:, split:]
    ly[...] = total[0, :, split:]


def two_from_out_kernel(ga, gb, ka, kb, gx, gy, kx, ky, sa, sb, la, lb):
    ma, mb, nx, ny = ka.shape[2], kb.shape[1], kx.shape[2], ky.shape[1]
    two_kernel(ga, gb, ka, kb, sa.at[:, :ma, :], sb.at[:, :mb, :], la.at[:, :ma, :], lb.at[:, :mb, :])
    x0, y0 = gx.shape[1] - 2 * nx, gy.shape[1] - 2 * ny
    la[:, ma:, :] = plus(gx[:, x0 : x0 + nx, :], kx[0])
    sa[:, ma:, :] = plus(gx[:, x0 + nx :, :], kx[1])
    lb[:, mb:, :] = plus(gy[:, y0 : y0 + ny, :], ky[:4])
    sb[:, mb:, :] = plus(gy[:, y0 + ny :, :], ky[4:])


def three_kernel(ga, gb, ka, kb, send, keep):
    m, mb = ka.shape[1], kb.shape[1]
    a, b = plus(ga[:, :m, :], ka[...]), plus(gb[:, :mb, :], kb[...])
    send[:, :m, :] = a[2:]
    keep[:, :m, :] = a[:2]
    send[:, m:, :] = b[2:]
    keep[:, m:, :] = b[:2]


def four_kernel(got, kept, send, keep):
    total = plus(got[...], kept[...])
    send[...] = total[1]
    keep[...] = total[0]


def five_kernel(got, kept, mine):
    mine[...] = plus(got[...], kept[...])


def six_kernel(info, mine, other, both):
    both[info[9]] = mine[...]
    both[1 - info[9]] = other[...]


def down_kernel(info, mine, other, out):
    m = mine.shape[1] // 2
    cols = mine.shape[2]
    for rc, ref in ((0, mine), (1, other)):
        for p in range(2):
            block = jnp.concatenate([ref[0, p * m : (p + 1) * m], ref[1, p * m : (p + 1) * m]], axis=0)
            at = (info[8] ^ rc) * 2 * cols + p * cols
            out[:, pl.ds(pl.multiple_of(at, cols), cols)] = block.astype(F32)


def up_kernel(info, mine, other, out):
    half = out.shape[0] // 2
    m = half // 2
    for rc, ref in ((0, mine), (1, other)):
        for a in range(2):
            at = (info[8] ^ rc) * half + a * m
            out[pl.ds(pl.multiple_of(at, m), m), :] = ref[a].astype(F32)


def qkv_kernel(info, mine, other, gq, gk, gv, go, *vecs):
    half = gq.shape[1] // 2
    for rc, ref in ((0, mine), (1, other)):
        at = pl.ds(pl.multiple_of((info[8] ^ rc) * half, half), half)

        def put(out, *spans):
            parts = [ref[a, i : i + m] for a, i, m in spans]
            out[:, at] = jnp.concatenate(parts, axis=0).astype(F32)

        put(gq, (0, 0, 48), (1, 0, 48))
        put(gk, (0, 48, 16), (1, 48, 16), (0, 160, 32), (1, 160, 32))
        put(gv, (0, 112, 48), (1, 112, 48))
        put(go, (0, 80, 32), (0, 192, 16), (1, 80, 32), (1, 192, 16))
    rs = vecs[0].shape[0]
    low = jnp.where(info[8] == 0, mine[:, 64:80, :].astype(F32), other[:, 64:80, :].astype(F32))
    for i, out in enumerate(vecs[:8]):
        out[...] = low[0, i, :rs]
    for c in range(4):
        vecs[8][pl.ds(c * rs, rs)] = low[1, c, :rs]


def local(n_dp, n_seq, *args):
    (
        tokens, seg_lengths, w_query, b_query, w_key, w_value, b_value, w_out, b_out,
        gain_attn, shift_attn, w_up, b_up, w_down, b_down, gain_ffn, shift_ffn,
        grad_output, grad_pooled,
    ) = args
    line = Line()
    me = lax.axis_index("seq")
    dp = lax.axis_index("dp")
    core, y = me % 2, me // 2
    rows, piece, width = tokens.shape
    tok = n_seq * piece
    ff = w_up.shape[1]
    fast = n_dp == 8
    n = n_dp if fast else 1
    rs = width // n
    half = width // 2
    xor = [[(i, i ^ r) for i in range(n_seq)] for r in range(n_seq)]

    if fast:
        j = jnp.arange(8, dtype=jnp.int32) ^ dp
        pos = (j % 2) * 4 + (j // 2 % 2) * 2 + j // 4
    else:
        pos = jnp.zeros((8,), jnp.int32)
    info = jnp.concatenate([pos, jnp.stack([core, y, me]), jnp.zeros((5,), jnp.int32)]).astype(jnp.int32)

    def rel(a, name):
        parts = line.call(
            split_kernel, [shape((piece, width))] * n_seq, (info, a), scalars=(0,), scratch=[sems(n_seq)],
            name=name, far_in=(1,),
        )
        return [parts[0]] + [lax.ppermute(parts[r], "seq", xor[r]) for r in range(1, n_seq)]

    xs = rel(tokens, "split_tokens")
    gs = rel(grad_output, "split_grads")

    lengths = lax.dynamic_index_in_dim(seg_lengths, me, 0, keepdims=False)
    ends = jnp.cumsum(lengths)
    order = me ^ jnp.arange(n_seq, dtype=jnp.int32)
    places = (order[:, None] * piece + jnp.arange(piece, dtype=jnp.int32)[None, :]).reshape(tok)
    seg = jnp.sum((places[:, None] >= ends[None, :]).astype(jnp.int32), axis=1)
    lane = jnp.arange(LANES, dtype=jnp.int32)
    hot = seg[:, None] == lane[None, :]
    onehot = hot.astype(BF)
    kaug = jnp.where((lane < SEGS)[None, :] & ~hot, NEG, 0.0).astype(BF)
    onehot_t = (seg[None, :] == jnp.arange(16, dtype=jnp.int32)[:, None]).astype(BF)
    length_col = lengths.astype(F32)[:, None]
    gpool = lax.dynamic_index_in_dim(grad_pooled, me, 0, keepdims=False).astype(F32) / length_col
    gp_hi = gpool.astype(BF)
    gp_low = (gpool - gp_hi.astype(F32)).astype(BF)
    zeros = jnp.zeros((LANES - SEGS, width), BF)
    gpl = jnp.concatenate([gp_hi, zeros, gp_low, zeros], axis=0)


    sq = shape((tok, width))
    sqf = shape((tok, width), F32)
    row_lengths = jnp.broadcast_to(seg_lengths.astype(F32)[:, :, None], (rows, SEGS, LANES))
    lanes = shape((tok, LANES))
    lanes_f = shape((tok, LANES), F32)
    x, q, k, v, att, inv, qaug, n1 = line.call(
        attend_kernel,
        [sq, sq, sq, sq, sqf, lanes_f, lanes, sqf],
        (*xs, w_query, w_key, w_value, w_out, onehot, kaug, b_query, b_value, b_out),
        scratch=[buf((tok, width))] * 4
        + [buf((tok, width), F32), buf((tok, LANES), F32), buf((tok, LANES))]
        + [buf((width, width))] * 4
        + [buf((PART, tok), F32), sems(15)],
        name="attend",
        mib=20,
        far_in=range(4, 8),
        far_out=range(7),
    )

    halves = 2 if fast else 1
    lay = (n, halves, rs)
    wire_d = shape((halves, n, rs // halves, ff // 2))
    steps = ff // width
    *outs, gp, d_send, d_keep, pool, r2, vec_b = line.call(
        functools.partial(ffn_kernel, lay),
        [shape((piece, width))] * 4
        + [shape((tok, ff)), wire_d, wire_d, shape((16, width), F32), sqf, shape((8, width), F32)],
        (
            info, n1, gain_attn, shift_attn, b_down, gain_ffn, shift_ffn, w_up, b_up, w_down, *gs, onehot, onehot_t, gpl,
        ),
        scalars=(0,),
        scratch=[
            buf((tok, width)), buf((tok, width), F32), buf((tok, ff)), buf((width, tok)), buf((tok, ff)), buf((ff, width)),
            buf((1, ff), F32), sems(steps), sems(steps),
        ],
        name="ffn",
        mib=24,
        far_in=(9,),
        far_out=(4,),
    )

    pp_core = lambda a: lax.ppermute(a, "seq", xor[1])
    pp_y = lambda a: lax.ppermute(a, "seq", xor[2])

    def pp_dp(bit):
        return lambda a: lax.ppermute(a, "dp", [(i, i ^ bit) for i in range(n_dp)])

    pp_x, pp_z1, pp_z2 = pp_dp(1), pp_dp(2), pp_dp(4)

    def join_rows(parts):
        return parts[0] if len(parts) == 1 else jnp.concatenate(parts, axis=-2)

    class Sum:
        def __init__(self, name, got, kept, cuts_a, cuts_b):
            self.name, self.got, self.kept = name, got, kept
            self.cuts = cuts_a, cuts_b

        def run(self, kernel, outs, args, scalars=()):
            name = self.name + kernel_name(kernel)
            return line.call(
                kernel, [shape(o) for o in outs], args, scalars=scalars, name=name, mib=16, us=COSTS.get(name, 0.3)
            )

        def one(self):
            a, b = (sum(r1 - r0 for _, ((r0, r1), _) in cut) for cut in self.cuts)
            c = self.cuts[0][0][1][1]
            c = c[1] - c[0]
            sa, sb, ka, kb = self.run(
                functools.partial(one_kernel, *self.cuts, len(self.got)),
                [(2, 4, a, c), (8, b, c), (2, 4, a, c), (8, b, c)],
                (*self.got, *self.kept),
            )
            self.got, self.kept = (pp_x(sa), pp_y(sb)), (ka, kb)
            self.dims = a, b, c

        def two(self):
            a, b, c = self.dims
            sa, sb, ka, kb = self.run(two_kernel, [(4, a, c), (4, b, c)] * 2, (*self.got, *self.kept))
            self.got, self.kept = (pp_y(sa), pp_x(sb)), (ka, kb)

        def two_with_out(self, got, kept, split):
            a, b, c = self.dims
            m = kept.shape[2]
            rest = m - split
            sa, sb, ka, kb, kx, ky = self.run(
                functools.partial(two_with_out_kernel, split),
                [(4, a + 2 * rest, c), (4, b + 2 * split, c), (4, a, c), (4, b, c), (2, 4, split, c), (8, rest, c)],
                (*self.got, *self.kept, got, kept),
            )
            self.got, self.kept = (pp_y(sa), pp_x(sb)), (ka, kb)
            return self.got[1], self.got[0], kx, ky

        def two_from_out(self, gx, gy, kx, ky):
            a, b, c = self.dims
            a, b = a + kx.shape[2], b + ky.shape[1]
            self.dims = a, b, c
            sa, sb, ka, kb = self.run(
                two_from_out_kernel, [(4, a, c), (4, b, c)] * 2, (*self.got, *self.kept, gx, gy, kx, ky)
            )
            self.got, self.kept = (pp_y(sa), pp_x(sb)), (ka, kb)

        def three(self):
            a, b, c = self.dims
            send, keep = self.run(three_kernel, [(2, a + b, c)] * 2, (*self.got, *self.kept))
            self.got, self.kept = pp_z1(send), keep

        def four(self):
            a, b, c = self.dims
            send, keep = self.run(four_kernel, [(a + b, c)] * 2, (self.got, self.kept))
            self.got, self.kept = pp_z2(send), keep

        def five(self):
            a, b, c = self.dims
            (mine,) = self.run(five_kernel, [(a + b, c)], (self.got, self.kept))
            self.got, self.kept = pp_y(mine), mine

        def six(self):
            a, b, c = self.dims
            (both,) = self.run(six_kernel, [(2, a + b, c)], (info, self.kept, self.got), scalars=(0,))
            self.got, self.kept = pp_core(both), both

        def end(self, kernel, outs):
            return line.call(
                kernel, outs, (info, self.kept, self.got), scalars=(0,), name=self.name + "end", mib=16
            )

    wire_u = shape((halves, n, half // halves, ff // n))
    if fast:
        d_got = pp_core(d_send)
    u_send, u_keep, bup, gpre = line.call(
        functools.partial(ffn_back_kernel, lay),
        [wire_u, wire_u, shape((8, ff), F32), shape((tok, ff))],
        (info, r2, gp, w_down, n1, gain_attn, shift_attn),
        scalars=(0,),
        scratch=[buf((tok, width)), buf((width, tok)), buf((tok, ff)), sems(steps)],
        name="ffn_back",
        mib=12,
        far_in=(2,),
    )
    if fast:
        u_got = pp_core(u_send)
        c, m = ff // 4, rs // 2
        down = Sum("down_", [d_got], [d_keep], [(0, ((0, m), (0, c)))], [(0, ((0, m), (c, 2 * c)))])
        down.one()
    wire_o = shape((halves, n, rs // halves, half))
    r1, gatt, gaug, vec_c, o_send, o_keep = line.call(
        functools.partial(norm_back_kernel, lay),
        [sqf, sq, shape((tok, LANES)), shape((8, width), F32), wire_o, wire_o],
        (info, r2, gpre, w_up, n1, inv, gain_attn, w_out, att),
        scalars=(0,),
        scratch=[buf((width, tok)), buf((tok, width), F32), buf((tok, width), F32), sems(4)],
        name="norm_back",
        mib=14,
        far_out=(0,),
    )
    if fast:
        o_got = pp_core(o_send)
        m = half // 2
        up = Sum("up_", [u_got], [u_keep], [(0, ((0, m // 2), (0, half)))], [(0, ((m // 2, m), (0, half)))])
        up.one()

    gq, gk, gv, gqt, gkt, gvt, vec_d = line.call(
        attend_back_kernel,
        [sq] * 3 + [shape((width, tok))] * 3 + [shape((8, width), F32)],
        (q, k, v, gatt, qaug, kaug, gaug),
        name="attend_back",
        mib=10,
    )
    vecs = jnp.concatenate([vec_d[:2], vec_c[:3], vec_b[:3]], axis=0)
    if fast:
        down.two()
    rows_a, rows_b = (80, 80) if fast else (2 * width, width)
    wire_a, wire_b = shape((halves, n, rows_a, half)), shape((halves, n, rows_b, half))
    qa_send, qb_send, qa_keep, qb_keep, *ins = line.call(
        functools.partial(project_back_kernel, lay),
        [wire_a, wire_b, wire_a, wire_b] + [shape((piece, width))] * 4,
        (info, gq, gk, gv, gqt, gkt, gvt, x, r1, w_query, w_key, w_value, vecs, bup),
        scalars=(0,),
        name="project_back",
        mib=16,
    )

    def send_back():
        packs = line.call(
            pack_kernel, [shape((2 * piece + 2 * SEGS, width))] * n_seq, (*outs, *ins, pool), name="pack"
        )
        return [packs[0]] + [lax.ppermute(packs[r], "seq", xor[r]) for r in range(1, n_seq)]

    def take_back(packs):
        return line.call(
            unpack_kernel,
            [shape((rows, piece, width)), shape((rows, piece, width)), shape((rows, SEGS, width), F32)],
            (info, row_lengths, *packs),
            scalars=(0,),
            name="unpack",
        )

    if fast:
        qkv = Sum(
            "qkv_", [pp_core(qa_send), pp_core(qb_send)], [qa_keep, qb_keep],
            [(0, ((0, 80), (0, half)))],
            [(1, ((0, 80), (0, half)))],
        )
        f32 = lambda *d: shape(d, F32)
        out_sum = up.two_with_out(o_got, o_keep, 32)
        down.three()
        qkv.one()
        packs = send_back()
        up.three()
        down.four()
        qkv.two_from_out(*out_sum)
        up.four()
        down.five()
        down.six()
        qkv.three()
        up.five()
        up.six()
        qkv.four()
        (g_down,) = down.end(down_kernel, [f32(rs, ff)])
        (g_up,) = up.end(up_kernel, [f32(width, ff // n)])
        qkv.five()
        output, grad_tokens, pooled = take_back(packs)
        qkv.six()
        *g_qkv, g_out, v0, v1, v2, v3, v4, v5, v6, v7, v8 = qkv.end(
            qkv_kernel, [f32(rs, width)] * 4 + [f32(rs)] * 8 + [f32(4 * rs)]
        )
        g_down, g_out, g_qkv = g_down.T, g_out.T, [g.T for g in g_qkv]
        small = [v0, v1, v2, v3, v4, v5, v6, v7, v8]
    else:
        output, grad_tokens, pooled = take_back(send_back())

        def total(send, keep, dim):
            h = keep.astype(F32) + pp_core(send).astype(F32)
            h = h + pp_y(h.astype(BF)).astype(F32)
            return lax.psum_scatter(h, "dp", scatter_dimension=dim, tiled=True).astype(BF)

        def whole(send, keep, dim, along):
            mine = total(send, keep, dim)
            other = pp_core(mine)
            lo, hi = jnp.where(core == 0, mine, other), jnp.where(core == 0, other, mine)
            return jnp.concatenate([lo, hi], axis=along).astype(F32)

        g_down = whole(d_send[0, 0], d_keep[0, 0], 0, 1).T
        g_up = whole(u_send[0, 0], u_keep[0, 0], 1, 0)
        g_out = whole(o_send[0, 0], o_keep[0, 0], 0, 1).T
        g_qkv = [
            whole(send, keep, 0, 1).T
            for send, keep in (
                (qa_send[0, 0, :width], qa_keep[0, 0, :width]),
                (qa_send[0, 0, width:], qa_keep[0, 0, width:]),
                (qb_send[0, 0], qb_keep[0, 0]),
            )
        ]
        flat = lax.psum(jnp.concatenate([vecs.reshape(-1), bup[0]]), ("dp", "seq"))
        mine = width // n_dp
        small = [
            lax.dynamic_slice_in_dim(flat, i * width + dp * mine, mine) for i in range(8)
        ] + [lax.dynamic_slice_in_dim(flat, 8 * width + dp * 4 * mine, 4 * mine)]

    bq, bv, b_o, gain1, shift1, b_d, gain2, shift2, b_u = small
    return (
        output, pooled, grad_tokens, g_qkv[0], bq, g_qkv[1], g_qkv[2], bv, g_out, b_o, gain1, shift1,
        g_up, b_u, g_down, b_d, gain2, shift2,
    )


def solution(mesh):
    rows = P("dp", "seq", None)
    placed = (rows, P("dp", None)) + (P(),) * 15 + (rows, P("dp", None, None))
    col, one = P(None, "dp"), P("dp")
    return jax.shard_map(
        functools.partial(local, mesh.shape["dp"], mesh.shape["seq"]),
        mesh=mesh,
        in_specs=placed,
        out_specs=(
            rows, P("dp", None, None), rows, col, one, col, col, one, col, one, one, one,
            col, one, col, one, one, one,
        ),
        check_vma=False,
    )
```

```python
import functools

import jax
import jax.numpy as jnp
from jax import lax
from jax.experimental import pallas as pl
from jax.experimental.pallas import tpu as pltpu
from jax.sharding import PartitionSpec as P

HD = 64
SEGS = 8
BF = jnp.bfloat16
F32 = jnp.float32
EPS = 1e-06
NEG = -1e30
LANES = 128

PART = 16
ROWS = 32


def nn(a, b):
    return jnp.dot(a, b, preferred_element_type=F32)


def nt(a, b):
    return lax.dot_general(a, b, (((1,), (1,)), ((), ())), preferred_element_type=F32)


def three_parts(v):
    hi = v.astype(BF)
    rest = v - hi.astype(F32)
    mid = rest.astype(BF)
    low = (rest - mid.astype(F32)).astype(BF)
    return hi, mid, low


def two_parts(v):
    hi = v.astype(BF)
    return hi, (v - hi.astype(F32)).astype(BF)


def norm(value):
    centre = value - jnp.mean(value, axis=-1, keepdims=True)
    inverse = lax.rsqrt(jnp.mean(centre * centre, axis=-1, keepdims=True) + EPS)
    return centre * inverse, inverse


def norm_back(grad, normed, inverse):
    a = jnp.mean(grad, axis=-1, keepdims=True)
    b = jnp.mean(grad * normed, axis=-1, keepdims=True)
    return (grad - a - normed * b) * inverse


def gelu_both(x):
    phi = 0.5 + 0.5 * lax.erf(x * (0.5**0.5))
    density = 0.3989422804014327 * jnp.exp(x * x * -0.5)
    return x * phi, phi + x * density


def row(ref):
    return ref[...].astype(F32).reshape(1, ref.shape[0])


def fold(v):
    out = v[:8]
    for i in range(8, v.shape[0], 8):
        out += v[i : i + 8]
    return out


def total(v):
    return jnp.sum(v, axis=0, keepdims=True)


def head_lane(h):
    lane = lax.broadcasted_iota(jnp.int32, (1, LANES), 1)
    return (lane % PART == h) & (lane >= PART) & (lane < 4 * PART)


def put_rows(out_ref, lead, y, rows, halves, cols, value):
    n = value.shape[0] // halves
    for a in range(halves):
        side = jnp.where(y == a, 0, 1) if halves > 1 else 0
        out_ref[side, lead, pl.ds(rows, n), cols] = value[a * n : (a + 1) * n].astype(BF)


def put_shards(out_ref, info, lay, cols, value, rows=0, first=0):
    n, halves, rs = lay
    count = value.shape[0] // rs
    for i in range(count):
        lead = info[first * count + i] if n > 1 else 0
        put_rows(out_ref, lead, info[9], rows, halves, cols, value[i * rs : (i + 1) * rs])


def copies(pairs, sems, first=0):
    out = []
    for i, (src, dst) in enumerate(pairs):
        out.append(pltpu.make_async_copy(src, dst, sems.at[first + i]))
        out[-1].start()
    return out


def wait(moves):
    for m in moves:
        m.wait()


def split_kernel(info, x_ref, *refs):
    outs, sems = refs[:-1], refs[-1]
    wait(copies([(x_ref.at[info[10] ^ r], outs[r]) for r in range(len(outs))], sems))


def fetch_kernel(a, b, c, x, y, z, sems):
    wait(copies([(a, x), (b, y), (c, z)], sems))


def pack_kernel(o0, o1, o2, o3, i0, i1, i2, i3, pool, p0, p1, p2, p3):
    n = o0.shape[0]
    hi, low = two_parts(pool[:SEGS, :])
    for p, o, i in ((p0, o0, i0), (p1, o1, i1), (p2, o2, i2), (p3, o3, i3)):
        p[:n, :] = o[...]
        p[n : 2 * n, :] = i[...]
        p[2 * n : 2 * n + SEGS, :] = hi
        p[2 * n + SEGS :, :] = low


def unpack_kernel(info, lengths, p0, p1, p2, p3, out, grad, pool):
    me = info[10]
    n = out.shape[1]
    for r, p in enumerate((p0, p1, p2, p3)):
        out[me ^ r] = p[:n, :]
        grad[me ^ r] = p[n : 2 * n, :]
        sums = p[2 * n :, :].astype(F32)
        pool[me ^ r] = (sums[:SEGS] + sums[SEGS:]) / lengths[me ^ r][:, :1]


def attend_kernel(
    x0, x1, x2, x3, wq, wk, wv, wo_h, oh_ref, ka_ref, bq_ref, bv_ref, bo_ref,
    x_h, q_h, k_h, v_h, att_h, inv_h, qa_h, n1_out,
    x_out, q_out, k_out, v_out, att_out, inv_out, qa_out, wo, stat, sems,
):
    n = x0.shape[0]
    bq, bv, bo = row(bq_ref), row(bv_ref), row(bo_ref)
    last = copies([(wo_h, wo)], sems, 4)
    for r, ref in enumerate((x0, x1, x2, x3)):
        x_out[r * n : (r + 1) * n] = ref[...]
    outs = copies([(x_out, x_h)], sems, 8)
    x = x_out[...]
    q_out[...] = ((nn(x, wq[...]) + bq).astype(BF).astype(F32) * (HD**-0.5)).astype(BF)
    outs += copies([(q_out, q_h)], sems, 9)
    k_out[...] = nn(x, wk[...]).astype(BF)
    outs += copies([(k_out, k_h)], sems, 10)
    v_out[...] = (nn(x, wv[...]) + bv).astype(BF)
    outs += copies([(v_out, v_h)], sems, 11)
    tok, width = x.shape
    stat[...] = jnp.zeros_like(stat)
    ones = jnp.ones((16, tok), BF)

    def pair(p, carry):
        sl = pl.ds(pl.multiple_of(p * LANES, LANES), LANES)
        qcat = jnp.concatenate([q_out[:, sl], oh_ref[...]], axis=1)
        kp = k_out[:, sl]
        vt = v_out[:, sl].T
        lane = lax.broadcasted_iota(jnp.int32, (1, LANES), 1)
        parts = []
        for h in range(2):
            kh = jnp.where((lane < HD) == (h == 0), kp, jnp.zeros_like(kp))
            st = nt(jnp.concatenate([kh, ka_ref[...]], axis=1), qcat)
            m = jnp.max(st, axis=0, keepdims=True)
            pb = jnp.exp(st - m).astype(BF)
            ot = nn(jnp.concatenate([vt[h * HD : (h + 1) * HD], ones], axis=0), pb)
            total = ot[HD : HD + 1]
            stat[pl.ds(2 * p + h, 1), :] = m + jnp.log(total)
            parts.append(ot[:HD] / total)
        att_out[:, sl] = jnp.concatenate(parts, axis=0).T
        return carry

    lax.fori_loop(0, width // LANES, pair, 0, unroll=2)
    outs += copies([(att_out, att_h)], sems, 12)
    hi, mid, low = three_parts(stat[...])
    zero = jnp.zeros((PART, tok), BF)
    qa_out[...] = jnp.concatenate([zero, hi, mid, low, zero, zero, zero, zero], axis=0).T + oh_ref[...]
    outs += copies([(qa_out, qa_h)], sems, 13)
    wait(last)
    n1_out[...] = nn(att_out[...].astype(BF), wo[...])
    for at in range(0, tok, ROWS):
        rows = slice(at, at + ROWS)
        n1, inv = norm(x_out[rows, :].astype(F32) + (n1_out[rows, :] + bo))
        n1_out[rows, :] = n1
        inv_out[rows, :] = jnp.broadcast_to(inv, (ROWS, LANES))
    outs += copies([(inv_out, inv_h)], sems, 14)
    wait(outs)


def ffn_kernel(
    lay, info, n1_ref, ga_ref, sa_ref, bd_ref, gf_ref, sf_ref, wu, bu_ref, wd_h, g0, g1, g2, g3, oh_ref, oht_ref, gpl,
    o0, o1, o2, o3, gp_out, send, keep, pool_out, r2_out, vec_out,
    hl, acc, act, gt, wd, bu, gsum, hi, low, gl, sem_w,
):
    n = g0.shape[0]
    ga, sa, bd, gf, sf = row(ga_ref), row(sa_ref), row(bd_ref), row(gf_ref), row(sf_ref)
    bu[...] = row(bu_ref)
    tok, width = acc.shape
    ff = act.shape[1]
    tile = width
    steps = ff // tile

    def weights(t):
        rows = pl.ds(pl.multiple_of(t * tile, tile), tile)
        return pltpu.make_async_copy(wd_h.at[rows, :], wd.at[rows, :], sem_w.at[t])

    for t in range(steps):
        weights(t).start()
    hl[...] = (n1_ref[...] * ga + sa).astype(BF)
    acc[...] = jnp.zeros_like(acc)

    def step(t, carry):
        cols = pl.ds(pl.multiple_of(t * tile, tile), tile)
        weights(t).wait()
        for r in range(2):
            rows = pl.ds(r * 2 * n, 2 * n)
            a, d = gelu_both(nn(hl[rows, :], wu[:, cols]) + bu[:, cols])
            ab = a.astype(BF)
            act[rows, cols] = ab
            gp_out[rows, cols] = d.astype(BF)
            acc[rows, :] += nn(ab, wd[cols, :])
        return carry

    lax.fori_loop(0, steps, step, 0)
    oh = oh_ref[...]
    gsum[...] = nn(jnp.concatenate([oh, oh], axis=1), gpl[...])
    gain, shift, bias = (jnp.zeros((8, width), F32) for _ in range(3))
    gs, os = (g0, g1, g2, g3), (o0, o1, o2, o3)
    for at in range(0, tok, ROWS):
        rows = slice(at, at + ROWS)
        r, of = at // n, slice(at % n, at % n + ROWS)
        hidden = n1_ref[rows, :] * ga + sa
        n2, inv = norm(hidden + (acc[rows, :] + bd))
        result = n2 * gf + sf
        os[r][of, :] = result.astype(BF)
        hi[rows, :], low[rows, :] = two_parts(result)
        gout = gs[r][of, :].astype(F32) + gsum[rows, :]
        gain += fold(gout * n2)
        shift += fold(gout)
        gr2 = norm_back(gout * gf, n2, inv)
        r2_out[rows, :] = gr2
        low_g = gr2.astype(BF)
        bias += fold(low_g.astype(F32))
        gl[rows, :] = low_g
    gt[...] = gl[...].T
    pool_out[...] = nn(oht_ref[...], hi[...]) + nn(oht_ref[...], low[...])
    vec_out[...] = jnp.concatenate([total(v) for v in (bias, gain, shift)] + [jnp.zeros((5, width), F32)], axis=0)
    half = ff // 2
    part = 768

    def piece(i, carry):
        for rc, ref in ((1, send), (0, keep)):
            at = (info[8] ^ rc) * half + i * part
            res = nn(gt[...], act[:, pl.ds(pl.multiple_of(at, part), part)])
            put_shards(ref, info, lay, pl.ds(pl.multiple_of(i * part, part), part), res)
        return carry

    lax.fori_loop(0, half // part, piece, 0)


def ffn_back_kernel(
    lay, info, r2_ref, gp, wd, n1_ref, ga_ref, sa_ref,
    send, keep, bup_out, gpre_out,
    gl, hlt,
):
    ga, sa = row(ga_ref), row(sa_ref)
    width = hlt.shape[0]
    half = width // 2
    ff = gp.shape[1]
    tile = width
    steps = ff // tile

    gl[...] = r2_ref[...].astype(BF)
    hlt[...] = (n1_ref[...] * ga + sa).astype(BF).T
    per = 2 if lay[0] > 1 else 1

    def step(t, carry):
        cols = pl.ds(pl.multiple_of(t * tile, tile), tile)
        gpre = (nt(gl[...], wd[cols, :]) * gp[:, cols].astype(F32)).astype(BF)
        gpre_out[:, cols] = gpre
        bup_out[:, cols] = jnp.broadcast_to(
            jnp.sum(gpre.astype(F32), axis=0, keepdims=True), (bup_out.shape[0], tile)
        )
        for rc, ref in ((1, send), (0, keep)):
            at = pl.multiple_of((info[8] ^ rc) * half, half)
            res = nn(hlt[pl.ds(at, half), :], gpre)
            for i in range(per):
                if lay[0] > 1:
                    put_rows(ref, info[per * t + i], info[9], 0, lay[1], slice(None), res[:, i * half : (i + 1) * half])
                else:
                    put_rows(ref, 0, info[9], 0, lay[1], cols, res)
        return carry

    lax.fori_loop(0, steps, step, 0)


def norm_back_kernel(
    lay, info, r2_ref, gpre, wu, n1_ref, inv_ref, ga_ref, wo, att,
    r1_out, gatt_out, gaug_out, vec_out, osend, okeep,
    gt, acc, gm, hi, low,
):
    ga = row(ga_ref)
    tok, width = r2_ref.shape
    half = width // 2
    head = lax.broadcasted_iota(jnp.int32, (width, LANES), 0) // HD
    lane = lax.broadcasted_iota(jnp.int32, (width, LANES), 1)
    pick = ((lane % PART == head) & (lane >= PART) & (lane < 4 * PART)).astype(BF)
    lane1 = lax.broadcasted_iota(jnp.int32, (1, LANES), 1)

    def step(t, carry):
        cols = pl.ds(pl.multiple_of(t * width, width), width)
        acc[...] += nt(gpre[:, cols], wu[:, cols])
        return carry

    acc[...] = r2_ref[...]
    lax.fori_loop(0, gpre.shape[1] // width, step, 0)
    gain, shift, bias = (jnp.zeros((8, width), F32) for _ in range(3))
    for at in range(0, tok, ROWS):
        rows = slice(at, at + ROWS)
        gh = acc[rows, :]
        n1 = n1_ref[rows, :]
        gain += fold(gh * n1)
        shift += fold(gh)
        gr1 = norm_back(gh * ga, n1, inv_ref[rows, :1])
        r1_out[rows, :] = gr1
        low_g = gr1.astype(BF)
        bias += fold(low_g.astype(F32))
        gm[rows, :] = low_g
    gt[...] = gm[...].T
    gatt_out[...] = nt(gm[...], wo[...]).astype(BF)
    for at in range(0, tok, ROWS):
        rows = slice(at, at + ROWS)
        hi[rows, :], low[rows, :] = two_parts(gatt_out[rows, :].astype(F32) * att[rows, :])
    a, b, c = three_parts(nn(hi[...], pick) + nn(low[...], pick))
    gaug_out[...] = jnp.where(lane1 < 2 * PART, a, jnp.where(lane1 < 3 * PART, b, c))
    vec_out[...] = jnp.concatenate([total(v) for v in (bias, gain, shift)] + [jnp.zeros((5, width), F32)], axis=0)
    sides = [att[:, pl.ds(pl.multiple_of((info[8] ^ rc) * half, half), half)].astype(BF) for rc in (1, 0)]
    res = nn(gt[...], jnp.concatenate(sides, axis=1))
    put_shards(osend, info, lay, slice(None), res[:, :half])
    put_shards(okeep, info, lay, slice(None), res[:, half:])


def attend_back_kernel(
    q, k, v, g, qa, ka, ga,
    gq, gk, gv, gqt, gkt, gvt, vec_out,
):
    tok, width = q.shape

    def pair(p, carry):
        sl = pl.ds(pl.multiple_of(p * LANES, LANES), LANES)
        qp, kp, vp, gp = q[:, sl], k[:, sl], v[:, sl], g[:, sl]
        qcat = jnp.concatenate([qp, qa[...]], axis=1)
        gcat = jnp.concatenate([gp, ga[...]], axis=1)
        kt = kp.T
        lane = lax.broadcasted_iota(jnp.int32, (1, LANES), 1)
        gkp = jnp.zeros((tok, LANES), F32)
        gvp = jnp.zeros((tok, LANES), F32)
        parts = []
        zero = jnp.zeros_like(kp)
        for h in range(2):
            mine = (lane < HD) == (h == 0)
            pick = head_lane(2 * p + h)
            kaug = jnp.where(pick, -jnp.ones((), BF), ka[...])
            vaug = jnp.where(pick, -jnp.ones((), BF), jnp.zeros((tok, LANES), BF))
            prob = jnp.exp(nt(jnp.concatenate([jnp.where(mine, kp, zero), kaug], axis=1), qcat))
            dp = nt(jnp.concatenate([jnp.where(mine, vp, zero), vaug], axis=1), gcat)
            ds = (prob * dp).astype(BF)
            gvp += nn(prob.astype(BF), jnp.where(mine, gp, zero))
            gkp += nn(ds, jnp.where(mine, qp, zero))
            parts.append(nn(kt[h * HD : (h + 1) * HD], ds))
        gqp = (jnp.concatenate(parts, axis=0) * (HD**-0.5)).astype(BF)
        gqt[sl, :] = gqp
        gq[:, sl] = gqp.T
        gkb, gvb = gkp.astype(BF), gvp.astype(BF)
        gk[:, sl] = gkb
        gv[:, sl] = gvb
        gkt[sl, :] = gkb.T
        gvt[sl, :] = gvb.T
        return carry

    lax.fori_loop(0, width // LANES, pair, 0, unroll=6)
    bq = jnp.sum(gq[...].astype(F32), axis=0, keepdims=True)
    bv = jnp.sum(gv[...].astype(F32), axis=0, keepdims=True)
    vec_out[...] = jnp.concatenate([bq, bv, jnp.zeros((6, width), F32)], axis=0)


def weights_back_kernel(lay, info, gqt, gkt, gvt, x_ref, vecs, bups, send_a, send_b, keep_a, keep_b):
    width = x_ref.shape[1]
    n, halves, rs = lay
    half = width // 2
    sides = [x_ref[:, pl.ds(pl.multiple_of((info[8] ^ rc) * half, half), half)] for rc in (1, 0)]
    right = jnp.concatenate(sides, axis=1)
    wires = ((1, (send_a, send_b)), (0, (keep_a, keep_b)))
    for m, left in enumerate((gqt, gkt, gvt)):
        both = nn(left[...], right)
        for rc, (wa, wb) in wires:
            res = both[:, :half] if rc else both[:, half:]
            if n > 1:
                for j in range(n):
                    rows = res[j * rs : (j + 1) * rs]
                    put = functools.partial(put_rows, lead=info[j], y=info[9], halves=halves, cols=slice(None))
                    if m == 0:
                        put(wa, rows=0, value=rows)
                    elif m == 1:
                        put(wa, rows=48, value=rows[:32])
                        put(wb, rows=48, value=rows[32:])
                    else:
                        put(wb, rows=0, value=rows)
            elif m < 2:
                wa[0, 0, pl.ds(m * width, width), :] = res.astype(BF)
            else:
                wb[0, 0] = res.astype(BF)
    if n > 1:
        for j in range(n):
            bup = bups[:1, j * 4 * rs : (j + 1) * 4 * rs]
            block = jnp.concatenate(
                [vecs[:, j * rs : (j + 1) * rs], jnp.zeros((8, rs), F32)]
                + [bup[:, c * rs : (c + 1) * rs] for c in range(4)]
                + [jnp.zeros((12, rs), F32)],
                axis=0,
            )
            block = jnp.concatenate([block, jnp.zeros((32, half - rs), F32)], axis=1)
            for rc, (wa, _) in wires:
                mine = jnp.where((info[8] ^ rc) == 0, 1.0, 0.0)
                put_rows(wa, info[j], info[9], 64, halves, slice(None), block * mine)


def input_back_kernel(gq, gk, gv, r1, wq, wk, wv, o0, o1, o2, o3):
    whole = r1[...] + nt(gq[...], wq[...]) + nt(gk[...], wk[...]) + nt(gv[...], wv[...])
    for r, o in enumerate((o0, o1, o2, o3)):
        c = o.shape[0]
        o[...] = whole[r * c : (r + 1) * c].astype(BF)


WHOLE = pl.BlockSpec(memory_space=pltpu.VMEM)
SCALARS = pl.BlockSpec(memory_space=pltpu.SMEM)
FAR = pl.BlockSpec(memory_space=pltpu.HBM)


def shape(dims, dtype=BF):
    return jax.ShapeDtypeStruct(tuple(dims), dtype)


def buf(dims, dtype=BF):
    return pltpu.VMEM(tuple(dims), dtype)


def sems(count):
    return pltpu.SemaphoreType.DMA((count,))


def params(mib):
    return pltpu.CompilerParams(vmem_limit_bytes=mib * 1024 * 1024)


def cost(us):
    return pl.CostEstimate(flops=int(us * 10**9) + 1, bytes_accessed=1, transcendentals=0)


COSTS = {
    "down_one": 0.1, "up_one": 0.1, "down_two": 0.1, "up_two": 1.0, "down_three": 8.0, "qkv_one": 0.1, "up_three": 3.0,
    "down_four": 1.0, "down_end": 0.02, "up_end": 0.02,
}


class Line:
    def __init__(self):
        self.token = None

    def call(self, kernel, outs, args, scalars=(), scratch=(), name=None, mib=8, far_in=(), far_out=(), us=0.0):
        args = [pltpu.with_memory_space_constraint(a, pltpu.HBM) if i in far_in else a for i, a in enumerate(args)]
        ins = [SCALARS if i in scalars else FAR if i in far_in else WHOLE for i in range(len(args))]
        to = [FAR if i in far_out else WHOLE for i in range(len(outs))]
        outs = [pltpu.HBM(o.shape, o.dtype) if i in far_out else o for i, o in enumerate(outs)]
        tokens = [] if self.token is None else [self.token]
        n_in, n_tok, n_out = len(args), len(tokens), len(outs)

        def body(*refs):
            left, right = refs[:n_in], refs[n_in + n_tok :]
            kernel(*left, *right[:n_out], *right[n_out + 1 :])
            right[n_out][...] = jnp.zeros((8, LANES), F32)

        *got, self.token = pl.pallas_call(
            body,
            out_shape=[*outs, shape((8, LANES), F32)],
            in_specs=ins + [WHOLE] * n_tok,
            out_specs=[*to, WHOLE],
            scratch_shapes=list(scratch),
            compiler_params=params(mib),
            cost_estimate=cost(us),
            name=name,
        )(*args, *tokens)
        return got


def kernel_name(kernel):
    return getattr(kernel, "func", kernel).__name__.split("_")[0]


def plus(a, b):
    return (a.astype(F32) + b.astype(F32)).astype(BF)


def view(ref, cut):
    return ref[:, :, slice(*cut[0]), slice(*cut[1])]


def one_kernel(cuts_a, cuts_b, count, *refs):
    got, kept = refs[:count], refs[count : 2 * count]
    sa, sb, ka, kb = refs[2 * count :]
    at = 0
    for i, cut in cuts_a:
        total = plus(view(got[i], cut), view(kept[i], cut))
        m = total.shape[2]
        sa[:, :, at : at + m, :] = total[:, 4:]
        ka[:, :, at : at + m, :] = total[:, :4]
        at += m
    at = 0
    for i, cut in cuts_b:
        total = plus(view(got[i], cut), view(kept[i], cut))
        m = total.shape[2]
        sb[:, at : at + m, :] = total[1]
        kb[:, at : at + m, :] = total[0]
        at += m


def two_kernel(ga, gb, ka, kb, sa, sb, la, lb):
    a = plus(ga[...], ka[...])
    sa[...] = a[1]
    la[...] = a[0]
    b = plus(gb[...], kb[...])
    sb[...] = b[4:]
    lb[...] = b[:4]


def two_with_out_kernel(split, ga, gb, ka, kb, go, ko, sa, sb, la, lb, lx, ly):
    ma, mb, mo = ka.shape[2], kb.shape[1], ko.shape[2]
    two_kernel(ga, gb, ka, kb, sa.at[:, :ma, :], sb.at[:, :mb, :], la, lb)
    total = plus(go[...], ko[...])
    rest = mo - split
    sb[:, mb : mb + split, :] = total[0, 4:, :split]
    sb[:, mb + split :, :] = total[1, 4:, :split]
    lx[...] = total[:, :4, :split]
    sa[:, ma : ma + rest, :] = total[1, :4, split:]
    sa[:, ma + rest :, :] = total[1, 4:, split:]
    ly[...] = total[0, :, split:]


def two_from_out_kernel(ga, gb, ka, kb, gx, gy, kx, ky, sa, sb, la, lb):
    ma, mb, nx, ny = ka.shape[2], kb.shape[1], kx.shape[2], ky.shape[1]
    two_kernel(ga, gb, ka, kb, sa.at[:, :ma, :], sb.at[:, :mb, :], la.at[:, :ma, :], lb.at[:, :mb, :])
    x0, y0 = gx.shape[1] - 2 * nx, gy.shape[1] - 2 * ny
    la[:, ma:, :] = plus(gx[:, x0 : x0 + nx, :], kx[0])
    sa[:, ma:, :] = plus(gx[:, x0 + nx :, :], kx[1])
    lb[:, mb:, :] = plus(gy[:, y0 : y0 + ny, :], ky[:4])
    sb[:, mb:, :] = plus(gy[:, y0 + ny :, :], ky[4:])


def three_kernel(ga, gb, ka, kb, send, keep):
    m, mb = ka.shape[1], kb.shape[1]
    a, b = plus(ga[:, :m, :], ka[...]), plus(gb[:, :mb, :], kb[...])
    send[:, :m, :] = a[2:]
    keep[:, :m, :] = a[:2]
    send[:, m:, :] = b[2:]
    keep[:, m:, :] = b[:2]


def four_kernel(got, kept, send, keep):
    total = plus(got[...], kept[...])
    send[...] = total[1]
    keep[...] = total[0]


def five_kernel(got, kept, mine):
    mine[...] = plus(got[...], kept[...])


def six_kernel(info, mine, other, both):
    both[info[9]] = mine[...]
    both[1 - info[9]] = other[...]


def down_kernel(info, mine, other, out):
    m = mine.shape[1] // 2
    cols = mine.shape[2]
    for rc, ref in ((0, mine), (1, other)):
        for p in range(2):
            block = jnp.concatenate([ref[0, p * m : (p + 1) * m], ref[1, p * m : (p + 1) * m]], axis=0)
            at = (info[8] ^ rc) * 2 * cols + p * cols
            out[:, pl.ds(pl.multiple_of(at, cols), cols)] = block.astype(F32)


def up_kernel(info, mine, other, out):
    half = out.shape[0] // 2
    m = half // 2
    for rc, ref in ((0, mine), (1, other)):
        for a in range(2):
            at = (info[8] ^ rc) * half + a * m
            out[pl.ds(pl.multiple_of(at, m), m), :] = ref[a].astype(F32)


def qkv_kernel(info, here, over_y, over_core, over_both, gq, gk, gv, go, *vecs):
    half = gq.shape[1] // 2
    y0 = info[9] == 0
    mine, other = (
        [jnp.where(y0, a[...], b[...]), jnp.where(y0, b[...], a[...])] for a, b in ((here, over_y), (over_core, over_both))
    )
    for rc, ref in ((0, mine), (1, other)):
        at = pl.ds(pl.multiple_of((info[8] ^ rc) * half, half), half)

        def put(out, *spans):
            parts = [ref[a][i : i + m] for a, i, m in spans]
            out[:, at] = jnp.concatenate(parts, axis=0).astype(F32)

        put(gq, (0, 0, 48), (1, 0, 48))
        put(gk, (0, 48, 16), (1, 48, 16), (0, 160, 32), (1, 160, 32))
        put(gv, (0, 112, 48), (1, 112, 48))
        put(go, (0, 80, 32), (0, 192, 16), (1, 80, 32), (1, 192, 16))
    rs = vecs[0].shape[0]
    low = [jnp.where(info[8] == 0, m[64:80].astype(F32), o[64:80].astype(F32)) for m, o in zip(mine, other)]
    for i, out in enumerate(vecs[:8]):
        out[...] = low[0][i, :rs]
    for c in range(4):
        vecs[8][pl.ds(c * rs, rs)] = low[1][c, :rs]


def local(n_dp, n_seq, *args):
    (
        tokens, seg_lengths, w_query, b_query, w_key, w_value, b_value, w_out, b_out,
        gain_attn, shift_attn, w_up, b_up, w_down, b_down, gain_ffn, shift_ffn,
        grad_output, grad_pooled,
    ) = args
    line = Line()
    me = lax.axis_index("seq")
    dp = lax.axis_index("dp")
    core, y = me % 2, me // 2
    rows, piece, width = tokens.shape
    tok = n_seq * piece
    ff = w_up.shape[1]
    fast = n_dp == 8
    n = n_dp if fast else 1
    rs = width // n
    half = width // 2
    xor = [[(i, i ^ r) for i in range(n_seq)] for r in range(n_seq)]

    if fast:
        j = jnp.arange(8, dtype=jnp.int32) ^ dp
        pos = (j % 2) * 4 + (j // 2 % 2) * 2 + j // 4
    else:
        pos = jnp.zeros((8,), jnp.int32)
    info = jnp.concatenate([pos, jnp.stack([core, y, me]), jnp.zeros((5,), jnp.int32)]).astype(jnp.int32)

    def rel(a, name):
        parts = line.call(
            split_kernel, [shape((piece, width))] * n_seq, (info, a), scalars=(0,), scratch=[sems(n_seq)],
            name=name, far_in=(1,),
        )
        return [parts[0]] + [lax.ppermute(parts[r], "seq", xor[r]) for r in range(1, n_seq)]

    xs = rel(tokens, "split_tokens")
    gs = rel(grad_output, "split_grads")

    lengths = lax.dynamic_index_in_dim(seg_lengths, me, 0, keepdims=False)
    ends = jnp.cumsum(lengths)
    order = me ^ jnp.arange(n_seq, dtype=jnp.int32)
    places = (order[:, None] * piece + jnp.arange(piece, dtype=jnp.int32)[None, :]).reshape(tok)
    seg = jnp.sum((places[:, None] >= ends[None, :]).astype(jnp.int32), axis=1)
    lane = jnp.arange(LANES, dtype=jnp.int32)
    hot = seg[:, None] == lane[None, :]
    onehot = hot.astype(BF)
    kaug = jnp.where((lane < SEGS)[None, :] & ~hot, NEG, 0.0).astype(BF)
    onehot_t = (seg[None, :] == jnp.arange(16, dtype=jnp.int32)[:, None]).astype(BF)
    length_col = lengths.astype(F32)[:, None]
    gpool = lax.dynamic_index_in_dim(grad_pooled, me, 0, keepdims=False).astype(F32) / length_col
    gp_hi = gpool.astype(BF)
    gp_low = (gpool - gp_hi.astype(F32)).astype(BF)
    zeros = jnp.zeros((LANES - SEGS, width), BF)
    gpl = jnp.concatenate([gp_hi, zeros, gp_low, zeros], axis=0)


    sq = shape((tok, width))
    sqf = shape((tok, width), F32)
    row_lengths = jnp.broadcast_to(seg_lengths.astype(F32)[:, :, None], (rows, SEGS, LANES))
    near = line.call(
        fetch_kernel, [shape((width, width))] * 3, (w_query, w_key, w_value), scratch=[sems(3)], name="fetch",
        far_in=range(3),
    )
    lanes = shape((tok, LANES))
    lanes_f = shape((tok, LANES), F32)
    x, q, k, v, att, inv, qaug, n1 = line.call(
        attend_kernel,
        [sq, sq, sq, sq, sqf, lanes_f, lanes, sqf],
        (*xs, *near, w_out, onehot, kaug, b_query, b_value, b_out),
        scratch=[buf((tok, width))] * 4
        + [buf((tok, width), F32), buf((tok, LANES), F32), buf((tok, LANES))]
        + [buf((width, width)), buf((PART, tok), F32), sems(15)],
        name="attend",
        mib=20,
        far_in=(7,),
        far_out=range(7),
    )

    halves = 2 if fast else 1
    lay = (n, halves, rs)
    wire_d = shape((halves, n, rs // halves, ff // 2))
    steps = ff // width
    *outs, gp, d_send, d_keep, pool, r2, vec_b = line.call(
        functools.partial(ffn_kernel, lay),
        [shape((piece, width))] * 4
        + [shape((tok, ff)), wire_d, wire_d, shape((16, width), F32), sqf, shape((8, width), F32)],
        (
            info, n1, gain_attn, shift_attn, b_down, gain_ffn, shift_ffn, w_up, b_up, w_down, *gs, onehot, onehot_t, gpl,
        ),
        scalars=(0,),
        scratch=[
            buf((tok, width)), buf((tok, width), F32), buf((tok, ff)), buf((width, tok)), buf((ff, width)),
            buf((1, ff), F32), buf((tok, width), F32), buf((tok, width)), buf((tok, width)), buf((tok, width)),
            sems(steps),
        ],
        name="ffn",
        mib=24,
        far_in=(9,),
    )

    pp_core = lambda a: lax.ppermute(a, "seq", xor[1])
    pp_y = lambda a: lax.ppermute(a, "seq", xor[2])

    def pp_dp(bit):
        return lambda a: lax.ppermute(a, "dp", [(i, i ^ bit) for i in range(n_dp)])

    pp_x, pp_z1, pp_z2 = pp_dp(1), pp_dp(2), pp_dp(4)

    def join_rows(parts):
        return parts[0] if len(parts) == 1 else jnp.concatenate(parts, axis=-2)

    class Sum:
        def __init__(self, name, got, kept, cuts_a, cuts_b):
            self.name, self.got, self.kept = name, got, kept
            self.cuts = cuts_a, cuts_b

        def run(self, kernel, outs, args, scalars=()):
            name = self.name + kernel_name(kernel)
            return line.call(
                kernel, [shape(o) for o in outs], args, scalars=scalars, name=name, mib=16, us=COSTS.get(name, 0.3)
            )

        def one(self):
            a, b = (sum(r1 - r0 for _, ((r0, r1), _) in cut) for cut in self.cuts)
            c = self.cuts[0][0][1][1]
            c = c[1] - c[0]
            sa, sb, ka, kb = self.run(
                functools.partial(one_kernel, *self.cuts, len(self.got)),
                [(2, 4, a, c), (8, b, c), (2, 4, a, c), (8, b, c)],
                (*self.got, *self.kept),
            )
            self.got, self.kept = (pp_x(sa), pp_y(sb)), (ka, kb)
            self.dims = a, b, c

        def two(self):
            a, b, c = self.dims
            sa, sb, ka, kb = self.run(two_kernel, [(4, a, c), (4, b, c)] * 2, (*self.got, *self.kept))
            self.got, self.kept = (pp_y(sa), pp_x(sb)), (ka, kb)

        def two_with_out(self, got, kept, split):
            a, b, c = self.dims
            m = kept.shape[2]
            rest = m - split
            sa, sb, ka, kb, kx, ky = self.run(
                functools.partial(two_with_out_kernel, split),
                [(4, a + 2 * rest, c), (4, b + 2 * split, c), (4, a, c), (4, b, c), (2, 4, split, c), (8, rest, c)],
                (*self.got, *self.kept, got, kept),
            )
            self.got, self.kept = (pp_y(sa), pp_x(sb)), (ka, kb)
            return self.got[1], self.got[0], kx, ky

        def two_from_out(self, gx, gy, kx, ky):
            a, b, c = self.dims
            a, b = a + kx.shape[2], b + ky.shape[1]
            self.dims = a, b, c
            sa, sb, ka, kb = self.run(
                two_from_out_kernel, [(4, a, c), (4, b, c)] * 2, (*self.got, *self.kept, gx, gy, kx, ky)
            )
            self.got, self.kept = (pp_y(sa), pp_x(sb)), (ka, kb)

        def three(self):
            a, b, c = self.dims
            send, keep = self.run(three_kernel, [(2, a + b, c)] * 2, (*self.got, *self.kept))
            self.got, self.kept = pp_z1(send), keep

        def four(self):
            a, b, c = self.dims
            send, keep = self.run(four_kernel, [(a + b, c)] * 2, (self.got, self.kept))
            self.got, self.kept = pp_z2(send), keep

        def five(self):
            a, b, c = self.dims
            (mine,) = self.run(five_kernel, [(a + b, c)], (self.got, self.kept))
            self.got, self.kept = pp_y(mine), mine

        def five_all(self):
            (mine,) = self.run(five_kernel, [(self.dims[0] + self.dims[1], self.dims[2])], (self.got, self.kept))
            self.kept, self.got = mine, [pp_y(mine), pp_core(mine), lax.ppermute(mine, "seq", xor[3])]

        def six(self):
            a, b, c = self.dims
            (both,) = self.run(six_kernel, [(2, a + b, c)], (info, self.kept, self.got), scalars=(0,))
            self.got, self.kept = pp_core(both), both

        def end(self, kernel, outs):
            return line.call(
                kernel, outs, (info, self.kept, *(self.got if isinstance(self.got, list) else [self.got])), scalars=(0,),
                name=self.name + "end", mib=16,
            )

    wire_u = shape((halves, n, half // halves, ff // n))
    if fast:
        d_got = pp_core(d_send)
    u_send, u_keep, bup, gpre = line.call(
        functools.partial(ffn_back_kernel, lay),
        [wire_u, wire_u, shape((8, ff), F32), shape((tok, ff))],
        (info, r2, gp, w_down, n1, gain_attn, shift_attn),
        scalars=(0,),
        scratch=[buf((tok, width)), buf((width, tok))],
        name="ffn_back",
        mib=12,
    )
    if fast:
        u_got = pp_core(u_send)
        c, m = ff // 4, rs // 2
        down = Sum("down_", [d_got], [d_keep], [(0, ((0, m), (0, c)))], [(0, ((0, m), (c, 2 * c)))])
        down.one()
    wire_o = shape((halves, n, rs // halves, half))
    r1, gatt, gaug, vec_c, o_send, o_keep = line.call(
        functools.partial(norm_back_kernel, lay),
        [sqf, sq, shape((tok, LANES)), shape((8, width), F32), wire_o, wire_o],
        (info, r2, gpre, w_up, n1, inv, gain_attn, w_out, att),
        scalars=(0,),
        scratch=[buf((width, tok)), buf((tok, width), F32)] + [buf((tok, width))] * 3,
        name="norm_back",
        mib=14,
    )
    if fast:
        o_got = pp_core(o_send)
        m = half // 2
        up = Sum("up_", [u_got], [u_keep], [(0, ((0, m // 2), (0, half)))], [(0, ((m // 2, m), (0, half)))])
        up.one()

    gq, gk, gv, gqt, gkt, gvt, vec_d = line.call(
        attend_back_kernel,
        [sq] * 3 + [shape((width, tok))] * 3 + [shape((8, width), F32)],
        (q, k, v, gatt, qaug, kaug, gaug),
        name="attend_back",
        mib=10,
    )
    vecs = jnp.concatenate([vec_d[:2], vec_c[:3], vec_b[:3]], axis=0)
    if fast:
        down.two()
    rows_a, rows_b = (80, 80) if fast else (2 * width, width)
    wire_a, wire_b = shape((halves, n, rows_a, half)), shape((halves, n, rows_b, half))
    qa_send, qb_send, qa_keep, qb_keep = line.call(
        functools.partial(weights_back_kernel, lay),
        [wire_a, wire_b, wire_a, wire_b],
        (info, gqt, gkt, gvt, x, vecs, bup),
        scalars=(0,),
        name="weights_back",
        mib=16,
    )

    def send_back():
        ins = line.call(
            input_back_kernel, [shape((piece, width))] * 4, (gq, gk, gv, r1, w_query, w_key, w_value),
            name="input_back", mib=16,
        )
        packs = line.call(
            pack_kernel, [shape((2 * piece + 2 * SEGS, width))] * n_seq, (*outs, *ins, pool), name="pack"
        )
        return [packs[0]] + [lax.ppermute(packs[r], "seq", xor[r]) for r in range(1, n_seq)]

    def take_back(packs):
        return line.call(
            unpack_kernel,
            [shape((rows, piece, width)), shape((rows, piece, width)), shape((rows, SEGS, width), F32)],
            (info, row_lengths, *packs),
            scalars=(0,),
            name="unpack",
            us=1.0,
        )

    if fast:
        qkv = Sum(
            "qkv_", [pp_core(qa_send), pp_core(qb_send)], [qa_keep, qb_keep],
            [(0, ((0, 80), (0, half)))],
            [(1, ((0, 80), (0, half)))],
        )
        f32 = lambda *d: shape(d, F32)
        out_sum = up.two_with_out(o_got, o_keep, 32)
        down.three()
        qkv.one()
        packs = send_back()
        up.three()
        down.four()
        qkv.two_from_out(*out_sum)
        up.four()
        down.five()
        down.six()
        qkv.three()
        up.five()
        up.six()
        qkv.four()
        (g_down,) = down.end(down_kernel, [f32(rs, ff)])
        (g_up,) = up.end(up_kernel, [f32(width, ff // n)])
        qkv.five_all()
        output, grad_tokens, pooled = take_back(packs)
        *g_qkv, g_out, v0, v1, v2, v3, v4, v5, v6, v7, v8 = qkv.end(
            qkv_kernel, [f32(rs, width)] * 4 + [f32(rs)] * 8 + [f32(4 * rs)]
        )
        g_down, g_out, g_qkv = g_down.T, g_out.T, [g.T for g in g_qkv]
        small = [v0, v1, v2, v3, v4, v5, v6, v7, v8]
    else:
        output, grad_tokens, pooled = take_back(send_back())

        def total(send, keep, dim):
            h = keep.astype(F32) + pp_core(send).astype(F32)
            h = h + pp_y(h.astype(BF)).astype(F32)
            return lax.psum_scatter(h, "dp", scatter_dimension=dim, tiled=True).astype(BF)

        def whole(send, keep, dim, along):
            mine = total(send, keep, dim)
            other = pp_core(mine)
            lo, hi = jnp.where(core == 0, mine, other), jnp.where(core == 0, other, mine)
            return jnp.concatenate([lo, hi], axis=along).astype(F32)

        g_down = whole(d_send[0, 0], d_keep[0, 0], 0, 1).T
        g_up = whole(u_send[0, 0], u_keep[0, 0], 1, 0)
        g_out = whole(o_send[0, 0], o_keep[0, 0], 0, 1).T
        g_qkv = [
            whole(send, keep, 0, 1).T
            for send, keep in (
                (qa_send[0, 0, :width], qa_keep[0, 0, :width]),
                (qa_send[0, 0, width:], qa_keep[0, 0, width:]),
                (qb_send[0, 0], qb_keep[0, 0]),
            )
        ]
        flat = lax.psum(jnp.concatenate([vecs.reshape(-1), bup[0]]), ("dp", "seq"))
        mine = width // n_dp
        small = [
            lax.dynamic_slice_in_dim(flat, i * width + dp * mine, mine) for i in range(8)
        ] + [lax.dynamic_slice_in_dim(flat, 8 * width + dp * 4 * mine, 4 * mine)]

    bq, bv, b_o, gain1, shift1, b_d, gain2, shift2, b_u = small
    return (
        output, pooled, grad_tokens, g_qkv[0], bq, g_qkv[1], g_qkv[2], bv, g_out, b_o, gain1, shift1,
        g_up, b_u, g_down, b_d, gain2, shift2,
    )


def solution(mesh):
    rows = P("dp", "seq", None)
    placed = (rows, P("dp", None)) + (P(),) * 15 + (rows, P("dp", None, None))
    col, one = P(None, "dp"), P("dp")
    return jax.shard_map(
        functools.partial(local, mesh.shape["dp"], mesh.shape["seq"]),
        mesh=mesh,
        in_specs=placed,
        out_specs=(
            rows, P("dp", None, None), rows, col, one, col, col, one, col, one, one, one,
            col, one, col, one, one, one,
        ),
        check_vma=False,
    )
```

```python
import functools

import jax
import jax.numpy as jnp
from jax import lax
from jax.experimental import pallas as pl
from jax.experimental.pallas import tpu as pltpu
from jax.sharding import PartitionSpec as P

HD = 64
SEGS = 8
BF = jnp.bfloat16
F32 = jnp.float32
EPS = 1e-06
NEG = -1e30
LANES = 128

PART = 16
ROWS = 32


def nn(a, b):
    return jnp.dot(a, b, preferred_element_type=F32)


def nt(a, b):
    return lax.dot_general(a, b, (((1,), (1,)), ((), ())), preferred_element_type=F32)


def three_parts(v):
    hi = v.astype(BF)
    rest = v - hi.astype(F32)
    mid = rest.astype(BF)
    low = (rest - mid.astype(F32)).astype(BF)
    return hi, mid, low


def two_parts(v):
    hi = v.astype(BF)
    return hi, (v - hi.astype(F32)).astype(BF)


def norm(value):
    centre = value - jnp.mean(value, axis=-1, keepdims=True)
    inverse = lax.rsqrt(jnp.mean(centre * centre, axis=-1, keepdims=True) + EPS)
    return centre * inverse, inverse


def norm_back(grad, normed, inverse):
    a = jnp.mean(grad, axis=-1, keepdims=True)
    b = jnp.mean(grad * normed, axis=-1, keepdims=True)
    return (grad - a - normed * b) * inverse


def gelu_both(x):
    phi = 0.5 + 0.5 * lax.erf(x * (0.5**0.5))
    density = 0.3989422804014327 * jnp.exp(x * x * -0.5)
    return x * phi, phi + x * density


def row(ref):
    return ref[...].astype(F32).reshape(1, ref.shape[0])


def fold(v):
    out = v[:8]
    for i in range(8, v.shape[0], 8):
        out += v[i : i + 8]
    return out


def total(v):
    return jnp.sum(v, axis=0, keepdims=True)


def head_lane(h):
    lane = lax.broadcasted_iota(jnp.int32, (1, LANES), 1)
    return (lane % PART == h) & (lane >= PART) & (lane < 4 * PART)


def put_rows(out_ref, lead, y, rows, halves, cols, value):
    n = value.shape[0] // halves
    for a in range(halves):
        side = jnp.where(y == a, 0, 1) if halves > 1 else 0
        out_ref[side, lead, pl.ds(rows, n), cols] = value[a * n : (a + 1) * n].astype(BF)


def put_shards(out_ref, info, lay, cols, value, rows=0, first=0):
    n, halves, rs = lay
    count = value.shape[0] // rs
    for i in range(count):
        lead = info[first * count + i] if n > 1 else 0
        put_rows(out_ref, lead, info[9], rows, halves, cols, value[i * rs : (i + 1) * rs])


def copies(pairs, sems, first=0):
    out = []
    for i, (src, dst) in enumerate(pairs):
        out.append(pltpu.make_async_copy(src, dst, sems.at[first + i]))
        out[-1].start()
    return out


def wait(moves):
    for m in moves:
        m.wait()


def split_kernel(info, x_ref, *refs):
    outs, sems = refs[:-1], refs[-1]
    wait(copies([(x_ref.at[info[10] ^ r], outs[r]) for r in range(len(outs))], sems))


def fetch_kernel(a, b, c, x, y, z, sems):
    wait(copies([(a, x), (b, y), (c, z)], sems))


def pack_kernel(o0, o1, o2, o3, i0, i1, i2, i3, pool, p0, p1, p2, p3):
    n = o0.shape[0]
    hi, low = two_parts(pool[:SEGS, :])
    for p, o, i in ((p0, o0, i0), (p1, o1, i1), (p2, o2, i2), (p3, o3, i3)):
        p[:n, :] = o[...]
        p[n : 2 * n, :] = i[...]
        p[2 * n : 2 * n + SEGS, :] = hi
        p[2 * n + SEGS :, :] = low


def unpack_kernel(info, lengths, p0, p1, p2, p3, out, grad, pool):
    me = info[10]
    n = out.shape[1]
    for r, p in enumerate((p0, p1, p2, p3)):
        out[me ^ r] = p[:n, :]
        grad[me ^ r] = p[n : 2 * n, :]
        sums = p[2 * n :, :].astype(F32)
        pool[me ^ r] = (sums[:SEGS] + sums[SEGS:]) / lengths[me ^ r][:, :1]


def attend_kernel(
    x0, x1, x2, x3, wq, wk, wv, wo_h, oh_ref, ka_ref, bq_ref, bv_ref, bo_ref,
    x_h, q_h, k_h, v_h, att_h, inv_h, qa_h, n1_out,
    x_out, q_out, k_out, v_out, att_out, inv_out, qa_out, wo, stat, sems,
):
    n = x0.shape[0]
    bq, bv, bo = row(bq_ref), row(bv_ref), row(bo_ref)
    last = copies([(wo_h, wo)], sems, 4)
    for r, ref in enumerate((x0, x1, x2, x3)):
        x_out[r * n : (r + 1) * n] = ref[...]
    outs = copies([(x_out, x_h)], sems, 8)
    x = x_out[...]
    q_out[...] = ((nn(x, wq[...]) + bq).astype(BF).astype(F32) * (HD**-0.5)).astype(BF)
    outs += copies([(q_out, q_h)], sems, 9)
    k_out[...] = nn(x, wk[...]).astype(BF)
    outs += copies([(k_out, k_h)], sems, 10)
    v_out[...] = (nn(x, wv[...]) + bv).astype(BF)
    outs += copies([(v_out, v_h)], sems, 11)
    tok, width = x.shape
    stat[...] = jnp.zeros_like(stat)
    ones = jnp.ones((16, tok), BF)

    def pair(p, carry):
        sl = pl.ds(pl.multiple_of(p * LANES, LANES), LANES)
        qcat = jnp.concatenate([q_out[:, sl], oh_ref[...]], axis=1)
        kp = k_out[:, sl]
        vt = v_out[:, sl].T
        lane = lax.broadcasted_iota(jnp.int32, (1, LANES), 1)
        parts = []
        for h in range(2):
            kh = jnp.where((lane < HD) == (h == 0), kp, jnp.zeros_like(kp))
            st = nt(jnp.concatenate([kh, ka_ref[...]], axis=1), qcat)
            m = jnp.max(st, axis=0, keepdims=True)
            pb = jnp.exp(st - m).astype(BF)
            ot = nn(jnp.concatenate([vt[h * HD : (h + 1) * HD], ones], axis=0), pb)
            total = ot[HD : HD + 1]
            stat[pl.ds(2 * p + h, 1), :] = m + jnp.log(total)
            parts.append(ot[:HD] / total)
        att_out[:, sl] = jnp.concatenate(parts, axis=0).T
        return carry

    lax.fori_loop(0, width // LANES, pair, 0, unroll=3)
    outs += copies([(att_out, att_h)], sems, 12)
    hi, mid, low = three_parts(stat[...])
    zero = jnp.zeros((PART, tok), BF)
    qa_out[...] = jnp.concatenate([zero, hi, mid, low, zero, zero, zero, zero], axis=0).T + oh_ref[...]
    outs += copies([(qa_out, qa_h)], sems, 13)
    wait(last)
    n1_out[...] = nn(att_out[...].astype(BF), wo[...])
    for at in range(0, tok, ROWS):
        rows = slice(at, at + ROWS)
        n1, inv = norm(x_out[rows, :].astype(F32) + (n1_out[rows, :] + bo))
        n1_out[rows, :] = n1
        inv_out[rows, :] = jnp.broadcast_to(inv, (ROWS, LANES))
    outs += copies([(inv_out, inv_h)], sems, 14)
    wait(outs)


def ffn_kernel(
    lay, info, n1_ref, ga_ref, sa_ref, bd_ref, gf_ref, sf_ref, wu, bu_ref, wd_h, g0, g1, g2, g3, oh_ref, oht_ref, gpl,
    o0, o1, o2, o3, gp_out, send, keep, pool_out, r2_out, vec_out,
    hl, acc, act, gt, wd, bu, gsum, hi, low, gl, sem_w,
):
    n = g0.shape[0]
    ga, sa, bd, gf, sf = row(ga_ref), row(sa_ref), row(bd_ref), row(gf_ref), row(sf_ref)
    bu[...] = row(bu_ref)
    tok, width = acc.shape
    ff = act.shape[1]
    tile = width
    steps = ff // tile

    def weights(t):
        rows = pl.ds(pl.multiple_of(t * tile, tile), tile)
        return pltpu.make_async_copy(wd_h.at[rows, :], wd.at[rows, :], sem_w.at[t])

    for t in range(steps):
        weights(t).start()
    hl[...] = (n1_ref[...] * ga + sa).astype(BF)
    acc[...] = jnp.zeros_like(acc)

    def step(t, carry):
        cols = pl.ds(pl.multiple_of(t * tile, tile), tile)
        weights(t).wait()
        for r in range(2):
            rows = pl.ds(r * 2 * n, 2 * n)
            a, d = gelu_both(nn(hl[rows, :], wu[:, cols]) + bu[:, cols])
            ab = a.astype(BF)
            act[rows, cols] = ab
            gp_out[rows, cols] = d.astype(BF)
            acc[rows, :] += nn(ab, wd[cols, :])
        return carry

    lax.fori_loop(0, steps, step, 0)
    oh = oh_ref[...]
    gsum[...] = nn(jnp.concatenate([oh, oh], axis=1), gpl[...])
    gain, shift, bias = (jnp.zeros((8, width), F32) for _ in range(3))
    gs, os = (g0, g1, g2, g3), (o0, o1, o2, o3)
    for at in range(0, tok, ROWS):
        rows = slice(at, at + ROWS)
        r, of = at // n, slice(at % n, at % n + ROWS)
        hidden = n1_ref[rows, :] * ga + sa
        n2, inv = norm(hidden + (acc[rows, :] + bd))
        result = n2 * gf + sf
        os[r][of, :] = result.astype(BF)
        hi[rows, :], low[rows, :] = two_parts(result)
        gout = gs[r][of, :].astype(F32) + gsum[rows, :]
        gain += fold(gout * n2)
        shift += fold(gout)
        gr2 = norm_back(gout * gf, n2, inv)
        r2_out[rows, :] = gr2
        low_g = gr2.astype(BF)
        bias += fold(low_g.astype(F32))
        gl[rows, :] = low_g
    gt[...] = gl[...].T
    pool_out[...] = nn(oht_ref[...], hi[...]) + nn(oht_ref[...], low[...])
    vec_out[...] = jnp.concatenate([total(v) for v in (bias, gain, shift)] + [jnp.zeros((5, width), F32)], axis=0)
    half = ff // 2
    part = 768

    def piece(i, carry):
        for rc, ref in ((1, send), (0, keep)):
            at = (info[8] ^ rc) * half + i * part
            res = nn(gt[...], act[:, pl.ds(pl.multiple_of(at, part), part)])
            put_shards(ref, info, lay, pl.ds(pl.multiple_of(i * part, part), part), res)
        return carry

    lax.fori_loop(0, half // part, piece, 0, unroll=2)


def ffn_back_kernel(
    lay, info, r2_ref, gp, wd, n1_ref, ga_ref, sa_ref,
    send, keep, bup_out, gpre_out,
    gl, hlt,
):
    ga, sa = row(ga_ref), row(sa_ref)
    width = hlt.shape[0]
    half = width // 2
    ff = gp.shape[1]
    tile = width
    steps = ff // tile

    gl[...] = r2_ref[...].astype(BF)
    hlt[...] = (n1_ref[...] * ga + sa).astype(BF).T
    per = 2 if lay[0] > 1 else 1

    def step(t, carry):
        cols = pl.ds(pl.multiple_of(t * tile, tile), tile)
        gpre = (nt(gl[...], wd[cols, :]) * gp[:, cols].astype(F32)).astype(BF)
        gpre_out[:, cols] = gpre
        bup_out[:, cols] = jnp.broadcast_to(
            jnp.sum(gpre.astype(F32), axis=0, keepdims=True), (bup_out.shape[0], tile)
        )
        for rc, ref in ((1, send), (0, keep)):
            at = pl.multiple_of((info[8] ^ rc) * half, half)
            res = nn(hlt[pl.ds(at, half), :], gpre)
            for i in range(per):
                if lay[0] > 1:
                    put_rows(ref, info[per * t + i], info[9], 0, lay[1], slice(None), res[:, i * half : (i + 1) * half])
                else:
                    put_rows(ref, 0, info[9], 0, lay[1], cols, res)
        return carry

    lax.fori_loop(0, steps, step, 0, unroll=4)


def norm_back_kernel(
    lay, info, r2_ref, gpre, wu, n1_ref, inv_ref, ga_ref, wo, att,
    r1_out, gatt_out, gaug_out, vec_out, osend, okeep,
    gt, acc, gm, hi, low,
):
    ga = row(ga_ref)
    tok, width = r2_ref.shape
    half = width // 2
    head = lax.broadcasted_iota(jnp.int32, (width, LANES), 0) // HD
    lane = lax.broadcasted_iota(jnp.int32, (width, LANES), 1)
    pick = ((lane % PART == head) & (lane >= PART) & (lane < 4 * PART)).astype(BF)
    lane1 = lax.broadcasted_iota(jnp.int32, (1, LANES), 1)

    def step(t, carry):
        cols = pl.ds(pl.multiple_of(t * width, width), width)
        acc[...] += nt(gpre[:, cols], wu[:, cols])
        return carry

    acc[...] = r2_ref[...]
    lax.fori_loop(0, gpre.shape[1] // width, step, 0)
    gain, shift, bias = (jnp.zeros((8, width), F32) for _ in range(3))
    for at in range(0, tok, ROWS):
        rows = slice(at, at + ROWS)
        gh = acc[rows, :]
        n1 = n1_ref[rows, :]
        gain += fold(gh * n1)
        shift += fold(gh)
        gr1 = norm_back(gh * ga, n1, inv_ref[rows, :1])
        r1_out[rows, :] = gr1
        low_g = gr1.astype(BF)
        bias += fold(low_g.astype(F32))
        gm[rows, :] = low_g
    gt[...] = gm[...].T
    gatt_out[...] = nt(gm[...], wo[...]).astype(BF)
    for at in range(0, tok, ROWS):
        rows = slice(at, at + ROWS)
        hi[rows, :], low[rows, :] = two_parts(gatt_out[rows, :].astype(F32) * att[rows, :])
    a, b, c = three_parts(nn(hi[...], pick) + nn(low[...], pick))
    gaug_out[...] = jnp.where(lane1 < 2 * PART, a, jnp.where(lane1 < 3 * PART, b, c))
    vec_out[...] = jnp.concatenate([total(v) for v in (bias, gain, shift)] + [jnp.zeros((5, width), F32)], axis=0)
    sides = [att[:, pl.ds(pl.multiple_of((info[8] ^ rc) * half, half), half)].astype(BF) for rc in (1, 0)]
    res = nn(gt[...], jnp.concatenate(sides, axis=1))
    put_shards(osend, info, lay, slice(None), res[:, :half])
    put_shards(okeep, info, lay, slice(None), res[:, half:])


def attend_back_kernel(
    q, k, v, g, qa, ka, ga,
    gq, gk, gv, gqt, gkt, gvt, vec_out,
):
    tok, width = q.shape

    def pair(p, carry):
        sl = pl.ds(pl.multiple_of(p * LANES, LANES), LANES)
        qp, kp, vp, gp = q[:, sl], k[:, sl], v[:, sl], g[:, sl]
        qcat = jnp.concatenate([qp, qa[...]], axis=1)
        gcat = jnp.concatenate([gp, ga[...]], axis=1)
        kt = kp.T
        lane = lax.broadcasted_iota(jnp.int32, (1, LANES), 1)
        gkp = jnp.zeros((tok, LANES), F32)
        gvp = jnp.zeros((tok, LANES), F32)
        parts = []
        zero = jnp.zeros_like(kp)
        for h in range(2):
            mine = (lane < HD) == (h == 0)
            pick = head_lane(2 * p + h)
            kaug = jnp.where(pick, -jnp.ones((), BF), ka[...])
            vaug = jnp.where(pick, -jnp.ones((), BF), jnp.zeros((tok, LANES), BF))
            prob = jnp.exp(nt(jnp.concatenate([jnp.where(mine, kp, zero), kaug], axis=1), qcat))
            dp = nt(jnp.concatenate([jnp.where(mine, vp, zero), vaug], axis=1), gcat)
            ds = (prob * dp).astype(BF)
            gvp += nn(prob.astype(BF), jnp.where(mine, gp, zero))
            gkp += nn(ds, jnp.where(mine, qp, zero))
            parts.append(nn(kt[h * HD : (h + 1) * HD], ds))
        gqp = (jnp.concatenate(parts, axis=0) * (HD**-0.5)).astype(BF)
        gqt[sl, :] = gqp
        gq[:, sl] = gqp.T
        gkb, gvb = gkp.astype(BF), gvp.astype(BF)
        gk[:, sl] = gkb
        gv[:, sl] = gvb
        gkt[sl, :] = gkb.T
        gvt[sl, :] = gvb.T
        return carry

    lax.fori_loop(0, width // LANES, pair, 0, unroll=2)
    bq = jnp.sum(gq[...].astype(F32), axis=0, keepdims=True)
    bv = jnp.sum(gv[...].astype(F32), axis=0, keepdims=True)
    vec_out[...] = jnp.concatenate([bq, bv, jnp.zeros((6, width), F32)], axis=0)


def weights_back_kernel(lay, info, gqt, gkt, gvt, x_ref, vecs, bups, osend, okeep, send_a, send_b, keep_a, keep_b):
    width = x_ref.shape[1]
    n, halves, rs = lay
    half = width // 2
    sides = [x_ref[:, pl.ds(pl.multiple_of((info[8] ^ rc) * half, half), half)] for rc in (1, 0)]
    right = jnp.concatenate(sides, axis=1)
    wires = ((1, (send_a, send_b)), (0, (keep_a, keep_b)))
    for m, left in enumerate((gqt, gkt, gvt)):
        both = nn(left[...], right)
        for rc, (wa, wb) in wires:
            res = both[:, :half] if rc else both[:, half:]
            if n > 1:
                for j in range(n):
                    rows = res[j * rs : (j + 1) * rs]
                    put = functools.partial(put_rows, lead=info[j], y=info[9], halves=halves, cols=slice(None))
                    if m == 0:
                        put(wa, rows=0, value=rows)
                    elif m == 1:
                        put(wa, rows=48, value=rows[:32])
                        put(wb, rows=48, value=rows[32:])
                    else:
                        put(wb, rows=0, value=rows)
            elif m < 2:
                wa[0, 0, pl.ds(m * width, width), :] = res.astype(BF)
            else:
                wb[0, 0] = res.astype(BF)
    if n > 1:
        for o, (wa, wb) in ((osend, (send_a, send_b)), (okeep, (keep_a, keep_b))):
            wa[:, :, 80:, :] = o[:, :, :16, :]
            wb[:, :, 80:, :] = o[:, :, 16:, :]
        for j in range(n):
            bup = bups[:1, j * 4 * rs : (j + 1) * 4 * rs]
            block = jnp.concatenate(
                [vecs[:, j * rs : (j + 1) * rs], jnp.zeros((8, rs), F32)]
                + [bup[:, c * rs : (c + 1) * rs] for c in range(4)]
                + [jnp.zeros((12, rs), F32)],
                axis=0,
            )
            block = jnp.concatenate([block, jnp.zeros((32, half - rs), F32)], axis=1)
            for rc, (wa, _) in wires:
                mine = jnp.where((info[8] ^ rc) == 0, 1.0, 0.0)
                put_rows(wa, info[j], info[9], 64, halves, slice(None), block * mine)


def input_back_kernel(gq, gk, gv, r1, wq, wk, wv, o0, o1, o2, o3):
    whole = r1[...] + nt(gq[...], wq[...]) + nt(gk[...], wk[...]) + nt(gv[...], wv[...])
    for r, o in enumerate((o0, o1, o2, o3)):
        c = o.shape[0]
        o[...] = whole[r * c : (r + 1) * c].astype(BF)


WHOLE = pl.BlockSpec(memory_space=pltpu.VMEM)
SCALARS = pl.BlockSpec(memory_space=pltpu.SMEM)
FAR = pl.BlockSpec(memory_space=pltpu.HBM)


def shape(dims, dtype=BF):
    return jax.ShapeDtypeStruct(tuple(dims), dtype)


def buf(dims, dtype=BF):
    return pltpu.VMEM(tuple(dims), dtype)


def sems(count):
    return pltpu.SemaphoreType.DMA((count,))


def params(mib):
    return pltpu.CompilerParams(vmem_limit_bytes=mib * 1024 * 1024)


def cost(us):
    return pl.CostEstimate(flops=int(us * 10**9) + 1, bytes_accessed=1, transcendentals=0)


COSTS = {'down_one': 0.1, 'up_one': 0.1, 'down_two': 0.1, 'up_two': 1.0, 'down_three': 14.0, 'qkv_one': 0.1, 'up_three': 3.0, 'down_four': 1.0, 'down_end': 0.02, 'up_end': 0.02}


class Line:
    def __init__(self):
        self.token = None

    def call(self, kernel, outs, args, scalars=(), scratch=(), name=None, mib=8, far_in=(), far_out=(), us=0.0):
        args = [pltpu.with_memory_space_constraint(a, pltpu.HBM) if i in far_in else a for i, a in enumerate(args)]
        ins = [SCALARS if i in scalars else FAR if i in far_in else WHOLE for i in range(len(args))]
        to = [FAR if i in far_out else WHOLE for i in range(len(outs))]
        outs = [pltpu.HBM(o.shape, o.dtype) if i in far_out else o for i, o in enumerate(outs)]
        tokens = [] if self.token is None else [self.token]
        n_in, n_tok, n_out = len(args), len(tokens), len(outs)

        def body(*refs):
            left, right = refs[:n_in], refs[n_in + n_tok :]
            kernel(*left, *right[:n_out], *right[n_out + 1 :])
            right[n_out][...] = jnp.zeros((8, LANES), F32)

        *got, self.token = pl.pallas_call(
            body,
            out_shape=[*outs, shape((8, LANES), F32)],
            in_specs=ins + [WHOLE] * n_tok,
            out_specs=[*to, WHOLE],
            scratch_shapes=list(scratch),
            compiler_params=params(mib),
            cost_estimate=cost(us),
            name=name,
        )(*args, *tokens)
        return got


def plus(a, b):
    return (a.astype(F32) + b.astype(F32)).astype(BF)


def half_of(ref, axis, side, rows, cols):
    lead = [slice(None)] * (len(ref.shape) - 2)
    lead[axis] = side
    return ref[(*lead, slice(*rows), slice(*cols))]


def split_sum_kernel(parts, n_got, n_kept, n_send, *refs):
    got, kept, out = refs[:n_got], refs[n_got : n_got + n_kept], refs[n_got + n_kept :]
    for axis, spans, (send, send_at), (keep, keep_at) in parts:
        done = 0
        for g, g_rows, g_cols, k, k_rows, k_cols in spans:
            m = g_rows[1] - g_rows[0]
            for side, ref, at in ((1, out[send], send_at), (0, out[n_send + keep], keep_at)):
                lead = [slice(None)] * (len(ref.shape) - 2)
                ref[(*lead, slice(at + done, at + done + m), slice(None))] = plus(
                    half_of(got[g], axis, side, g_rows, g_cols), half_of(kept[k], axis, side, k_rows, k_cols)
                )
            done += m


def five_kernel(got, kept, mine):
    mine[...] = plus(got[...], kept[...])


def six_kernel(info, mine, other, both):
    both[info[9]] = mine[...]
    both[1 - info[9]] = other[...]


def down_kernel(info, mine, other, out):
    m = mine.shape[1] // 3
    cols = mine.shape[2]
    for rc, ref in ((0, mine), (1, other)):
        for p in range(3):
            block = jnp.concatenate([ref[0, p * m : (p + 1) * m], ref[1, p * m : (p + 1) * m]], axis=0)
            at = (info[8] ^ rc) * 3 * cols + p * cols
            out[:, pl.ds(pl.multiple_of(at, cols), cols)] = block.astype(F32)


def up_kernel(info, mine, other, out):
    half = out.shape[0] // 2
    m = half // 2
    for rc, ref in ((0, mine), (1, other)):
        for a in range(2):
            at = (info[8] ^ rc) * half + a * m
            out[pl.ds(pl.multiple_of(at, m), m), :] = ref[a].astype(F32)


def qkv_kernel(info, here, over_y, over_core, over_both, gq, gk, gv, go, *vecs):
    half = gq.shape[1] // 2
    y0 = info[9] == 0
    mine, other = (
        [jnp.where(y0, a[...], b[...]), jnp.where(y0, b[...], a[...])] for a, b in ((here, over_y), (over_core, over_both))
    )
    for rc, ref in ((0, mine), (1, other)):
        at = pl.ds(pl.multiple_of((info[8] ^ rc) * half, half), half)

        def put(out, *spans):
            parts = [ref[a][i : i + m] for a, i, m in spans]
            out[:, at] = jnp.concatenate(parts, axis=0).astype(F32)

        put(gq, (0, 0, 48), (1, 0, 48))
        put(gk, (0, 48, 16), (1, 48, 16), (0, 144, 32), (1, 144, 32))
        put(gv, (0, 96, 48), (1, 96, 48))
        put(go, (0, 80, 16), (0, 176, 32), (1, 80, 16), (1, 176, 32))
    rs = vecs[0].shape[0]
    low = [jnp.where(info[8] == 0, m[64:80].astype(F32), o[64:80].astype(F32)) for m, o in zip(mine, other)]
    for i, out in enumerate(vecs[:8]):
        out[...] = low[0][i, :rs]
    for c in range(4):
        vecs[8][pl.ds(c * rs, rs)] = low[1][c, :rs]


def local(n_dp, n_seq, *args):
    (
        tokens, seg_lengths, w_query, b_query, w_key, w_value, b_value, w_out, b_out,
        gain_attn, shift_attn, w_up, b_up, w_down, b_down, gain_ffn, shift_ffn,
        grad_output, grad_pooled,
    ) = args
    line = Line()
    me = lax.axis_index("seq")
    dp = lax.axis_index("dp")
    core, y = me % 2, me // 2
    rows, piece, width = tokens.shape
    tok = n_seq * piece
    ff = w_up.shape[1]
    fast = n_dp == 8
    n = n_dp if fast else 1
    rs = width // n
    half = width // 2
    xor = [[(i, i ^ r) for i in range(n_seq)] for r in range(n_seq)]

    if fast:
        j = jnp.arange(8, dtype=jnp.int32) ^ dp
        pos = (j % 2) * 4 + (j // 2 % 2) * 2 + j // 4
    else:
        pos = jnp.zeros((8,), jnp.int32)
    info = jnp.concatenate([pos, jnp.stack([core, y, me]), jnp.zeros((5,), jnp.int32)]).astype(jnp.int32)

    def rel(a, name):
        parts = line.call(
            split_kernel, [shape((piece, width))] * n_seq, (info, a), scalars=(0,), scratch=[sems(n_seq)],
            name=name, far_in=(1,),
        )
        return [parts[0]] + [lax.ppermute(parts[r], "seq", xor[r]) for r in range(1, n_seq)]

    xs = rel(tokens, "split_tokens")
    gs = rel(grad_output, "split_grads")

    lengths = lax.dynamic_index_in_dim(seg_lengths, me, 0, keepdims=False)
    ends = jnp.cumsum(lengths)
    order = me ^ jnp.arange(n_seq, dtype=jnp.int32)
    places = (order[:, None] * piece + jnp.arange(piece, dtype=jnp.int32)[None, :]).reshape(tok)
    seg = jnp.sum((places[:, None] >= ends[None, :]).astype(jnp.int32), axis=1)
    lane = jnp.arange(LANES, dtype=jnp.int32)
    hot = seg[:, None] == lane[None, :]
    onehot = hot.astype(BF)
    kaug = jnp.where((lane < SEGS)[None, :] & ~hot, NEG, 0.0).astype(BF)
    onehot_t = (seg[None, :] == jnp.arange(16, dtype=jnp.int32)[:, None]).astype(BF)
    length_col = lengths.astype(F32)[:, None]
    gpool = lax.dynamic_index_in_dim(grad_pooled, me, 0, keepdims=False).astype(F32) / length_col
    gp_hi = gpool.astype(BF)
    gp_low = (gpool - gp_hi.astype(F32)).astype(BF)
    zeros = jnp.zeros((LANES - SEGS, width), BF)
    gpl = jnp.concatenate([gp_hi, zeros, gp_low, zeros], axis=0)


    sq = shape((tok, width))
    sqf = shape((tok, width), F32)
    row_lengths = jnp.broadcast_to(seg_lengths.astype(F32)[:, :, None], (rows, SEGS, LANES))
    near = line.call(
        fetch_kernel, [shape((width, width))] * 3, (w_query, w_key, w_value), scratch=[sems(3)], name="fetch",
        far_in=range(3),
    )
    lanes = shape((tok, LANES))
    lanes_f = shape((tok, LANES), F32)
    x, q, k, v, att, inv, qaug, n1 = line.call(
        attend_kernel,
        [sq, sq, sq, sq, sqf, lanes_f, lanes, sqf],
        (*xs, *near, w_out, onehot, kaug, b_query, b_value, b_out),
        scratch=[buf((tok, width))] * 4
        + [buf((tok, width), F32), buf((tok, LANES), F32), buf((tok, LANES))]
        + [buf((width, width)), buf((PART, tok), F32), sems(15)],
        name="attend",
        mib=20,
        far_in=(7,),
        far_out=range(7),
    )

    halves = 2 if fast else 1
    lay = (n, halves, rs)
    wire_d = shape((halves, n, rs // halves, ff // 2))
    steps = ff // width
    *outs, gp, d_send, d_keep, pool, r2, vec_b = line.call(
        functools.partial(ffn_kernel, lay),
        [shape((piece, width))] * 4
        + [shape((tok, ff)), wire_d, wire_d, shape((16, width), F32), sqf, shape((8, width), F32)],
        (
            info, n1, gain_attn, shift_attn, b_down, gain_ffn, shift_ffn, w_up, b_up, w_down, *gs, onehot, onehot_t, gpl,
        ),
        scalars=(0,),
        scratch=[
            buf((tok, width)), buf((tok, width), F32), buf((tok, ff)), buf((width, tok)), buf((ff, width)),
            buf((1, ff), F32), buf((tok, width), F32), buf((tok, width)), buf((tok, width)), buf((tok, width)),
            sems(steps),
        ],
        name="ffn",
        mib=24,
        far_in=(9,),
    )

    pp_core = lambda a: lax.ppermute(a, "seq", xor[1])
    pp_y = lambda a: lax.ppermute(a, "seq", xor[2])

    def pp_dp(bit):
        return lambda a: lax.ppermute(a, "dp", [(i, i ^ bit) for i in range(n_dp)])

    pp_x, pp_z1, pp_z2 = pp_dp(1), pp_dp(2), pp_dp(4)

    def join_rows(parts):
        return parts[0] if len(parts) == 1 else jnp.concatenate(parts, axis=-2)

    send_along = {"x": pp_x, "y": pp_y, "z": pp_z1, "w": pp_z2}

    class Sum:
        def __init__(self, name, got, kept, parts):
            sides = lambda w: w.reshape(2, 2, 2, 2, *w.shape[2:])
            self.name = name
            self.got, self.kept = [sides(w) for w in got], [sides(w) for w in kept]
            self.spans = [[(i, r, c, i, r, c) for i, r, c in spans] for spans in parts]
            self.rows = [sum(r[1] - r[0] for _, r, _ in spans) for spans in parts]
            self.cols = parts[0][0][2][1] - parts[0][0][2][0]
            self.whole = sum(self.rows), self.cols
            self.left = ["yxzw"] * len(parts)

        def run(self, step, kernel, outs, args, scalars=()):
            name = self.name + step
            return line.call(
                kernel, [shape(o) for o in outs], args, scalars=scalars, name=name, mib=16, us=COSTS.get(name, 0.3)
            )

        def split(self, step, along):
            ways, last = list(dict.fromkeys(along)), along[0] == "w"
            height, kept_height, parts = dict.fromkeys(ways, 0), 0, []
            for p, a in enumerate(along):
                keep = (0, kept_height) if last else (p, 0)
                parts.append((self.left[p].index(a), self.spans[p], (ways.index(a), height[a]), keep))
                self.left[p] = self.left[p].replace(a, "")
                height[a] += self.rows[p]
                kept_height += self.rows[p]
            lead = (2,) * len(self.left[0])
            keeps = [sum(self.rows)] if last else self.rows
            out = self.run(
                step,
                functools.partial(split_sum_kernel, parts, len(self.got), len(self.kept), len(ways)),
                [(*lead, m, self.cols) for m in [*height.values(), *keeps]],
                (*self.got, *self.kept),
            )
            self.got = [send_along[a](w) for a, w in zip(ways, out[: len(ways)])]
            self.kept = out[len(ways) :]
            self.spans = [
                [(i, (at, at + m), (0, self.cols), k, (k_at, k_at + m), (0, self.cols))]
                for m, (_, _, (i, at), (k, k_at)) in zip(self.rows, parts)
            ]

        def one(self):
            self.split("one", "xyz"[: len(self.rows)])

        def two(self):
            self.split("two", "yxx"[: len(self.rows)])

        def three(self):
            self.split("three", "zzy"[: len(self.rows)])

        def four(self):
            self.split("four", "www"[: len(self.rows)])

        def mine(self):
            (mine,) = self.run("five", five_kernel, [self.whole], (*self.got, *self.kept))
            return mine

        def five(self):
            mine = self.mine()
            self.got, self.kept = pp_y(mine), mine

        def six(self):
            (both,) = self.run("six", six_kernel, [(2, *self.whole)], (info, self.kept, self.got), scalars=(0,))
            self.got, self.kept = pp_core(both), both

        def five_all(self):
            mine = self.mine()
            self.kept, self.got = mine, [pp_y(mine), pp_core(mine), lax.ppermute(mine, "seq", xor[3])]

        def end(self, kernel, outs):
            return line.call(
                kernel, outs, (info, self.kept, *(self.got if isinstance(self.got, list) else [self.got])), scalars=(0,),
                name=self.name + "end", mib=16,
            )

    wire_u = shape((halves, n, half // halves, ff // n))
    if fast:
        d_got = pp_core(d_send)
    u_send, u_keep, bup, gpre = line.call(
        functools.partial(ffn_back_kernel, lay),
        [wire_u, wire_u, shape((8, ff), F32), shape((tok, ff))],
        (info, r2, gp, w_down, n1, gain_attn, shift_attn),
        scalars=(0,),
        scratch=[buf((tok, width)), buf((width, tok))],
        name="ffn_back",
        mib=12,
    )
    if fast:
        u_got = pp_core(u_send)
        c, m = ff // 6, rs // 2
        down = Sum("down_", [d_got], [d_keep], [[(0, (0, m), (p * c, (p + 1) * c))] for p in range(3)])
        down.one()
    wire_o = shape((halves, n, rs // halves, half))
    r1, gatt, gaug, vec_c, o_send, o_keep = line.call(
        functools.partial(norm_back_kernel, lay),
        [sqf, sq, shape((tok, LANES)), shape((8, width), F32), wire_o, wire_o],
        (info, r2, gpre, w_up, n1, inv, gain_attn, w_out, att),
        scalars=(0,),
        scratch=[buf((width, tok)), buf((tok, width), F32)] + [buf((tok, width))] * 3,
        name="norm_back",
        mib=14,
    )
    if fast:
        m = half // 4
        up = Sum("up_", [u_got], [u_keep], [[(0, (p * m, (p + 1) * m), (0, half))] for p in range(2)])
        up.one()

    gq, gk, gv, gqt, gkt, gvt, vec_d = line.call(
        attend_back_kernel,
        [sq] * 3 + [shape((width, tok))] * 3 + [shape((8, width), F32)],
        (q, k, v, gatt, qaug, kaug, gaug),
        name="attend_back",
        mib=10,
    )
    vecs = jnp.concatenate([vec_d[:2], vec_c[:3], vec_b[:3]], axis=0)
    if fast:
        down.two()
    rows_a, rows_b = (96, 112) if fast else (2 * width, width)
    wire_a, wire_b = shape((halves, n, rows_a, half)), shape((halves, n, rows_b, half))
    qa_send, qb_send, qa_keep, qb_keep = line.call(
        functools.partial(weights_back_kernel, lay),
        [wire_a, wire_b, wire_a, wire_b],
        (info, gqt, gkt, gvt, x, vecs, bup, o_send, o_keep),
        scalars=(0,),
        name="weights_back",
        mib=16,
    )

    def send_back():
        ins = line.call(
            input_back_kernel, [shape((piece, width))] * 4, (gq, gk, gv, r1, w_query, w_key, w_value),
            name="input_back", mib=16,
        )
        packs = line.call(
            pack_kernel, [shape((2 * piece + 2 * SEGS, width))] * n_seq, (*outs, *ins, pool), name="pack"
        )
        return [packs[0]] + [lax.ppermute(packs[r], "seq", xor[r]) for r in range(1, n_seq)]

    def take_back(packs):
        return line.call(
            unpack_kernel,
            [shape((rows, piece, width)), shape((rows, piece, width)), shape((rows, SEGS, width), F32)],
            (info, row_lengths, *packs),
            scalars=(0,),
            name="unpack",
            us=1.0,
        )

    if fast:
        qkv = Sum(
            "qkv_", [pp_core(qa_send), pp_core(qb_send)], [qa_keep, qb_keep],
            [[(0, (0, rows_a), (0, half))], [(1, (0, rows_b), (0, half))]],
        )
        f32 = lambda *d: shape(d, F32)
        up.two()
        down.three()
        qkv.one()
        packs = send_back()
        down.four()
        up.three()
        qkv.two()
        up.four()
        down.five()
        down.six()
        qkv.three()
        up.five()
        up.six()
        qkv.four()
        (g_down,) = down.end(down_kernel, [f32(rs, ff)])
        (g_up,) = up.end(up_kernel, [f32(width, ff // n)])
        qkv.five_all()
        output, grad_tokens, pooled = take_back(packs)
        *g_qkv, g_out, v0, v1, v2, v3, v4, v5, v6, v7, v8 = qkv.end(
            qkv_kernel, [f32(rs, width)] * 4 + [f32(rs)] * 8 + [f32(4 * rs)]
        )
        g_down, g_out, g_qkv = g_down.T, g_out.T, [g.T for g in g_qkv]
        small = [v0, v1, v2, v3, v4, v5, v6, v7, v8]
    else:
        output, grad_tokens, pooled = take_back(send_back())

        def total(send, keep, dim):
            h = keep.astype(F32) + pp_core(send).astype(F32)
            h = h + pp_y(h.astype(BF)).astype(F32)
            return lax.psum_scatter(h, "dp", scatter_dimension=dim, tiled=True).astype(BF)

        def whole(send, keep, dim, along):
            mine = total(send, keep, dim)
            other = pp_core(mine)
            lo, hi = jnp.where(core == 0, mine, other), jnp.where(core == 0, other, mine)
            return jnp.concatenate([lo, hi], axis=along).astype(F32)

        g_down = whole(d_send[0, 0], d_keep[0, 0], 0, 1).T
        g_up = whole(u_send[0, 0], u_keep[0, 0], 1, 0)
        g_out = whole(o_send[0, 0], o_keep[0, 0], 0, 1).T
        g_qkv = [
            whole(send, keep, 0, 1).T
            for send, keep in (
                (qa_send[0, 0, :width], qa_keep[0, 0, :width]),
                (qa_send[0, 0, width:], qa_keep[0, 0, width:]),
                (qb_send[0, 0], qb_keep[0, 0]),
            )
        ]
        flat = lax.psum(jnp.concatenate([vecs.reshape(-1), bup[0]]), ("dp", "seq"))
        mine = width // n_dp
        small = [
            lax.dynamic_slice_in_dim(flat, i * width + dp * mine, mine) for i in range(8)
        ] + [lax.dynamic_slice_in_dim(flat, 8 * width + dp * 4 * mine, 4 * mine)]

    bq, bv, b_o, gain1, shift1, b_d, gain2, shift2, b_u = small
    return (
        output, pooled, grad_tokens, g_qkv[0], bq, g_qkv[1], g_qkv[2], bv, g_out, b_o, gain1, shift1,
        g_up, b_u, g_down, b_d, gain2, shift2,
    )


def solution(mesh):
    rows = P("dp", "seq", None)
    placed = (rows, P("dp", None)) + (P(),) * 15 + (rows, P("dp", None, None))
    col, one = P(None, "dp"), P("dp")
    return jax.shard_map(
        functools.partial(local, mesh.shape["dp"], mesh.shape["seq"]),
        mesh=mesh,
        in_specs=placed,
        out_specs=(
            rows, P("dp", None, None), rows, col, one, col, col, one, col, one, one, one,
            col, one, col, one, one, one,
        ),
        check_vma=False,
    )
```

```python
import functools

import jax
import jax.numpy as jnp
from jax import lax
from jax.experimental import pallas as pl
from jax.experimental.pallas import tpu as pltpu
from jax.sharding import PartitionSpec as P

HD = 64
SEGS = 8
BF = jnp.bfloat16
F32 = jnp.float32
EPS = 1e-06
NEG = -1e30
LANES = 128

PART = 16
ROWS = 32


def nn(a, b):
    return jnp.dot(a, b, preferred_element_type=F32)


def nt(a, b):
    return lax.dot_general(a, b, (((1,), (1,)), ((), ())), preferred_element_type=F32)


def three_parts(v):
    hi = v.astype(BF)
    rest = v - hi.astype(F32)
    mid = rest.astype(BF)
    low = (rest - mid.astype(F32)).astype(BF)
    return hi, mid, low


def two_parts(v):
    hi = v.astype(BF)
    return hi, (v - hi.astype(F32)).astype(BF)


def norm(value):
    centre = value - jnp.mean(value, axis=-1, keepdims=True)
    inverse = lax.rsqrt(jnp.mean(centre * centre, axis=-1, keepdims=True) + EPS)
    return centre * inverse, inverse


def norm_back(grad, normed, inverse):
    a = jnp.mean(grad, axis=-1, keepdims=True)
    b = jnp.mean(grad * normed, axis=-1, keepdims=True)
    return (grad - a - normed * b) * inverse


def gelu_both(x):
    phi = 0.5 + 0.5 * lax.erf(x * (0.5**0.5))
    density = 0.3989422804014327 * jnp.exp(x * x * -0.5)
    return x * phi, phi + x * density


def row(ref):
    return ref[...].astype(F32).reshape(1, ref.shape[0])


def fold(v):
    out = v[:8]
    for i in range(8, v.shape[0], 8):
        out += v[i : i + 8]
    return out


def total(v):
    return jnp.sum(v, axis=0, keepdims=True)


def head_lane(h):
    lane = lax.broadcasted_iota(jnp.int32, (1, LANES), 1)
    return (lane % PART == h) & (lane >= PART) & (lane < 4 * PART)


def put_rows(out_ref, lead, y, rows, halves, cols, value):
    n = value.shape[0] // halves
    for a in range(halves):
        side = jnp.where(y == a, 0, 1) if halves > 1 else 0
        out_ref[side, lead, pl.ds(rows, n), cols] = value[a * n : (a + 1) * n].astype(BF)


def put_shards(out_ref, info, lay, cols, value, rows=0, first=0):
    n, halves, rs = lay
    count = value.shape[0] // rs
    for i in range(count):
        lead = info[first * count + i] if n > 1 else 0
        put_rows(out_ref, lead, info[9], rows, halves, cols, value[i * rs : (i + 1) * rs])


def copies(pairs, sems, first=0):
    out = []
    for i, (src, dst) in enumerate(pairs):
        out.append(pltpu.make_async_copy(src, dst, sems.at[first + i]))
        out[-1].start()
    return out


def wait(moves):
    for m in moves:
        m.wait()


def split_kernel(info, x_ref, *refs):
    outs, sems = refs[:-1], refs[-1]
    wait(copies([(x_ref.at[info[10] ^ r], outs[r]) for r in range(len(outs))], sems))


def fetch_kernel(a, b, c, x, y, z, sems):
    wait(copies([(a, x), (b, y), (c, z)], sems))


def pack_kernel(o0, o1, o2, o3, i0, i1, i2, i3, pool, p0, p1, p2, p3):
    n = o0.shape[0]
    hi, low = two_parts(pool[:SEGS, :])
    for p, o, i in ((p0, o0, i0), (p1, o1, i1), (p2, o2, i2), (p3, o3, i3)):
        p[:n, :] = o[...]
        p[n : 2 * n, :] = i[...]
        p[2 * n : 2 * n + SEGS, :] = hi
        p[2 * n + SEGS :, :] = low


def unpack_kernel(info, lengths, p0, p1, p2, p3, out, grad, pool):
    me = info[10]
    n = out.shape[1]
    for r, p in enumerate((p0, p1, p2, p3)):
        out[me ^ r] = p[:n, :]
        grad[me ^ r] = p[n : 2 * n, :]
        sums = p[2 * n :, :].astype(F32)
        pool[me ^ r] = (sums[:SEGS] + sums[SEGS:]) / lengths[me ^ r][:, :1]


def attend_kernel(
    x0, x1, x2, x3, wq, wk, wv, wo_h, oh_ref, ka_ref, bq_ref, bv_ref, bo_ref,
    x_h, q_h, k_h, v_h, att_h, inv_h, qa_h, n1_out,
    x_out, q_out, k_out, v_out, att_out, inv_out, qa_out, wo, stat, sems,
):
    n = x0.shape[0]
    bq, bv, bo = row(bq_ref), row(bv_ref), row(bo_ref)
    last = copies([(wo_h, wo)], sems, 4)
    for r, ref in enumerate((x0, x1, x2, x3)):
        x_out[r * n : (r + 1) * n] = ref[...]
    outs = copies([(x_out, x_h)], sems, 8)
    x = x_out[...]
    q_out[...] = ((nn(x, wq[...]) + bq).astype(BF).astype(F32) * (HD**-0.5)).astype(BF)
    outs += copies([(q_out, q_h)], sems, 9)
    k_out[...] = nn(x, wk[...]).astype(BF)
    outs += copies([(k_out, k_h)], sems, 10)
    v_out[...] = (nn(x, wv[...]) + bv).astype(BF)
    outs += copies([(v_out, v_h)], sems, 11)
    tok, width = x.shape
    stat[...] = jnp.zeros_like(stat)
    ones = jnp.ones((16, tok), BF)

    def pair(p, carry):
        sl = pl.ds(pl.multiple_of(p * LANES, LANES), LANES)
        qcat = jnp.concatenate([q_out[:, sl], oh_ref[...]], axis=1)
        kp = k_out[:, sl]
        vt = v_out[:, sl].T
        lane = lax.broadcasted_iota(jnp.int32, (1, LANES), 1)
        parts = []
        for h in range(2):
            kh = jnp.where((lane < HD) == (h == 0), kp, jnp.zeros_like(kp))
            st = nt(jnp.concatenate([kh, ka_ref[...]], axis=1), qcat)
            m = jnp.max(st, axis=0, keepdims=True)
            pb = jnp.exp(st - m).astype(BF)
            ot = nn(jnp.concatenate([vt[h * HD : (h + 1) * HD], ones], axis=0), pb)
            total = ot[HD : HD + 1]
            stat[pl.ds(2 * p + h, 1), :] = m + jnp.log(total)
            parts.append(ot[:HD] / total)
        att_out[:, sl] = jnp.concatenate(parts, axis=0).T
        return carry

    lax.fori_loop(0, width // LANES, pair, 0, unroll=3)
    outs += copies([(att_out, att_h)], sems, 12)
    hi, mid, low = three_parts(stat[...])
    zero = jnp.zeros((PART, tok), BF)
    qa_out[...] = jnp.concatenate([zero, hi, mid, low, zero, zero, zero, zero], axis=0).T + oh_ref[...]
    outs += copies([(qa_out, qa_h)], sems, 13)
    wait(last)
    n1_out[...] = nn(att_out[...].astype(BF), wo[...])
    for at in range(0, tok, ROWS):
        rows = slice(at, at + ROWS)
        n1, inv = norm(x_out[rows, :].astype(F32) + (n1_out[rows, :] + bo))
        n1_out[rows, :] = n1
        inv_out[rows, :] = jnp.broadcast_to(inv, (ROWS, LANES))
    outs += copies([(inv_out, inv_h)], sems, 14)
    wait(outs)


def ffn_kernel(
    lay, info, n1_ref, ga_ref, sa_ref, bd_ref, gf_ref, sf_ref, wu, bu_ref, wd_h, g0, g1, g2, g3, oh_ref, oht_ref, gpl,
    o0, o1, o2, o3, gp_out, send, keep, pool_out, r2_out, vec_out,
    hl, acc, act, gt, wd, bu, gsum, hi, low, gl, sem_w,
):
    n = g0.shape[0]
    ga, sa, bd, gf, sf = row(ga_ref), row(sa_ref), row(bd_ref), row(gf_ref), row(sf_ref)
    bu[...] = row(bu_ref)
    tok, width = acc.shape
    ff = act.shape[1]
    tile = width
    steps = ff // tile

    def weights(t):
        rows = pl.ds(pl.multiple_of(t * tile, tile), tile)
        return pltpu.make_async_copy(wd_h.at[rows, :], wd.at[rows, :], sem_w.at[t])

    for t in range(steps):
        weights(t).start()
    hl[...] = (n1_ref[...] * ga + sa).astype(BF)
    acc[...] = jnp.zeros_like(acc)

    def step(t, carry):
        cols = pl.ds(pl.multiple_of(t * tile, tile), tile)
        weights(t).wait()
        for r in range(2):
            rows = pl.ds(r * 2 * n, 2 * n)
            a, d = gelu_both(nn(hl[rows, :], wu[:, cols]) + bu[:, cols])
            ab = a.astype(BF)
            act[rows, cols] = ab
            gp_out[rows, cols] = d.astype(BF)
            acc[rows, :] += nn(ab, wd[cols, :])
        return carry

    lax.fori_loop(0, steps, step, 0)
    oh = oh_ref[...]
    gsum[...] = nn(jnp.concatenate([oh, oh], axis=1), gpl[...])
    gain, shift, bias = (jnp.zeros((8, width), F32) for _ in range(3))
    gs, os = (g0, g1, g2, g3), (o0, o1, o2, o3)
    for at in range(0, tok, ROWS):
        rows = slice(at, at + ROWS)
        r, of = at // n, slice(at % n, at % n + ROWS)
        hidden = n1_ref[rows, :] * ga + sa
        n2, inv = norm(hidden + (acc[rows, :] + bd))
        result = n2 * gf + sf
        os[r][of, :] = result.astype(BF)
        hi[rows, :], low[rows, :] = two_parts(result)
        gout = gs[r][of, :].astype(F32) + gsum[rows, :]
        gain += fold(gout * n2)
        shift += fold(gout)
        gr2 = norm_back(gout * gf, n2, inv)
        r2_out[rows, :] = gr2
        low_g = gr2.astype(BF)
        bias += fold(low_g.astype(F32))
        gl[rows, :] = low_g
    gt[...] = gl[...].T
    pool_out[...] = nn(oht_ref[...], hi[...]) + nn(oht_ref[...], low[...])
    vec_out[...] = jnp.concatenate([total(v) for v in (bias, gain, shift)] + [jnp.zeros((5, width), F32)], axis=0)
    half = ff // 2
    part = 768

    def piece(i, carry):
        for rc, ref in ((1, send), (0, keep)):
            at = (info[8] ^ rc) * half + i * part
            res = nn(gt[...], act[:, pl.ds(pl.multiple_of(at, part), part)])
            put_shards(ref, info, lay, pl.ds(pl.multiple_of(i * part, part), part), res)
        return carry

    lax.fori_loop(0, half // part, piece, 0, unroll=2)


def ffn_back_kernel(
    lay, info, r2_ref, gp, wd, n1_ref, ga_ref, sa_ref,
    send, keep, bup_out, gpre_out,
    gl, hlt,
):
    ga, sa = row(ga_ref), row(sa_ref)
    width = hlt.shape[0]
    half = width // 2
    ff = gp.shape[1]
    tile = width
    steps = ff // tile

    gl[...] = r2_ref[...].astype(BF)
    hlt[...] = (n1_ref[...] * ga + sa).astype(BF).T
    per = 2 if lay[0] > 1 else 1

    def step(t, carry):
        cols = pl.ds(pl.multiple_of(t * tile, tile), tile)
        gpre = (nt(gl[...], wd[cols, :]) * gp[:, cols].astype(F32)).astype(BF)
        gpre_out[:, cols] = gpre
        bup_out[:, cols] = jnp.broadcast_to(
            jnp.sum(gpre.astype(F32), axis=0, keepdims=True), (bup_out.shape[0], tile)
        )
        for rc, ref in ((1, send), (0, keep)):
            at = pl.multiple_of((info[8] ^ rc) * half, half)
            res = nn(hlt[pl.ds(at, half), :], gpre)
            for i in range(per):
                if lay[0] > 1:
                    put_rows(ref, info[per * t + i], info[9], 0, lay[1], slice(None), res[:, i * half : (i + 1) * half])
                else:
                    put_rows(ref, 0, info[9], 0, lay[1], cols, res)
        return carry

    lax.fori_loop(0, steps, step, 0, unroll=4)


def norm_back_kernel(
    lay, info, r2_ref, gpre, wu, n1_ref, inv_ref, ga_ref, wo, att,
    r1_out, gatt_out, gaug_out, vec_out, osend, okeep,
    gt, acc, gm, hi, low,
):
    ga = row(ga_ref)
    tok, width = r2_ref.shape
    half = width // 2
    head = lax.broadcasted_iota(jnp.int32, (width, LANES), 0) // HD
    lane = lax.broadcasted_iota(jnp.int32, (width, LANES), 1)
    pick = ((lane % PART == head) & (lane >= PART) & (lane < 4 * PART)).astype(BF)
    lane1 = lax.broadcasted_iota(jnp.int32, (1, LANES), 1)

    def step(t, carry):
        cols = pl.ds(pl.multiple_of(t * width, width), width)
        acc[...] += nt(gpre[:, cols], wu[:, cols])
        return carry

    acc[...] = r2_ref[...]
    lax.fori_loop(0, gpre.shape[1] // width, step, 0)
    gain, shift, bias = (jnp.zeros((8, width), F32) for _ in range(3))
    for at in range(0, tok, ROWS):
        rows = slice(at, at + ROWS)
        gh = acc[rows, :]
        n1 = n1_ref[rows, :]
        gain += fold(gh * n1)
        shift += fold(gh)
        gr1 = norm_back(gh * ga, n1, inv_ref[rows, :1])
        r1_out[rows, :] = gr1
        low_g = gr1.astype(BF)
        bias += fold(low_g.astype(F32))
        gm[rows, :] = low_g
    gt[...] = gm[...].T
    gatt_out[...] = nt(gm[...], wo[...]).astype(BF)
    for at in range(0, tok, ROWS):
        rows = slice(at, at + ROWS)
        hi[rows, :], low[rows, :] = two_parts(gatt_out[rows, :].astype(F32) * att[rows, :])
    a, b, c = three_parts(nn(hi[...], pick) + nn(low[...], pick))
    gaug_out[...] = jnp.where(lane1 < 2 * PART, a, jnp.where(lane1 < 3 * PART, b, c))
    vec_out[...] = jnp.concatenate([total(v) for v in (bias, gain, shift)] + [jnp.zeros((5, width), F32)], axis=0)
    sides = [att[:, pl.ds(pl.multiple_of((info[8] ^ rc) * half, half), half)].astype(BF) for rc in (1, 0)]
    res = nn(gt[...], jnp.concatenate(sides, axis=1))
    put_shards(osend, info, lay, slice(None), res[:, :half])
    put_shards(okeep, info, lay, slice(None), res[:, half:])


def attend_back_kernel(
    q, k, v, g, qa, ka, ga,
    gq, gk, gv, gqt, gkt, gvt, vec_out,
):
    tok, width = q.shape

    def pair(p, carry):
        sl = pl.ds(pl.multiple_of(p * LANES, LANES), LANES)
        qp, kp, vp, gp = q[:, sl], k[:, sl], v[:, sl], g[:, sl]
        qcat = jnp.concatenate([qp, qa[...]], axis=1)
        gcat = jnp.concatenate([gp, ga[...]], axis=1)
        kt = kp.T
        lane = lax.broadcasted_iota(jnp.int32, (1, LANES), 1)
        gkp = jnp.zeros((tok, LANES), F32)
        gvp = jnp.zeros((tok, LANES), F32)
        parts = []
        zero = jnp.zeros_like(kp)
        for h in range(2):
            mine = (lane < HD) == (h == 0)
            pick = head_lane(2 * p + h)
            kaug = jnp.where(pick, -jnp.ones((), BF), ka[...])
            vaug = jnp.where(pick, -jnp.ones((), BF), jnp.zeros((tok, LANES), BF))
            prob = jnp.exp(nt(jnp.concatenate([jnp.where(mine, kp, zero), kaug], axis=1), qcat))
            dp = nt(jnp.concatenate([jnp.where(mine, vp, zero), vaug], axis=1), gcat)
            ds = (prob * dp).astype(BF)
            gvp += nn(prob.astype(BF), jnp.where(mine, gp, zero))
            gkp += nn(ds, jnp.where(mine, qp, zero))
            parts.append(nn(kt[h * HD : (h + 1) * HD], ds))
        gqp = (jnp.concatenate(parts, axis=0) * (HD**-0.5)).astype(BF)
        gqt[sl, :] = gqp
        gq[:, sl] = gqp.T
        gkb, gvb = gkp.astype(BF), gvp.astype(BF)
        gk[:, sl] = gkb
        gv[:, sl] = gvb
        gkt[sl, :] = gkb.T
        gvt[sl, :] = gvb.T
        return carry

    lax.fori_loop(0, width // LANES, pair, 0, unroll=3)
    bq = jnp.sum(gq[...].astype(F32), axis=0, keepdims=True)
    bv = jnp.sum(gv[...].astype(F32), axis=0, keepdims=True)
    vec_out[...] = jnp.concatenate([bq, bv, jnp.zeros((6, width), F32)], axis=0)


def weights_back_kernel(lay, info, gqt, gkt, gvt, x_ref, vecs, bups, osend, okeep, send_a, send_b, keep_a, keep_b):
    width = x_ref.shape[1]
    n, halves, rs = lay
    half = width // 2
    sides = [x_ref[:, pl.ds(pl.multiple_of((info[8] ^ rc) * half, half), half)] for rc in (1, 0)]
    right = jnp.concatenate(sides, axis=1)
    wires = ((1, (send_a, send_b)), (0, (keep_a, keep_b)))
    for m, left in enumerate((gqt, gkt, gvt)):
        both = nn(left[...], right)
        for rc, (wa, wb) in wires:
            res = both[:, :half] if rc else both[:, half:]
            if n > 1:
                for j in range(n):
                    rows = res[j * rs : (j + 1) * rs]
                    put = functools.partial(put_rows, lead=info[j], y=info[9], halves=halves, cols=slice(None))
                    if m == 0:
                        put(wa, rows=0, value=rows)
                    elif m == 1:
                        put(wa, rows=48, value=rows[:32])
                        put(wb, rows=48, value=rows[32:])
                    else:
                        put(wb, rows=0, value=rows)
            elif m < 2:
                wa[0, 0, pl.ds(m * width, width), :] = res.astype(BF)
            else:
                wb[0, 0] = res.astype(BF)
    if n > 1:
        for o, (wa, wb) in ((osend, (send_a, send_b)), (okeep, (keep_a, keep_b))):
            wa[:, :, 80:, :] = o[:, :, :16, :]
            wb[:, :, 80:, :] = o[:, :, 16:, :]
        for j in range(n):
            bup = bups[:1, j * 4 * rs : (j + 1) * 4 * rs]
            block = jnp.concatenate(
                [vecs[:, j * rs : (j + 1) * rs], jnp.zeros((8, rs), F32)]
                + [bup[:, c * rs : (c + 1) * rs] for c in range(4)]
                + [jnp.zeros((12, rs), F32)],
                axis=0,
            )
            block = jnp.concatenate([block, jnp.zeros((32, half - rs), F32)], axis=1)
            for rc, (wa, _) in wires:
                mine = jnp.where((info[8] ^ rc) == 0, 1.0, 0.0)
                put_rows(wa, info[j], info[9], 64, halves, slice(None), block * mine)


def input_back_kernel(gq, gk, gv, r1, wq, wk, wv, o0, o1, o2, o3):
    whole = r1[...] + nt(gq[...], wq[...]) + nt(gk[...], wk[...]) + nt(gv[...], wv[...])
    for r, o in enumerate((o0, o1, o2, o3)):
        c = o.shape[0]
        o[...] = whole[r * c : (r + 1) * c].astype(BF)


WHOLE = pl.BlockSpec(memory_space=pltpu.VMEM)
SCALARS = pl.BlockSpec(memory_space=pltpu.SMEM)
FAR = pl.BlockSpec(memory_space=pltpu.HBM)


def shape(dims, dtype=BF):
    return jax.ShapeDtypeStruct(tuple(dims), dtype)


def buf(dims, dtype=BF):
    return pltpu.VMEM(tuple(dims), dtype)


def sems(count):
    return pltpu.SemaphoreType.DMA((count,))


def params(mib):
    return pltpu.CompilerParams(vmem_limit_bytes=mib * 1024 * 1024)


def cost(us):
    return pl.CostEstimate(flops=int(us * 10**9) + 1, bytes_accessed=1, transcendentals=0)


COSTS = {'down_one': 0.1, 'up_one': 0.1, 'down_two': 0.1, 'up_two': 1.0, 'down_three': 14.0, 'qkv_one': 0.1, 'up_three': 3.0, 'down_four': 1.0, 'down_end': 0.02, 'up_end': 0.02}


class Line:
    def __init__(self):
        self.token = None

    def call(self, kernel, outs, args, scalars=(), scratch=(), name=None, mib=8, far_in=(), far_out=(), us=0.0):
        args = [pltpu.with_memory_space_constraint(a, pltpu.HBM) if i in far_in else a for i, a in enumerate(args)]
        ins = [SCALARS if i in scalars else FAR if i in far_in else WHOLE for i in range(len(args))]
        to = [FAR if i in far_out else WHOLE for i in range(len(outs))]
        outs = [pltpu.HBM(o.shape, o.dtype) if i in far_out else o for i, o in enumerate(outs)]
        tokens = [] if self.token is None else [self.token]
        n_in, n_tok, n_out = len(args), len(tokens), len(outs)

        def body(*refs):
            left, right = refs[:n_in], refs[n_in + n_tok :]
            kernel(*left, *right[:n_out], *right[n_out + 1 :])
            right[n_out][...] = jnp.zeros((8, LANES), F32)

        *got, self.token = pl.pallas_call(
            body,
            out_shape=[*outs, shape((8, LANES), F32)],
            in_specs=ins + [WHOLE] * n_tok,
            out_specs=[*to, WHOLE],
            scratch_shapes=list(scratch),
            compiler_params=params(mib),
            cost_estimate=cost(us),
            name=name,
        )(*args, *tokens)
        return got


def plus(a, b):
    return (a.astype(F32) + b.astype(F32)).astype(BF)


def half_of(ref, axis, side, rows, cols):
    lead = [slice(None)] * (len(ref.shape) - 2)
    lead[axis] = side
    return ref[(*lead, slice(*rows), slice(*cols))]


def split_sum_kernel(parts, n_got, n_kept, n_send, *refs):
    got, kept, out = refs[:n_got], refs[n_got : n_got + n_kept], refs[n_got + n_kept :]
    for axis, spans, (send, send_at), (keep, keep_at) in parts:
        done = 0
        for g, g_rows, g_cols, k, k_rows, k_cols in spans:
            m = g_rows[1] - g_rows[0]
            for side, ref, at in ((1, out[send], send_at), (0, out[n_send + keep], keep_at)):
                lead = [slice(None)] * (len(ref.shape) - 2)
                ref[(*lead, slice(at + done, at + done + m), slice(None))] = plus(
                    half_of(got[g], axis, side, g_rows, g_cols), half_of(kept[k], axis, side, k_rows, k_cols)
                )
            done += m


def five_kernel(got, kept, mine):
    mine[...] = plus(got[...], kept[...])


def six_kernel(info, mine, other, both):
    both[info[9]] = mine[...]
    both[1 - info[9]] = other[...]


def down_kernel(info, mine, other, out):
    m = mine.shape[1] // 3
    cols = mine.shape[2]
    for rc, ref in ((0, mine), (1, other)):
        for p in range(3):
            block = jnp.concatenate([ref[0, p * m : (p + 1) * m], ref[1, p * m : (p + 1) * m]], axis=0)
            at = (info[8] ^ rc) * 3 * cols + p * cols
            out[:, pl.ds(pl.multiple_of(at, cols), cols)] = block.astype(F32)


def up_kernel(info, mine, other, out):
    half = out.shape[0] // 2
    m = half // 2
    for rc, ref in ((0, mine), (1, other)):
        for a in range(2):
            at = (info[8] ^ rc) * half + a * m
            out[pl.ds(pl.multiple_of(at, m), m), :] = ref[a].astype(F32)


def qkv_kernel(info, here, over_y, over_core, over_both, gq, gk, gv, go, *vecs):
    half = gq.shape[1] // 2
    y0 = info[9] == 0
    mine, other = (
        [jnp.where(y0, a[...], b[...]), jnp.where(y0, b[...], a[...])] for a, b in ((here, over_y), (over_core, over_both))
    )
    for rc, ref in ((0, mine), (1, other)):
        at = pl.ds(pl.multiple_of((info[8] ^ rc) * half, half), half)

        def put(out, *spans):
            parts = [ref[a][i : i + m] for a, i, m in spans]
            out[:, at] = jnp.concatenate(parts, axis=0).astype(F32)

        put(gq, (0, 0, 48), (1, 0, 48))
        put(gk, (0, 48, 16), (1, 48, 16), (0, 144, 32), (1, 144, 32))
        put(gv, (0, 96, 48), (1, 96, 48))
        put(go, (0, 80, 16), (0, 176, 32), (1, 80, 16), (1, 176, 32))
    rs = vecs[0].shape[0]
    low = [jnp.where(info[8] == 0, m[64:80].astype(F32), o[64:80].astype(F32)) for m, o in zip(mine, other)]
    for i, out in enumerate(vecs[:8]):
        out[...] = low[0][i, :rs]
    for c in range(4):
        vecs[8][pl.ds(c * rs, rs)] = low[1][c, :rs]


def local(n_dp, n_seq, *args):
    (
        tokens, seg_lengths, w_query, b_query, w_key, w_value, b_value, w_out, b_out,
        gain_attn, shift_attn, w_up, b_up, w_down, b_down, gain_ffn, shift_ffn,
        grad_output, grad_pooled,
    ) = args
    line = Line()
    me = lax.axis_index("seq")
    dp = lax.axis_index("dp")
    core, y = me % 2, me // 2
    rows, piece, width = tokens.shape
    tok = n_seq * piece
    ff = w_up.shape[1]
    fast = n_dp == 8
    n = n_dp if fast else 1
    rs = width // n
    half = width // 2
    xor = [[(i, i ^ r) for i in range(n_seq)] for r in range(n_seq)]

    if fast:
        j = jnp.arange(8, dtype=jnp.int32) ^ dp
        pos = (j % 2) * 4 + (j // 2 % 2) * 2 + j // 4
    else:
        pos = jnp.zeros((8,), jnp.int32)
    info = jnp.concatenate([pos, jnp.stack([core, y, me]), jnp.zeros((5,), jnp.int32)]).astype(jnp.int32)

    def rel(a, name):
        parts = line.call(
            split_kernel, [shape((piece, width))] * n_seq, (info, a), scalars=(0,), scratch=[sems(n_seq)],
            name=name, far_in=(1,),
        )
        return [parts[0]] + [lax.ppermute(parts[r], "seq", xor[r]) for r in range(1, n_seq)]

    xs = rel(tokens, "split_tokens")
    gs = rel(grad_output, "split_grads")

    lengths = lax.dynamic_index_in_dim(seg_lengths, me, 0, keepdims=False)
    ends = jnp.cumsum(lengths)
    order = me ^ jnp.arange(n_seq, dtype=jnp.int32)
    places = (order[:, None] * piece + jnp.arange(piece, dtype=jnp.int32)[None, :]).reshape(tok)
    seg = jnp.sum((places[:, None] >= ends[None, :]).astype(jnp.int32), axis=1)
    lane = jnp.arange(LANES, dtype=jnp.int32)
    hot = seg[:, None] == lane[None, :]
    onehot = hot.astype(BF)
    kaug = jnp.where((lane < SEGS)[None, :] & ~hot, NEG, 0.0).astype(BF)
    onehot_t = (seg[None, :] == jnp.arange(16, dtype=jnp.int32)[:, None]).astype(BF)
    length_col = lengths.astype(F32)[:, None]
    gpool = lax.dynamic_index_in_dim(grad_pooled, me, 0, keepdims=False).astype(F32) / length_col
    gp_hi = gpool.astype(BF)
    gp_low = (gpool - gp_hi.astype(F32)).astype(BF)
    zeros = jnp.zeros((LANES - SEGS, width), BF)
    gpl = jnp.concatenate([gp_hi, zeros, gp_low, zeros], axis=0)


    sq = shape((tok, width))
    sqf = shape((tok, width), F32)
    row_lengths = jnp.broadcast_to(seg_lengths.astype(F32)[:, :, None], (rows, SEGS, LANES))
    near = line.call(
        fetch_kernel, [shape((width, width))] * 3, (w_query, w_key, w_value), scratch=[sems(3)], name="fetch",
        far_in=range(3),
    )
    lanes = shape((tok, LANES))
    lanes_f = shape((tok, LANES), F32)
    x, q, k, v, att, inv, qaug, n1 = line.call(
        attend_kernel,
        [sq, sq, sq, sq, sqf, lanes_f, lanes, sqf],
        (*xs, *near, w_out, onehot, kaug, b_query, b_value, b_out),
        scratch=[buf((tok, width))] * 4
        + [buf((tok, width), F32), buf((tok, LANES), F32), buf((tok, LANES))]
        + [buf((width, width)), buf((PART, tok), F32), sems(15)],
        name="attend",
        mib=20,
        far_in=(7,),
        far_out=range(7),
    )

    halves = 2 if fast else 1
    lay = (n, halves, rs)
    wire_d = shape((halves, n, rs // halves, ff // 2))
    steps = ff // width
    *outs, gp, d_send, d_keep, pool, r2, vec_b = line.call(
        functools.partial(ffn_kernel, lay),
        [shape((piece, width))] * 4
        + [shape((tok, ff)), wire_d, wire_d, shape((16, width), F32), sqf, shape((8, width), F32)],
        (
            info, n1, gain_attn, shift_attn, b_down, gain_ffn, shift_ffn, w_up, b_up, w_down, *gs, onehot, onehot_t, gpl,
        ),
        scalars=(0,),
        scratch=[
            buf((tok, width)), buf((tok, width), F32), buf((tok, ff)), buf((width, tok)), buf((ff, width)),
            buf((1, ff), F32), buf((tok, width), F32), buf((tok, width)), buf((tok, width)), buf((tok, width)),
            sems(steps),
        ],
        name="ffn",
        mib=24,
        far_in=(9,),
    )

    pp_core = lambda a: lax.ppermute(a, "seq", xor[1])
    pp_y = lambda a: lax.ppermute(a, "seq", xor[2])

    def pp_dp(bit):
        return lambda a: lax.ppermute(a, "dp", [(i, i ^ bit) for i in range(n_dp)])

    pp_x, pp_z1, pp_z2 = pp_dp(1), pp_dp(2), pp_dp(4)

    def join_rows(parts):
        return parts[0] if len(parts) == 1 else jnp.concatenate(parts, axis=-2)

    send_along = {"x": pp_x, "y": pp_y, "z": pp_z1, "w": pp_z2}

    class Sum:
        def __init__(self, name, got, kept, parts):
            sides = lambda w: w.reshape(2, 2, 2, 2, *w.shape[2:])
            self.name = name
            self.got, self.kept = [sides(w) for w in got], [sides(w) for w in kept]
            self.spans = [[(i, r, c, i, r, c) for i, r, c in spans] for spans in parts]
            self.rows = [sum(r[1] - r[0] for _, r, _ in spans) for spans in parts]
            self.cols = parts[0][0][2][1] - parts[0][0][2][0]
            self.whole = sum(self.rows), self.cols
            self.left = ["yxzw"] * len(parts)

        def run(self, step, kernel, outs, args, scalars=()):
            name = self.name + step
            return line.call(
                kernel, [shape(o) for o in outs], args, scalars=scalars, name=name, mib=16, us=COSTS.get(name, 0.3)
            )

        def split(self, step, along):
            ways, last = list(dict.fromkeys(along)), along[0] == "w"
            height, kept_height, parts = dict.fromkeys(ways, 0), 0, []
            for p, a in enumerate(along):
                keep = (0, kept_height) if last else (p, 0)
                parts.append((self.left[p].index(a), self.spans[p], (ways.index(a), height[a]), keep))
                self.left[p] = self.left[p].replace(a, "")
                height[a] += self.rows[p]
                kept_height += self.rows[p]
            lead = (2,) * len(self.left[0])
            keeps = [sum(self.rows)] if last else self.rows
            out = self.run(
                step,
                functools.partial(split_sum_kernel, parts, len(self.got), len(self.kept), len(ways)),
                [(*lead, m, self.cols) for m in [*height.values(), *keeps]],
                (*self.got, *self.kept),
            )
            self.got = [send_along[a](w) for a, w in zip(ways, out[: len(ways)])]
            self.kept = out[len(ways) :]
            self.spans = [
                [(i, (at, at + m), (0, self.cols), k, (k_at, k_at + m), (0, self.cols))]
                for m, (_, _, (i, at), (k, k_at)) in zip(self.rows, parts)
            ]

        def one(self):
            self.split("one", "xyz"[: len(self.rows)])

        def two(self):
            self.split("two", "yxx"[: len(self.rows)])

        def three(self):
            self.split("three", "zzy"[: len(self.rows)])

        def four(self):
            self.split("four", "www"[: len(self.rows)])

        def mine(self):
            (mine,) = self.run("five", five_kernel, [self.whole], (*self.got, *self.kept))
            return mine

        def five(self):
            mine = self.mine()
            self.got, self.kept = pp_y(mine), mine

        def six(self):
            (both,) = self.run("six", six_kernel, [(2, *self.whole)], (info, self.kept, self.got), scalars=(0,))
            self.got, self.kept = pp_core(both), both

        def five_all(self):
            mine = self.mine()
            self.kept, self.got = mine, [pp_y(mine), pp_core(mine), lax.ppermute(mine, "seq", xor[3])]

        def end(self, kernel, outs):
            return line.call(
                kernel, outs, (info, self.kept, *(self.got if isinstance(self.got, list) else [self.got])), scalars=(0,),
                name=self.name + "end", mib=16,
            )

    wire_u = shape((halves, n, half // halves, ff // n))
    if fast:
        d_got = pp_core(d_send)
    u_send, u_keep, bup, gpre = line.call(
        functools.partial(ffn_back_kernel, lay),
        [wire_u, wire_u, shape((8, ff), F32), shape((tok, ff))],
        (info, r2, gp, w_down, n1, gain_attn, shift_attn),
        scalars=(0,),
        scratch=[buf((tok, width)), buf((width, tok))],
        name="ffn_back",
        mib=12,
    )
    if fast:
        u_got = pp_core(u_send)
        c, m = ff // 6, rs // 2
        down = Sum("down_", [d_got], [d_keep], [[(0, (0, m), (p * c, (p + 1) * c))] for p in range(3)])
        down.one()
    wire_o = shape((halves, n, rs // halves, half))
    r1, gatt, gaug, vec_c, o_send, o_keep = line.call(
        functools.partial(norm_back_kernel, lay),
        [sqf, sq, shape((tok, LANES)), shape((8, width), F32), wire_o, wire_o],
        (info, r2, gpre, w_up, n1, inv, gain_attn, w_out, att),
        scalars=(0,),
        scratch=[buf((width, tok)), buf((tok, width), F32)] + [buf((tok, width))] * 3,
        name="norm_back",
        mib=14,
    )
    if fast:
        m = half // 4
        up = Sum("up_", [u_got], [u_keep], [[(0, (p * m, (p + 1) * m), (0, half))] for p in range(2)])
        up.one()

    gq, gk, gv, gqt, gkt, gvt, vec_d = line.call(
        attend_back_kernel,
        [sq] * 3 + [shape((width, tok))] * 3 + [shape((8, width), F32)],
        (q, k, v, gatt, qaug, kaug, gaug),
        name="attend_back",
        mib=10,
    )
    vecs = jnp.concatenate([vec_d[:2], vec_c[:3], vec_b[:3]], axis=0)
    if fast:
        down.two()
    rows_a, rows_b = (96, 112) if fast else (2 * width, width)
    wire_a, wire_b = shape((halves, n, rows_a, half)), shape((halves, n, rows_b, half))
    qa_send, qb_send, qa_keep, qb_keep = line.call(
        functools.partial(weights_back_kernel, lay),
        [wire_a, wire_b, wire_a, wire_b],
        (info, gqt, gkt, gvt, x, vecs, bup, o_send, o_keep),
        scalars=(0,),
        name="weights_back",
        mib=16,
    )

    def send_back():
        ins = line.call(
            input_back_kernel, [shape((piece, width))] * 4, (gq, gk, gv, r1, w_query, w_key, w_value),
            name="input_back", mib=16,
        )
        packs = line.call(
            pack_kernel, [shape((2 * piece + 2 * SEGS, width))] * n_seq, (*outs, *ins, pool), name="pack"
        )
        return [packs[0]] + [lax.ppermute(packs[r], "seq", xor[r]) for r in range(1, n_seq)]

    def take_back(packs):
        return line.call(
            unpack_kernel,
            [shape((rows, piece, width)), shape((rows, piece, width)), shape((rows, SEGS, width), F32)],
            (info, row_lengths, *packs),
            scalars=(0,),
            name="unpack",
            us=1.0,
        )

    if fast:
        qkv = Sum(
            "qkv_", [pp_core(qa_send), pp_core(qb_send)], [qa_keep, qb_keep],
            [[(0, (0, rows_a), (0, half))], [(1, (0, rows_b), (0, half))]],
        )
        f32 = lambda *d: shape(d, F32)
        up.two()
        down.three()
        qkv.one()
        packs = send_back()
        down.four()
        up.three()
        qkv.two()
        up.four()
        down.five()
        down.six()
        qkv.three()
        up.five()
        up.six()
        qkv.four()
        (g_down,) = down.end(down_kernel, [f32(rs, ff)])
        (g_up,) = up.end(up_kernel, [f32(width, ff // n)])
        qkv.five_all()
        output, grad_tokens, pooled = take_back(packs)
        *g_qkv, g_out, v0, v1, v2, v3, v4, v5, v6, v7, v8 = qkv.end(
            qkv_kernel, [f32(rs, width)] * 4 + [f32(rs)] * 8 + [f32(4 * rs)]
        )
        g_down, g_out, g_qkv = g_down.T, g_out.T, [g.T for g in g_qkv]
        small = [v0, v1, v2, v3, v4, v5, v6, v7, v8]
    else:
        output, grad_tokens, pooled = take_back(send_back())

        def total(send, keep, dim):
            h = keep.astype(F32) + pp_core(send).astype(F32)
            h = h + pp_y(h.astype(BF)).astype(F32)
            return lax.psum_scatter(h, "dp", scatter_dimension=dim, tiled=True).astype(BF)

        def whole(send, keep, dim, along):
            mine = total(send, keep, dim)
            other = pp_core(mine)
            lo, hi = jnp.where(core == 0, mine, other), jnp.where(core == 0, other, mine)
            return jnp.concatenate([lo, hi], axis=along).astype(F32)

        g_down = whole(d_send[0, 0], d_keep[0, 0], 0, 1).T
        g_up = whole(u_send[0, 0], u_keep[0, 0], 1, 0)
        g_out = whole(o_send[0, 0], o_keep[0, 0], 0, 1).T
        g_qkv = [
            whole(send, keep, 0, 1).T
            for send, keep in (
                (qa_send[0, 0, :width], qa_keep[0, 0, :width]),
                (qa_send[0, 0, width:], qa_keep[0, 0, width:]),
                (qb_send[0, 0], qb_keep[0, 0]),
            )
        ]
        flat = lax.psum(jnp.concatenate([vecs.reshape(-1), bup[0]]), ("dp", "seq"))
        mine = width // n_dp
        small = [
            lax.dynamic_slice_in_dim(flat, i * width + dp * mine, mine) for i in range(8)
        ] + [lax.dynamic_slice_in_dim(flat, 8 * width + dp * 4 * mine, 4 * mine)]

    bq, bv, b_o, gain1, shift1, b_d, gain2, shift2, b_u = small
    return (
        output, pooled, grad_tokens, g_qkv[0], bq, g_qkv[1], g_qkv[2], bv, g_out, b_o, gain1, shift1,
        g_up, b_u, g_down, b_d, gain2, shift2,
    )


def solution(mesh):
    rows = P("dp", "seq", None)
    placed = (rows, P("dp", None)) + (P(),) * 15 + (rows, P("dp", None, None))
    col, one = P(None, "dp"), P("dp")
    return jax.shard_map(
        functools.partial(local, mesh.shape["dp"], mesh.shape["seq"]),
        mesh=mesh,
        in_specs=placed,
        out_specs=(
            rows, P("dp", None, None), rows, col, one, col, col, one, col, one, one, one,
            col, one, col, one, one, one,
        ),
        check_vma=False,
    )
```
